32 devices in a mesh: dp: 4 (over x, core), seq: 8 (over z, y).
Axes of the slice: x: 2, y: 2, z: 4, core: 2. Of those that a mesh axis runs over, the one named last changes fastest.
Arguments:
- layer_input: bfloat16 [8192, 2048], P(('dp', 'seq')), may hold values from -6 to 6
- global_keys: bfloat16 [8192, 2048], P(('dp', 'seq')), may hold values from -8 to 8
- global_values: bfloat16 [8192, 2048], P(('dp', 'seq')), may hold values from -6 to 6
- lengths: int32 [4], P('dp'), may hold values from 256 to 2048, as said below
- attn_gain: bfloat16 [2048], P('seq'), may hold values from 0.25 to 1.75
- query_weight: bfloat16 [2048, 2048], P('seq'), may hold values from -0.125 to 0.125
- out_weight: bfloat16 [2048, 2048], P('seq'), may hold values from -2 to 2
- ffn_gain: bfloat16 [2048], P('seq'), may hold values from 0.25 to 1.75
- gate_weight: bfloat16 [5504, 2048], P('seq'), may hold values from -0.125 to 0.125
- up_weight: bfloat16 [5504, 2048], P('seq'), may hold values from -0.125 to 0.125
- down_weight: bfloat16 [5504, 2048], P('seq'), may hold values from -0.078125 to 0.078125
- cotangent: bfloat16 [8192, 2048], P(('dp', 'seq')), may hold values from -6 to 6
Outputs:
- layer_output: bfloat16 [8192, 2048], P(('dp', 'seq'))
- input_grad: bfloat16 [8192, 2048], P(('dp', 'seq'))
- key_grad: bfloat16 [8192, 2048], P(('dp', 'seq'))
- value_grad: bfloat16 [8192, 2048], P(('dp', 'seq'))
- attn_gain_grad: float32 [2048], P('seq')
- query_weight_grad: float32 [2048, 2048], P('seq')
- out_weight_grad: float32 [2048, 2048], P('seq')
- ffn_gain_grad: float32 [2048], P('seq')
- gate_weight_grad: float32 [5504, 2048], P('seq')
- up_weight_grad: float32 [5504, 2048], P('seq')
- down_weight_grad: float32 [5504, 2048], P('seq')
The draws below stay inside these ranges and needn't reach their ends.
Inputs may be any that keep to these rules, and one draw needn't show every extreme that they name: The first lengths[g] positions of bucket g are live and the rest are padding; in every draw at least one bucket is full.
All inputs are finite; a program needn't handle non-finite values.
Results may differ from the reference program's by a relative error of at most 0.02.
Values may be sent and summed in bfloat16 or wider, within the bound.
No kernel may reach another device: no remote copies, remote signals or barrier semaphores. Data moves between devices by JAX's collectives and lax.ppermute only.
A program may use at most 320 MiB of HBM per device.

```python
import jax
import jax.numpy as jnp
from jax import lax

D = 2048
HEADS = 16
HEAD_DIM = 128
FF = 5504
ATT_BLOCK = 512
SEQ_LEN = 2048
TOKENS = 8192
N_DP = 4


def draw_lengths(key, part):
    drawn = jax.random.randint(key, (N_DP,), SEQ_LEN // 8, SEQ_LEN + 1, dtype=jnp.int32)
    chosen = jax.random.randint(jax.random.fold_in(key, 7), (), 0, N_DP, dtype=jnp.int32)
    return jnp.where(jnp.arange(N_DP, dtype=jnp.int32) == chosen, SEQ_LEN, drawn).astype(jnp.int32)


def level_of(own_key, extent, pieces, low, top_value):
    factor_of, own = 1.0, jax.random.fold_in(own_key, 6)
    for position, shards_of in pieces:
        heights = jnp.exp(jax.random.uniform(jax.random.fold_in(own, position), (shards_of,), jnp.float32, low / len(pieces), top_value / len(pieces)))
        factor_of = factor_of * jnp.repeat(heights, extent[position] // shards_of).reshape([-1 if axis == position else 1 for axis in range(len(extent))])
    return factor_of


def centred(rng, dims, width, bound, pieces=(), kind=jnp.bfloat16):
    values = width * jax.random.normal(rng, dims, jnp.float32)
    if pieces:
        values = values * level_of(rng, dims, pieces, -0.22, 0.18)
    return jnp.clip(values, -bound, bound).astype(kind)


def setup_inputs(seed: int = 0) -> dict:
    arg_keys = jax.random.split(jax.random.key(seed), 13)
    layer_input = centred(arg_keys[0], (TOKENS, D), 1.0, 6.0, ((0, 32),))
    global_keys = centred(arg_keys[1], (TOKENS, D), 1.5, 8.0, ((0, 32),))
    global_values = centred(arg_keys[2], (TOKENS, D), 1.0, 6.0, ((0, 32),))
    lengths = draw_lengths(jax.random.fold_in(arg_keys[12], 71), 0)
    attn_gain = jnp.clip(1.0 + 0.15 * jax.random.normal(arg_keys[4], (D,), jnp.float32), 0.25, 1.75).astype(jnp.bfloat16)
    query_weight = centred(arg_keys[5], (D, D), D ** -0.5, 0.125, ((0, 8),))
    out_weight = centred(arg_keys[6], (D, D), (max(D // 256, 1)) ** -0.5, 2.0, ((0, 8),))
    ffn_gain = jnp.clip(1.0 + 0.15 * jax.random.normal(arg_keys[7], (D,), jnp.float32), 0.25, 1.75).astype(jnp.bfloat16)
    gate_weight = centred(arg_keys[8], (FF, D), D ** -0.5, 0.125, ((0, 8),))
    up_weight = centred(arg_keys[9], (FF, D), D ** -0.5, 0.125, ((0, 8),))
    down_weight = centred(arg_keys[10], (FF, D), FF ** -0.5, 0.078125, ((0, 8),))
    cotangent = centred(arg_keys[11], (TOKENS, D), 1.0, 6.0, ((0, 32),))
    return {"layer_input": layer_input, "global_keys": global_keys, "global_values": global_values, "lengths": lengths, "attn_gain": attn_gain, "query_weight": query_weight, "out_weight": out_weight, "ffn_gain": ffn_gain, "gate_weight": gate_weight, "up_weight": up_weight, "down_weight": down_weight, "cotangent": cotangent}


EPSILON = 1e-05
HIGHEST = lax.Precision.HIGHEST

@jax.custom_vjp
def low(v):
    return lax.optimization_barrier(v.astype(jnp.bfloat16)).astype(jnp.float32)

@jax.custom_vjp
def low_back(v):
    return v

def low_keep(v):
    return (low(v), None)

def low_pass(kept, grad):
    return (grad,)

def back_keep(v):
    return (v, None)

def back_low(kept, grad):
    return (low(grad),)
low.defvjp(low_keep, low_pass)
low_back.defvjp(back_keep, back_low)

def root_norm(values_in, gain_scale):
    return values_in * lax.rsqrt(lax.optimization_barrier(jnp.mean(values_in * values_in, axis=-1, keepdims=True)) + EPSILON) * gain_scale

def product(left_side, right_side):
    return jnp.dot(left_side, right_side, precision=HIGHEST)

def attention(queries, keys_used, values_used, length):
    score_scale = HEAD_DIM ** (-0.5)
    query_blocks = queries.reshape(SEQ_LEN // ATT_BLOCK, ATT_BLOCK, HEADS, HEAD_DIM)
    key_heads = keys_used.reshape(SEQ_LEN, HEADS, HEAD_DIM)
    value_heads = values_used.reshape(SEQ_LEN, HEADS, HEAD_DIM)
    key_pos = jnp.arange(SEQ_LEN, dtype=jnp.int32)

    def query_block(operands):
        query_rows, first_row = operands
        query_pos = first_row + jnp.arange(ATT_BLOCK, dtype=jnp.int32)
        scores = low_back(jnp.einsum('qhd,khd->hqk', query_rows, key_heads, precision=HIGHEST) * score_scale)
        causal = key_pos[None, :] <= query_pos[:, None]
        scores = jnp.where(causal[None], scores, -jnp.inf)
        weights_soft = jax.nn.softmax(scores, axis=-1)
        live_rows = (query_pos < length)[None, :, None]
        weights_soft = low(jnp.where(live_rows, weights_soft, 0.0))
        return jnp.einsum('hqk,khd->qhd', weights_soft, value_heads, precision=HIGHEST)
    starts = jnp.arange(SEQ_LEN // ATT_BLOCK, dtype=jnp.int32) * ATT_BLOCK
    blended = lax.map(jax.checkpoint(query_block), (query_blocks, starts))
    return blended.reshape(SEQ_LEN, D)

def block_layer(seq_input, seq_keys, seq_values, length, params):
    attn_gain, query_weight, out_weight, ffn_gain, gate_weight, up_weight, down_weight = params
    normed = low(root_norm(seq_input, attn_gain))
    queries = low_back(low(product(normed, query_weight)))
    mixed_heads = low_back(low(attention(queries, low_back(seq_keys), low_back(seq_values), length)))
    hidden = seq_input + low_back(product(mixed_heads, out_weight))
    normed_ffn = low(root_norm(hidden, ffn_gain))
    gate_value = low_back(product(normed_ffn, gate_weight.T))
    up_value = low_back(product(normed_ffn, up_weight.T))
    inner_act = low(jax.nn.silu(gate_value) * up_value)
    return hidden + product(inner_act, down_weight)

def whole_forward(lengths, input_wide, keys_wide, values_wide, *params):

    def by_sequence(array_in):
        return array_in.reshape(N_DP, SEQ_LEN, D)

    def scan_step(scan_carry, scan_item):
        seq_input, seq_keys, seq_values, length = scan_item
        return (scan_carry, jax.checkpoint(block_layer)(seq_input, seq_keys, seq_values, length, params))
    final_carry, results = lax.scan(scan_step, jnp.zeros((), jnp.float32), (by_sequence(input_wide), by_sequence(keys_wide), by_sequence(values_wide), lengths.astype(jnp.int32)))
    return results.reshape(TOKENS, D)

def reference(layer_input, global_keys, global_values, lengths, attn_gain, query_weight, out_weight, ffn_gain, gate_weight, up_weight, down_weight, cotangent):
    floats = tuple((array_in.astype(jnp.float32) for array_in in (layer_input, global_keys, global_values, attn_gain, query_weight, out_weight, ffn_gain, gate_weight, up_weight, down_weight)))

    def wrapped(*operands):
        return whole_forward(lengths, *operands)
    result, pullback = jax.vjp(wrapped, *floats)
    gradients = pullback(cotangent.astype(jnp.float32))
    return (result.astype(jnp.bfloat16), gradients[0].astype(jnp.bfloat16), gradients[1].astype(jnp.bfloat16), gradients[2].astype(jnp.bfloat16), gradients[3], gradients[4], gradients[5], gradients[6], gradients[7], gradients[8], gradients[9])
```

```python
import functools

import jax
import jax.numpy as jnp
from jax import lax
from jax.experimental import pallas as pl
from jax.experimental.pallas import tpu as pltpu
from jax.sharding import PartitionSpec as P

HEAD_DIM = 128
ATT_BLOCK = 512


EPSILON = 1e-05


def product(left_side, right_side):
    return jnp.dot(left_side, right_side, preferred_element_type=jnp.float32)


def inner_rows(left_side, right_side):
    return lax.dot_general(
        left_side, right_side, (((0,), (0,)), ((), ())), preferred_element_type=jnp.float32
    )


def outer_cols(left_side, right_side):
    return lax.dot_general(
        left_side, right_side, (((1,), (1,)), ((), ())), preferred_element_type=jnp.float32
    )


def silu_backward(gate_value, up_value, grad_inner):
    sigmoid_gate = jax.nn.sigmoid(gate_value)
    grad_gate = grad_inner * up_value * sigmoid_gate * (1.0 + gate_value * (1.0 - sigmoid_gate))
    grad_up = grad_inner * gate_value * sigmoid_gate
    return (grad_gate.astype(jnp.bfloat16), grad_up.astype(jnp.bfloat16))


def snake(count):
    deep = 4 if count % 4 == 0 else 1
    wide = count // deep
    if deep == 1 or wide == 1:
        return list(range(count))
    order = []
    for z in range(deep):
        across = range(1, wide) if z % 2 == 0 else range(wide - 1, 0, -1)
        order += [z * wide + y for y in across]
    return order + [z * wide for z in range(deep - 1, -1, -1)]


def after(value, *others):
    return lax.optimization_barrier((value, *others))[0]


def low(value):
    return value.astype(jnp.bfloat16)


def wide(value):
    return value.astype(jnp.float32)


class Links:
    def __init__(self, mesh):
        self.n = mesh.shape["seq"]
        self.nd = mesh.shape["dp"]
        self.order = snake(self.n)
        n = self.n
        self.right = [(self.order[k], self.order[(k + 1) % n]) for k in range(n)]
        self.left = [(b, a) for a, b in self.right]

    def place(self):
        me = lax.axis_index("seq")
        table = [0] * self.n
        for k, i in enumerate(self.order):
            table[i] = k
        return sum(jnp.where(me == i, table[i], 0) for i in range(self.n))

    def owner(self, place, distance):
        spot = (place + distance) % self.n
        return sum(jnp.where(spot == k, self.order[k], 0) for k in range(self.n))

    def to_right(self, x):
        return lax.ppermute(x, "seq", self.right)

    def to_left(self, x):
        return lax.ppermute(x, "seq", self.left)

    def swap(self, x, axis, r):
        count = self.n if axis == "seq" else self.nd
        return lax.ppermute(x, axis, [(k, k ^ r) for k in range(count)])

    def gather(self, x, watch=None):
        half = self.n // 2
        out = {0: x}
        from_left = from_right = x
        rows = x.shape[0] // 2
        for s in range(1, half):
            from_left, from_right = self.to_right(from_left), self.to_left(from_right)
            out[-s], out[s] = from_left, from_right
        out["a"] = self.to_right(from_left[:rows])
        out["b"] = self.to_left(from_right[rows:])
        return out

    def scatter(self, part):
        half = self.n // 2
        going_left = self.to_left(low(part("b")))
        going_right = self.to_right(low(part("a")))
        for s in range(half - 1, 0, -1):
            lshare, rshare = part(-s), part(s)
            if s == half - 1:
                rows = lshare.shape[0] // 2
                lshare = jnp.concatenate([lshare[:rows], lshare[rows:] + wide(going_left)])
                rshare = jnp.concatenate([rshare[:rows] + wide(going_right), rshare[rows:]])
            else:
                lshare = lshare + wide(going_left)
                rshare = rshare + wide(going_right)
            going_left, going_right = self.to_left(low(lshare)), self.to_right(low(rshare))
        return part(0), going_left, going_right


VMEM_LIMIT = 56 * 1024 * 1024
ANYWHERE = pl.BlockSpec(memory_space=pl.ANY)
IN_VMEM = pl.BlockSpec(memory_space=pltpu.VMEM)
IN_SMEM = pl.BlockSpec(memory_space=pltpu.SMEM)
LOG2_E = 1.4426950408889634
DEAD = 1e30


def nt_dot(a, b):
    return lax.dot_general(a, b, (((1,), (1,)), ((), ())), preferred_element_type=jnp.float32)


def tn_dot(a, b):
    return lax.dot_general(a, b, (((0,), (0,)), ((), ())), preferred_element_type=jnp.float32)


def call(body, operands, specs, outs, out_specs, scratch, flops, moved, name):
    return pl.pallas_call(
        body,
        name=name,
        in_specs=specs,
        out_specs=tuple(out_specs),
        out_shape=tuple(jax.ShapeDtypeStruct(s, t) for s, t in outs),
        scratch_shapes=scratch,
        compiler_params=pltpu.CompilerParams(vmem_limit_bytes=VMEM_LIMIT),
        cost_estimate=pl.CostEstimate(flops=flops, bytes_accessed=moved, transcendentals=0),
    )(*operands)


def start_all(copies):
    for copy in copies:
        copy.start()
    return copies


def wait_all(copies):
    for copy in copies:
        copy.wait()


def causal_mask(block):
    key_at = lax.broadcasted_iota(jnp.int32, (block, block), 0)
    query_at = lax.broadcasted_iota(jnp.int32, (block, block), 1)
    return key_at <= query_at


def forward_body(n, info, *refs):
    q_in, kv_in = refs[:n], refs[n : 2 * n]
    outs, stats, ot = refs[2 * n : 3 * n], refs[3 * n], refs[3 * n + 1]
    qs, ks, vs, vt, mixed, sems = refs[3 * n + 2 :]
    me, length = info[0], info[1]
    count, width = q_in[0].shape
    heads = width // HEAD_DIM
    total = n * count
    blocks = total // ATT_BLOCK
    copies = []
    for r in range(n):
        rows = pl.ds(pl.multiple_of((me ^ r) * count, count), count)
        for k, (src, dst) in enumerate(
            (
                (kv_in[r].at[:, pl.ds(0, width)], ks),
                (kv_in[r].at[:, pl.ds(width, width)], vs),
                (q_in[r], qs),
            )
        ):
            copies.append(pltpu.make_async_copy(src, dst.at[rows], sems.at[3 * r + k]))
    wait_all(start_all(copies))
    factor = HEAD_DIM ** (-0.5) * LOG2_E

    def transpose_values(b, _):
        at = pl.ds(pl.multiple_of(b * ATT_BLOCK, ATT_BLOCK), ATT_BLOCK)
        vt[:, at] = vs[at, :].T
        return 0

    lax.fori_loop(0, blocks, transpose_values, 0)
    live = jnp.minimum((length + ATT_BLOCK - 1) // ATT_BLOCK, blocks)

    def tile(qi, kj, state, masked):
        new = []
        q_at = pl.ds(pl.multiple_of(qi * ATT_BLOCK, ATT_BLOCK), ATT_BLOCK)
        k_at = pl.ds(pl.multiple_of(kj * ATT_BLOCK, ATT_BLOCK), ATT_BLOCK)
        for h in range(heads):
            cols = slice(h * HEAD_DIM, (h + 1) * HEAD_DIM)
            top, total_sum, acc = state[h]
            scores = nt_dot(ks[k_at, cols], qs[q_at, cols]) * factor
            if masked:
                scores = jnp.where(causal_mask(ATT_BLOCK), scores, -DEAD)
            higher = jnp.maximum(top, jnp.max(scores, axis=0, keepdims=True))
            weights = jnp.exp2(scores - higher)
            shrink = jnp.exp2(top - higher)
            total_sum = total_sum * shrink + jnp.sum(weights, axis=0, keepdims=True)
            acc = acc * shrink + jnp.dot(
                vt[cols, k_at], weights.astype(jnp.bfloat16), preferred_element_type=jnp.float32
            )
            new.append((higher, total_sum, acc))
        return tuple(new)

    stats[...] = jnp.full(stats.shape, DEAD, jnp.float32)

    def query_block(qi, _):
        first = tuple(
            (
                jnp.full((1, ATT_BLOCK), -DEAD, jnp.float32),
                jnp.zeros((1, ATT_BLOCK), jnp.float32),
                jnp.zeros((HEAD_DIM, ATT_BLOCK), jnp.float32),
            )
            for _ in range(heads)
        )
        state = lax.fori_loop(0, qi, lambda kj, s: tile(qi, kj, s, False), first)
        state = tile(qi, qi, state, True)
        q_at = pl.ds(pl.multiple_of(qi * ATT_BLOCK, ATT_BLOCK), ATT_BLOCK)
        spot = qi * ATT_BLOCK + lax.broadcasted_iota(jnp.int32, (1, ATT_BLOCK), 1)
        alive = spot < length
        for h in range(heads):
            cols = slice(h * HEAD_DIM, (h + 1) * HEAD_DIM)
            top, total_sum, acc = state[h]
            scaled = acc * jnp.where(alive, 1.0 / total_sum, 0.0)
            ot[cols, q_at] = scaled
            mixed[q_at, cols] = scaled.T.astype(jnp.bfloat16)
            stats[h : h + 1, q_at] = jnp.where(alive, top + jnp.log2(total_sum), DEAD)
        return 0

    lax.fori_loop(0, live, query_block, 0)

    def dead_block(qi, _):
        q_at = pl.ds(pl.multiple_of(qi * ATT_BLOCK, ATT_BLOCK), ATT_BLOCK)
        mixed[q_at, :] = jnp.zeros((ATT_BLOCK, width), jnp.bfloat16)
        ot[:, q_at] = jnp.zeros((width, ATT_BLOCK), jnp.float32)
        return 0

    lax.fori_loop(live, blocks, dead_block, 0)
    copies = []
    for r in range(n):
        rows = pl.ds(pl.multiple_of((me ^ r) * count, count), count)
        copies.append(pltpu.make_async_copy(mixed.at[rows], outs[r], sems.at[r]))
    wait_all(start_all(copies))


def attention_forward(info, q_blocks, kv_blocks):
    n = len(q_blocks)
    count, width = q_blocks[0].shape
    total = n * count
    got = call(
        functools.partial(forward_body, n),
        [info, *q_blocks, *kv_blocks],
        [IN_SMEM] + [ANYWHERE] * (2 * n),
        [((count, width), jnp.bfloat16)] * n
        + [((8, total), jnp.float32), ((width, total), jnp.float32)],
        [ANYWHERE] * n + [IN_VMEM] * 2,
        [pltpu.VMEM((total, width), jnp.bfloat16)] * 3
        + [pltpu.VMEM((width, total), jnp.bfloat16), pltpu.VMEM((total, width), jnp.bfloat16)]
        + [pltpu.SemaphoreType.DMA((3 * n,))],
        16 * 2 * total * total * width // 2,
        10 * total * width,
        "attention_forward",
    )
    return got[:n], got[n], got[n + 1]


def backward_body(n, info, *refs):
    q_in, kv_in, g_in = refs[:n], refs[n : 2 * n], refs[2 * n : 3 * n]
    stats, ot = refs[3 * n], refs[3 * n + 1]
    refs = refs[3 * n + 2 :]
    dq_out, dkv_out = refs[:n], refs[n : 2 * n]
    qs, ks, vs, gs, kt, delta, dqt, dk, dv, dq_low, dkv_low, sems = refs[2 * n :]
    me, length = info[0], info[1]
    count, width = q_in[0].shape
    heads = width // HEAD_DIM
    total = n * count
    blocks = total // ATT_BLOCK
    copies = []
    for r in range(n):
        rows = pl.ds(pl.multiple_of((me ^ r) * count, count), count)
        for k, (src, dst) in enumerate(
            (
                (kv_in[r].at[:, pl.ds(0, width)], ks),
                (kv_in[r].at[:, pl.ds(width, width)], vs),
                (q_in[r], qs),
                (g_in[r], gs),
            )
        ):
            copies.append(pltpu.make_async_copy(src, dst.at[rows], sems.at[4 * r + k]))
    start_all(copies)
    live = jnp.minimum((length + ATT_BLOCK - 1) // ATT_BLOCK, blocks)
    scale = HEAD_DIM ** (-0.5)
    factor = scale * LOG2_E

    def clear(b, _):
        at = pl.ds(pl.multiple_of(b * ATT_BLOCK, ATT_BLOCK), ATT_BLOCK)
        dqt[:, at] = jnp.zeros((width, ATT_BLOCK), jnp.float32)
        dk[at, :] = jnp.zeros((ATT_BLOCK, width), jnp.float32)
        dv[at, :] = jnp.zeros((ATT_BLOCK, width), jnp.float32)
        return 0

    lax.fori_loop(0, blocks, clear, 0)
    wait_all(copies)

    def prepare(b, _):
        at = pl.ds(pl.multiple_of(b * ATT_BLOCK, ATT_BLOCK), ATT_BLOCK)
        kt[:, at] = ks[at, :].T
        both = gs[at, :].astype(jnp.float32).T * ot[:, at]
        for h in range(heads):
            cols = slice(h * HEAD_DIM, (h + 1) * HEAD_DIM)
            delta[h : h + 1, at] = jnp.sum(both[cols], axis=0, keepdims=True)
        return 0

    lax.fori_loop(0, blocks, prepare, 0)

    def tile(qi, kj, masked):
        q_at = pl.ds(pl.multiple_of(qi * ATT_BLOCK, ATT_BLOCK), ATT_BLOCK)
        k_at = pl.ds(pl.multiple_of(kj * ATT_BLOCK, ATT_BLOCK), ATT_BLOCK)
        for h in range(heads):
            cols = slice(h * HEAD_DIM, (h + 1) * HEAD_DIM)
            q, g = qs[q_at, cols], gs[q_at, cols]
            scores = nt_dot(ks[k_at, cols], q) * factor - stats[h : h + 1, q_at]
            if masked:
                scores = jnp.where(causal_mask(ATT_BLOCK), scores, -DEAD)
            weights = jnp.exp2(scores)
            grad_weights = nt_dot(vs[k_at, cols], g)
            grad_scores = (weights * (grad_weights - delta[h : h + 1, q_at])).astype(jnp.bfloat16)
            dv[k_at, cols] += jnp.dot(
                weights.astype(jnp.bfloat16), g, preferred_element_type=jnp.float32
            )
            dk[k_at, cols] += jnp.dot(grad_scores, q, preferred_element_type=jnp.float32)
            dqt[cols, q_at] += jnp.dot(
                kt[cols, k_at], grad_scores, preferred_element_type=jnp.float32
            )

    def query_block(qi, _):
        def step(kj, _):
            tile(qi, kj, False)
            return 0

        lax.fori_loop(0, qi, step, 0)
        tile(qi, qi, True)
        return 0

    lax.fori_loop(0, live, query_block, 0)

    def finish(b, _):
        at = pl.ds(pl.multiple_of(b * ATT_BLOCK, ATT_BLOCK), ATT_BLOCK)
        dq_low[at, :] = (dqt[:, at] * scale).T.astype(jnp.bfloat16)
        dkv_low[at, :width] = (dk[at, :] * scale).astype(jnp.bfloat16)
        dkv_low[at, width:] = dv[at, :].astype(jnp.bfloat16)
        return 0

    lax.fori_loop(0, blocks, finish, 0)
    copies = []
    for r in range(n):
        rows = pl.ds(pl.multiple_of((me ^ r) * count, count), count)
        copies.append(pltpu.make_async_copy(dq_low.at[rows], dq_out[r], sems.at[2 * r]))
        copies.append(pltpu.make_async_copy(dkv_low.at[rows], dkv_out[r], sems.at[2 * r + 1]))
    wait_all(start_all(copies))


def attention_backward(info, q_blocks, kv_blocks, g_blocks, stats, ot):
    n = len(q_blocks)
    count, width = q_blocks[0].shape
    total = n * count
    low_all = pltpu.VMEM((total, width), jnp.bfloat16)
    got = call(
        functools.partial(backward_body, n),
        [info, *q_blocks, *kv_blocks, *g_blocks, stats, ot],
        [IN_SMEM] + [ANYWHERE] * (3 * n) + [IN_VMEM] * 2,
        [((count, width), jnp.bfloat16)] * n + [((count, 2 * width), jnp.bfloat16)] * n,
        [ANYWHERE] * (2 * n),
        [low_all] * 4
        + [
            pltpu.VMEM((width, total), jnp.bfloat16),
            pltpu.VMEM((8, total), jnp.float32),
            pltpu.VMEM((width, total), jnp.float32),
            pltpu.VMEM((total, width), jnp.float32),
            pltpu.VMEM((total, width), jnp.float32),
            low_all,
            pltpu.VMEM((total, 2 * width), jnp.bfloat16),
            pltpu.SemaphoreType.DMA((4 * n,)),
        ],
        40 * 2 * total * total * width // 2,
        20 * total * width,
        "attention_backward",
    )
    return got[:n], got[n:]


def aligned(index, unit):
    return pl.multiple_of(index * unit, unit)


def pack_body(n, info, keys, values, *refs):
    outs, sems = refs[:n], refs[n]
    me = info[0]
    width = outs[0].shape[1] // 2
    copies = []
    for r in range(n):
        cols = pl.ds(aligned(me ^ r, width), width)
        copies.append(
            pltpu.make_async_copy(keys.at[:, cols], outs[r].at[:, pl.ds(0, width)], sems.at[2 * r])
        )
        copies.append(
            pltpu.make_async_copy(
                values.at[:, cols], outs[r].at[:, pl.ds(width, width)], sems.at[2 * r + 1]
            )
        )
    wait_all(start_all(copies))


def pack_keys_values(n, info, keys, values):
    count, depth = keys.shape
    return call(
        functools.partial(pack_body, n),
        [info, keys, values],
        [IN_SMEM, ANYWHERE, ANYWHERE],
        [((count, 2 * depth // n), jnp.bfloat16)] * n,
        [IN_VMEM] * n,
        [pltpu.SemaphoreType.DMA((2 * n,))],
        0,
        8 * count * depth,
        "pack_keys_values",
    )


GAIN_ROWS = 32


def norm_parts(v):
    return lax.rsqrt(jnp.mean(v * v, axis=-1, keepdims=True) + EPSILON)


def query_body(n, info, x, *refs):
    pieces = 2 * (n + 1)
    mine, other = refs[: n + 1], refs[n + 1 : pieces]
    q_out = refs[pieces : pieces + n]
    normed, gains, weight_out = refs[pieces + n : pieces + n + 3]
    weight, gain_rows, sems, out_sem = refs[pieces + n + 3 :]
    me, core = info[0], info[2]
    depth = x.shape[1]
    half = mine[0].shape[1]
    wrows = mine[0].shape[0] - GAIN_ROWS
    upper = (wrows + GAIN_ROWS) // 2 - GAIN_ROWS
    copies = []
    for k in range(n + 1):
        who = info[3 + min(k, n - 1)]
        if k < n - 1:
            skip, rows, at = GAIN_ROWS, wrows, who * wrows
        elif k == n - 1:
            skip, rows, at = GAIN_ROWS, upper, who * wrows
        else:
            skip, rows, at = 0, wrows - upper, who * wrows + upper
        at = pl.multiple_of(at, 16)
        for j, (ref, side) in enumerate(((mine, core), (other, 1 - core))):
            copies.append(
                pltpu.make_async_copy(
                    ref[k].at[pl.ds(skip, rows)],
                    weight.at[pl.ds(at, rows), pl.ds(aligned(side, half), half)],
                    sems.at[3 * k + j],
                )
            )
        if k < n:
            copies.append(
                pltpu.make_async_copy(
                    mine[k].at[pl.ds(0, 16)],
                    gain_rows.at[pl.ds(aligned(who, 16), 16)],
                    sems.at[3 * k + 2],
                )
            )
    wait_all(start_all(copies))
    save = pltpu.make_async_copy(weight, weight_out, out_sem)
    save.start()
    share = depth // n
    for o in range(n):
        row = gain_rows[o * 16 : o * 16 + 16, : 2 * share].astype(jnp.float32)
        gains[0:1, o * share : (o + 1) * share] = row[0:1, :share]
        gains[1:2, o * share : (o + 1) * share] = row[0:1, share:]
    v = x[...].astype(jnp.float32)
    normed[...] = (v * norm_parts(v) * gains[0:1, :]).astype(jnp.bfloat16)
    for r in range(n):
        cols = pl.ds(aligned(me ^ r, share), share)
        q_out[r][...] = jnp.dot(
            normed[...], weight[:, cols], preferred_element_type=jnp.float32
        ).astype(jnp.bfloat16)
    save.wait()


def project_queries(n, info, x, mine, other):
    count, depth = x.shape
    got = call(
        functools.partial(query_body, n),
        [info, x, *mine, *other],
        [IN_SMEM, IN_VMEM] + [ANYWHERE] * (2 * n + 2),
        [((count, depth // n), jnp.bfloat16)] * n
        + [
            ((count, depth), jnp.bfloat16),
            ((8, depth), jnp.float32),
            ((depth, depth), jnp.bfloat16),
        ],
        [IN_VMEM] * (n + 2) + [ANYWHERE],
        [
            pltpu.VMEM((depth, depth), jnp.bfloat16),
            pltpu.VMEM((n * 16, mine[0].shape[1]), jnp.bfloat16),
            pltpu.SemaphoreType.DMA((3 * n + 3,)),
            pltpu.SemaphoreType.DMA,
        ],
        2 * count * depth * depth,
        6 * depth * depth,
        "project_queries",
    )
    return got[:n], got[n], got[n + 1], got[n + 2]


def stack_body(n, info, *refs):
    blocks, out, sems = refs[: n + 1], refs[n + 1], refs[n + 2]
    wrows = blocks[0].shape[0]
    copies = []
    for k in range(n + 1):
        who = info[3 + min(k, n - 1)]
        rows = blocks[k].shape[0]
        at = who * wrows + (rows if k == n else 0)
        copies.append(
            pltpu.make_async_copy(
                blocks[k], out.at[pl.ds(pl.multiple_of(at, 16), rows)], sems.at[k]
            )
        )
    wait_all(start_all(copies))


def stack_ring(n, info, blocks):
    wrows, width = blocks[0].shape
    return call(
        functools.partial(stack_body, n),
        [info, *blocks],
        [IN_SMEM] + [ANYWHERE] * (n + 1),
        [((n * wrows, width), jnp.bfloat16)],
        [IN_VMEM],
        [pltpu.SemaphoreType.DMA((n + 1,))],
        0,
        4 * n * wrows * width,
        "stack_ring",
    )[0]


def hidden_body(n, nd, info, x, gains, *refs):
    blocks, parts = refs[:n], refs[n : n + nd]
    hidden, normed, mixed, weight_out = refs[n + nd : n + nd + 4]
    weight, sems, out_sem = refs[n + nd + 4 :]
    me, dp = info[0], info[1]
    share, quarter = blocks[0].shape[1], parts[0].shape[1]
    copies = []
    for r in range(nd):
        cols = pl.ds(aligned(dp ^ r, quarter), quarter)
        copies.append(pltpu.make_async_copy(parts[r], weight.at[:, cols], sems.at[r]))
    for r in range(n):
        cols = pl.ds(aligned(me ^ r, share), share)
        copies.append(pltpu.make_async_copy(blocks[r], mixed.at[:, cols], sems.at[nd + r]))
    wait_all(start_all(copies))
    save = pltpu.make_async_copy(weight, weight_out, out_sem)
    save.start()
    depth = x.shape[1]
    piece = 512

    def step(c, total):
        cols = pl.ds(aligned(c, piece), piece)
        v = x[:, cols].astype(jnp.float32) + jnp.dot(
            mixed[...], weight[:, cols], preferred_element_type=jnp.float32
        )
        hidden[:, cols] = v
        return total + jnp.sum(v * v, axis=-1, keepdims=True)

    total = lax.fori_loop(0, depth // piece, step, jnp.zeros((x.shape[0], 1), jnp.float32))
    normed[...] = (
        hidden[...] * lax.rsqrt(total / depth + EPSILON) * gains[1:2, :]
    ).astype(jnp.bfloat16)
    save.wait()


def project_mixed(n, nd, info, x, gains, blocks, parts):
    count, depth = x.shape
    return call(
        functools.partial(hidden_body, n, nd),
        [info, x, gains, *blocks, *parts],
        [IN_SMEM, IN_VMEM, IN_VMEM] + [ANYWHERE] * (n + nd),
        [
            ((count, depth), jnp.float32),
            ((count, depth), jnp.bfloat16),
            ((count, depth), jnp.bfloat16),
            ((depth, depth), jnp.bfloat16),
        ],
        [IN_VMEM] * 3 + [ANYWHERE],
        [
            pltpu.VMEM((depth, depth), jnp.bfloat16),
            pltpu.SemaphoreType.DMA((n + nd,)),
            pltpu.SemaphoreType.DMA,
        ],
        2 * count * depth * depth,
        6 * depth * depth,
        "project_mixed",
    )


def norm_grad(v, gain, upstream):
    scale = norm_parts(v)
    weighted = upstream * gain
    through = weighted * scale - v * (scale**3) * jnp.mean(weighted * v, axis=-1, keepdims=True)
    return through, jnp.sum(upstream * v * scale, axis=0, keepdims=True)


def branch_body(n, nd, info, hidden, gains, cotangent, own, first, second, weight_in, *refs):
    gm_out, cols_out = refs[:n], refs[n : n + nd]
    grad_hidden, gain_part, branch, weight, sem = refs[n + nd :]
    me, dp = info[0], info[1]
    load = pltpu.make_async_copy(weight_in, weight, sem)
    load.start()
    upstream = own[...] + first[...].astype(jnp.float32) + second[...].astype(jnp.float32)
    through, gain = norm_grad(hidden[...], gains[1:2, :], upstream)
    gain_part[...] = jnp.broadcast_to(gain, gain_part.shape)
    total = cotangent[...].astype(jnp.float32) + through
    grad_hidden[...] = total
    branch[...] = total.astype(jnp.bfloat16)
    quarter = cols_out[0].shape[1]
    for r in range(nd):
        cols_out[r][...] = branch[:, pl.ds(aligned(dp ^ r, quarter), quarter)]
    load.wait()
    share = gm_out[0].shape[1]
    for r in range(n):
        rows = pl.ds(aligned(me ^ r, share), share)
        gm_out[r][...] = nt_dot(branch[...], weight[rows, :]).astype(jnp.bfloat16)


def branch_gradient(n, nd, info, hidden, gains, cotangent, sums, weight):
    count, depth = cotangent.shape
    got = call(
        functools.partial(branch_body, n, nd),
        [info, hidden, gains, cotangent, *sums, weight],
        [IN_SMEM] + [IN_VMEM] * 6 + [ANYWHERE],
        [((count, depth // n), jnp.bfloat16)] * n
        + [((count, depth // nd), jnp.bfloat16)] * nd
        + [((count, depth), jnp.float32), ((8, depth), jnp.float32)],
        [IN_VMEM] * (n + nd + 2),
        [
            pltpu.VMEM((count, depth), jnp.bfloat16),
            pltpu.VMEM((depth, depth), jnp.bfloat16),
            pltpu.SemaphoreType.DMA,
        ],
        2 * count * depth * depth,
        6 * depth * depth,
        "branch_gradient",
    )
    return got[:n], got[n : n + nd], got[n + nd], got[n + nd + 1]


def sort_body(n, nd, info, *refs):
    blocks, out, cols_out = refs[:n], refs[n], refs[n + 1 : n + 1 + nd]
    rows, sems = refs[n + 1 + nd :]
    me, dp = info[0], info[1]
    share, quarter = blocks[0].shape[1], cols_out[0].shape[1]
    copies = []
    for r in range(n):
        cols = pl.ds(aligned(me ^ r, share), share)
        copies.append(pltpu.make_async_copy(blocks[r], rows.at[:, cols], sems.at[r]))
    wait_all(start_all(copies))
    copies = [pltpu.make_async_copy(rows, out, sems.at[0])]
    for r in range(nd):
        cols = pl.ds(aligned(dp ^ r, quarter), quarter)
        copies.append(pltpu.make_async_copy(rows.at[:, cols], cols_out[r], sems.at[1 + r]))
    wait_all(start_all(copies))


def sort_columns(n, nd, info, blocks):
    count, share = blocks[0].shape
    depth = n * share
    got = call(
        functools.partial(sort_body, n, nd),
        [info, *blocks],
        [IN_SMEM] + [ANYWHERE] * n,
        [((count, depth), jnp.bfloat16)] + [((count, depth // nd), jnp.bfloat16)] * nd,
        [ANYWHERE] * (nd + 1),
        [
            pltpu.VMEM((count, depth), jnp.bfloat16),
            pltpu.SemaphoreType.DMA((max(n, nd + 1),)),
        ],
        0,
        6 * count * depth,
        "sort_columns",
    )
    return got[0], got[1:]


def split_body(n, info, *refs):
    blocks, keys, values, sems = refs[:n], refs[n], refs[n + 1], refs[n + 2]
    me = info[0]
    share = blocks[0].shape[1] // 2
    copies = []
    for r in range(n):
        cols = pl.ds(aligned(me ^ r, share), share)
        copies.append(
            pltpu.make_async_copy(blocks[r].at[:, pl.ds(0, share)], keys.at[:, cols], sems.at[2 * r])
        )
        copies.append(
            pltpu.make_async_copy(
                blocks[r].at[:, pl.ds(share, share)], values.at[:, cols], sems.at[2 * r + 1]
            )
        )
    wait_all(start_all(copies))


def split_keys_values(n, info, blocks):
    count, share = blocks[0].shape
    depth = n * share // 2
    return call(
        functools.partial(split_body, n),
        [info, *blocks],
        [IN_SMEM] + [ANYWHERE] * n,
        [((count, depth), jnp.bfloat16)] * 2,
        [IN_VMEM] * 2,
        [pltpu.SemaphoreType.DMA((2 * n,))],
        0,
        8 * count * depth,
        "split_keys_values",
    )


def input_body(x, gains, grad_query, grad_hidden, weight, out, gain_part, upstream):
    piece = 512

    def step(c, _):
        rows = pl.ds(aligned(c, piece), piece)
        upstream[:, rows] = nt_dot(grad_query[...], weight[rows, :])
        return 0

    lax.fori_loop(0, x.shape[1] // piece, step, 0)
    through, gain = norm_grad(x[...].astype(jnp.float32), gains[0:1, :], upstream[...])
    gain_part[...] = jnp.broadcast_to(gain, gain_part.shape)
    out[...] = (grad_hidden[...] + through).astype(jnp.bfloat16)


def input_gradient(x, gains, grad_query, grad_hidden, weight):
    count, depth = x.shape
    return call(
        input_body,
        [x, gains, grad_query, grad_hidden, weight],
        [IN_VMEM] * 5,
        [((count, depth), jnp.bfloat16), ((8, depth), jnp.float32)],
        [IN_VMEM] * 2,
        [pltpu.VMEM((count, depth), jnp.float32)],
        2 * count * depth * depth,
        6 * depth * depth,
        "input_gradient",
    )


def tree_sum(parts):
    while len(parts) > 1:
        parts = [parts[k] + parts[k + 1] for k in range(0, len(parts), 2)]
    return parts[0]


def columns(x, start, width):
    return lax.dynamic_slice_in_dim(x, start, width, 1)


def rows_of(x, start, count):
    return lax.dynamic_slice_in_dim(x, start, count, 0)


def make_local(mesh):
    net = Links(mesh)
    n, nd = net.n, net.nd
    dp_order = list(range(0, nd, 2)) + list(range(1, nd, 2))
    half_way = n // 2
    ring_order = [0] + [s for k in range(1, half_way) for s in (-k, k)] + ["a", "b"]

    def exchange(blocks, axis="seq"):
        return [b if r == 0 else net.swap(b, axis, r) for r, b in enumerate(blocks)]

    def keyed_rows(place, key, count):
        if key in ("a", "b"):
            first = net.owner(place, half_way) * count
            return (first if key == "a" else first + count // 2), count // 2
        return net.owner(place, key) * count, count

    def dp_rows(x):
        near = jnp.concatenate([x] + [net.swap(x, "dp", r) for r in range(2, nd, 2)], 0)
        return jnp.concatenate([near, net.swap(near, "dp", 1)], 0)

    def dp_parts(x):
        near = {0: x}
        for r in range(2, nd, 2):
            near[r] = net.swap(x, "dp", r)
        far = {r + 1: net.swap(v, "dp", 1) for r, v in near.items()}
        return {**near, **far}

    def dp_total(x, mine):
        core = mine % 2
        half = x.shape[1] // 2
        x = low(x)
        kept = wide(columns(x, core * half, half))
        kept = low(kept + wide(net.swap(columns(x, (1 - core) * half, half), "dp", 1)))
        total = low(
            tree_sum([wide(kept)] + [wide(net.swap(kept, "dp", r)) for r in range(2, nd, 2)])
        )
        other = net.swap(total, "dp", 1)
        first = core == 0
        return jnp.concatenate(
            [wide(jnp.where(first, total, other)), wide(jnp.where(first, other, total))], 1
        )

    def local(
        layer_input,
        global_keys,
        global_values,
        lengths,
        attn_gain,
        query_weight,
        out_weight,
        ffn_gain,
        gate_weight,
        up_weight,
        down_weight,
        cotangent,
    ):
        length = lengths[0]
        me, mine = lax.axis_index("seq"), lax.axis_index("dp")
        core = mine % 2
        place = net.place()
        depth = layer_input.shape[1]
        wrows = query_weight.shape[0]
        quarter = depth // nd
        owners = [net.owner(place, key) for key in ring_order[:-2]] + [net.owner(place, half_way)]
        info = jnp.stack([me, mine, core, *owners]).astype(jnp.int32)
        length_info = jnp.stack([me, length]).astype(jnp.int32)

        half = depth // 2
        gains = jnp.concatenate([attn_gain, ffn_gain])
        per_half = jnp.tile(gains, half // gains.shape[0])
        gain_rows = jnp.broadcast_to(per_half[None], (GAIN_ROWS, half))
        piece = jnp.concatenate([gain_rows, columns(query_weight, core * half, half)], 0)
        got = net.gather(piece)
        fetched = [got[k] for k in ring_order]
        kv_sent = pack_keys_values(n, info, global_keys, global_values)
        kv_blocks = exchange(kv_sent)
        q_sent, normed, gains, full_query = project_queries(
            n, info, layer_input, fetched, [net.swap(b, "dp", 1) for b in fetched]
        )
        q_blocks = exchange(q_sent)
        mixed_sent, stats, ot = attention_forward(length_info, q_blocks, kv_blocks)

        out_piece = columns(out_weight, mine * quarter, quarter)
        out_got = net.gather(after(out_piece, got["a"]))
        out_quarter = stack_ring(n, info, [out_got[k] for k in ring_order])
        out_parts = dp_parts(out_quarter)

        mixed_blocks = exchange(mixed_sent)
        hidden, normed_ffn, mixed, full_out = project_mixed(
            n, nd, info, layer_input, gains, mixed_blocks, [out_parts[r] for r in range(nd)]
        )

        cot = net.gather(after(cotangent, q_blocks[n - 1]))
        nf = net.gather(normed_ffn)
        inner, grad_gate, grad_up = {}, {}, {}
        for key in nf:
            gate_value = outer_cols(nf[key], gate_weight)
            up_value = outer_cols(nf[key], up_weight)
            grad_inner = outer_cols(cot[key], down_weight)
            inner[key] = low(jax.nn.silu(gate_value) * up_value)
            grad_gate[key], grad_up[key] = silu_backward(gate_value, up_value, grad_inner)

        def grad_share(key):
            return product(grad_gate[key], gate_weight) + product(grad_up[key], up_weight)

        grad_sums = net.scatter(grad_share)
        gm_sent, branch_cols, grad_hidden, ffn_gain_part = branch_gradient(
            n, nd, info, hidden, gains, cotangent, grad_sums, full_out
        )
        gm_blocks = exchange(gm_sent)

        def joined(blocks):
            return jnp.concatenate([blocks[k] for k in ring_order], 0)

        nf_all, cot_all = joined(nf), joined(cot)
        gate_grad = dp_total(inner_rows(joined(grad_gate), nf_all), mine)
        up_grad = dp_total(inner_rows(joined(grad_up), nf_all), mine)
        down_grad = dp_total(inner_rows(joined(inner), cot_all), mine)

        inner_late = {k: after(v, gm_blocks[n - 1]) for k, v in inner.items()}
        own, first, second = net.scatter(lambda key: product(inner_late[key], down_weight))
        layer_output = low(hidden + (own + wide(first) + wide(second)))

        dq_sent, dkv_sent = attention_backward(
            length_info, q_blocks, kv_blocks, gm_blocks, stats, ot
        )
        grad_query, query_cols = sort_columns(n, nd, info, exchange(dq_sent))
        dkv_late = [after(b, grad_query) for b in dkv_sent]
        key_grad, value_grad = split_keys_values(n, info, exchange(dkv_late))
        input_grad, attn_gain_part = input_gradient(
            layer_input, gains, grad_query, grad_hidden, full_query
        )

        def dp_join(cols):
            got_cols = exchange(cols, "dp")
            return jnp.concatenate([got_cols[r] for r in dp_order], 0)

        out_part = inner_rows(dp_rows(mixed), dp_join(branch_cols))
        query_part = inner_rows(dp_rows(normed), dp_join(query_cols))
        gain_part = jnp.concatenate(
            [attn_gain_part[0].reshape(n, -1), ffn_gain_part[0].reshape(n, -1)], 1
        )

        def out_rows(key):
            return rows_of(out_part, *keyed_rows(place, key, wrows))

        def total_of(sums):
            own, first, second = sums
            return low(own + wide(first) + wide(second))

        out_mine = total_of(net.scatter(out_rows))

        def query_rows(key):
            first, size = keyed_rows(place, key, wrows)
            block = rows_of(query_part, first, size)
            if key == "a":
                return jnp.concatenate([block, jnp.zeros((16, quarter), jnp.float32)], 0)
            row = rows_of(gain_part, first // wrows, 1)
            row = jnp.pad(row, ((0, 0), (0, quarter - row.shape[1])))
            tail = jnp.broadcast_to(row, (16, quarter))
            if key == "b":
                return jnp.concatenate([block, tail], 0)
            middle = jnp.zeros((16, quarter), jnp.float32)
            return jnp.concatenate([block[: size // 2], middle, block[size // 2 :], tail], 0)

        query_mine = total_of(net.scatter(query_rows))

        def whole_rows(parts):
            first = jnp.zeros((), jnp.int32)
            out = jnp.zeros((wrows, depth), jnp.float32)
            for r, part in parts.items():
                out = lax.dynamic_update_slice(out, wide(part), (first, (mine ^ r) * quarter))
            return out

        out_grad = whole_rows(dp_parts(out_mine))
        query_parts = dp_parts(query_mine)
        body = {
            r: jnp.concatenate([v[: wrows // 2], v[wrows // 2 + 16 : wrows + 16]], 0)
            for r, v in query_parts.items()
        }
        query_grad = whole_rows(body)
        gain_sum = tree_sum([wide(query_parts[r][wrows + 16]) for r in range(nd)])
        attn_count = attn_gain.shape[0]
        return (
            layer_output,
            input_grad,
            key_grad,
            value_grad,
            gain_sum[:attn_count],
            query_grad,
            out_grad,
            gain_sum[attn_count : 2 * attn_count],
            gate_grad,
            up_grad,
            down_grad,
        )

    return local


def solution(mesh):
    placed = (
        P(("dp", "seq"), None),
        P(("dp", "seq"), None),
        P(("dp", "seq"), None),
        P("dp"),
        P("seq"),
        P("seq", None),
        P("seq", None),
        P("seq"),
        P("seq", None),
        P("seq", None),
        P("seq", None),
        P(("dp", "seq"), None),
    )
    return jax.shard_map(
        make_local(mesh),
        mesh=mesh,
        in_specs=placed,
        out_specs=(
            P(("dp", "seq"), None),
            P(("dp", "seq"), None),
            P(("dp", "seq"), None),
            P(("dp", "seq"), None),
            P("seq"),
            P("seq", None),
            P("seq", None),
            P("seq"),
            P("seq", None),
            P("seq", None),
            P("seq", None),
        ),
        check_vma=False,
    )
```

```python
import functools

import jax
import jax.numpy as jnp
from jax import lax
from jax.experimental import pallas as pl
from jax.experimental.pallas import tpu as pltpu
from jax.sharding import PartitionSpec as P

HEAD_DIM = 128
ATT_BLOCK = 512


EPSILON = 1e-05


def product(left_side, right_side):
    return jnp.dot(left_side, right_side, preferred_element_type=jnp.float32)


def inner_rows(left_side, right_side):
    return lax.dot_general(
        left_side, right_side, (((0,), (0,)), ((), ())), preferred_element_type=jnp.float32
    )


def outer_cols(left_side, right_side):
    return lax.dot_general(
        left_side, right_side, (((1,), (1,)), ((), ())), preferred_element_type=jnp.float32
    )


def snake(count):
    deep = 4 if count % 4 == 0 else 1
    wide = count // deep
    if deep == 1 or wide == 1:
        return list(range(count))
    order = []
    for z in range(deep):
        across = range(1, wide) if z % 2 == 0 else range(wide - 1, 0, -1)
        order += [z * wide + y for y in across]
    return order + [z * wide for z in range(deep - 1, -1, -1)]


def after(value, *others):
    return lax.optimization_barrier((value, *others))[0] if others else value


def tie(values, *others):
    return list(lax.optimization_barrier((*values, *others))[: len(values)])


def low(value):
    return value.astype(jnp.bfloat16)


def wide(value):
    return value.astype(jnp.float32)


class Links:
    def __init__(self, mesh):
        self.n = mesh.shape["seq"]
        self.nd = mesh.shape["dp"]
        self.order = snake(self.n)
        n = self.n
        self.right = [(self.order[k], self.order[(k + 1) % n]) for k in range(n)]
        self.left = [(b, a) for a, b in self.right]

    def group(self, d):
        return d % 2 * (self.nd // 2) + d // 2

    def place(self):
        me = lax.axis_index("seq")
        table = [0] * self.n
        for k, i in enumerate(self.order):
            table[i] = k
        return sum(jnp.where(me == i, table[i], 0) for i in range(self.n))

    def owner(self, place, distance):
        spot = (place + distance) % self.n
        return sum(jnp.where(spot == k, self.order[k], 0) for k in range(self.n))

    def to_right(self, x):
        return lax.ppermute(x, "seq", self.right)

    def to_left(self, x):
        return lax.ppermute(x, "seq", self.left)

    def to_heads(self, x, m):
        per, nx = self.n // self.nd, self.nd // 2
        pairs = []
        for d in range(self.nd):
            for s in range(self.n):
                j = s ^ m
                group = j // per
                to = group % nx * 2 + group // nx
                pairs.append((d * self.n + s, to * self.n + self.group(d) * per + j % per))
        return lax.ppermute(x, ("dp", "seq"), pairs)

    def swap(self, x, axis, r):
        count = self.n if axis == "seq" else self.nd
        return lax.ppermute(x, axis, [(k, k ^ r) for k in range(count)])


class RingGather:
    def __init__(self, net, x):
        self.net, self.got, self.at = net, {0: x}, 0
        self.from_left = self.from_right = x

    def step(self, *deps):
        net, half = self.net, self.net.n // 2
        self.at += 1
        left, right = self.from_left, self.from_right
        if self.at == half:
            rows = left.shape[0] // 2
            left, right = left[:rows], right[rows:]
        if self.at == 1 and half > 1:
            left = right = after(left, *deps)
        else:
            left, right = tie([left, right], *deps)
        self.from_left, self.from_right = net.to_right(left), net.to_left(right)
        keys = ("a", "b") if self.at == half else (-self.at, self.at)
        self.got[keys[0]], self.got[keys[1]] = self.from_left, self.from_right
        return self.from_left, self.from_right

    def rest(self):
        while self.at < self.net.n // 2:
            self.step()
        return self.got


class RowSum:
    def __init__(self, net, part):
        self.net, self.part, self.at = net, part, net.n // 2
        self.going_left = self.going_right = None

    def step(self, *deps):
        net, half, s = self.net, self.net.n // 2, self.at
        if s == half:
            left, right = self.part("b"), self.part("a")
        else:
            left, right = self.part(-s), self.part(s)
            if s == half - 1:
                rows = left.shape[0] // 2
                left = jnp.concatenate([left[:rows], left[rows:] + wide(self.going_left)])
                right = jnp.concatenate([right[:rows] + wide(self.going_right), right[rows:]])
            else:
                left = left + wide(self.going_left)
                right = right + wide(self.going_right)
        left, right = tie([low(left), low(right)], *deps)
        self.going_left, self.going_right = net.to_left(left), net.to_right(right)
        self.at -= 1
        return self.going_left, self.going_right

    def rest(self):
        while self.at:
            self.step()
        return self.part(0), self.going_left, self.going_right


VMEM_LIMIT = 56 * 1024 * 1024
COST_SHARE = 4
ANYWHERE = pl.BlockSpec(memory_space=pl.ANY)
IN_VMEM = pl.BlockSpec(memory_space=pltpu.VMEM)
IN_SMEM = pl.BlockSpec(memory_space=pltpu.SMEM)
LOG2_E = 1.4426950408889634
DEAD = 1e30


def nt_dot(a, b):
    return lax.dot_general(a, b, (((1,), (1,)), ((), ())), preferred_element_type=jnp.float32)


def tn_dot(a, b):
    return lax.dot_general(a, b, (((0,), (0,)), ((), ())), preferred_element_type=jnp.float32)


def call(body, operands, specs, outs, out_specs, scratch, flops, moved, name):
    return pl.pallas_call(
        body,
        name=name,
        in_specs=specs,
        out_specs=tuple(out_specs),
        out_shape=tuple(jax.ShapeDtypeStruct(s, t) for s, t in outs),
        scratch_shapes=scratch,
        compiler_params=pltpu.CompilerParams(vmem_limit_bytes=VMEM_LIMIT),
        cost_estimate=pl.CostEstimate(
            flops=flops // COST_SHARE, bytes_accessed=moved // COST_SHARE, transcendentals=0
        ),
    )(*operands)


def aligned(index, unit):
    return pl.multiple_of(index * unit, unit)


def start_all(copies):
    for copy in copies:
        copy.start()
    return copies


def wait_all(copies):
    for copy in copies:
        copy.wait()


def causal_mask(block):
    key_at = lax.broadcasted_iota(jnp.int32, (block, block), 0)
    query_at = lax.broadcasted_iota(jnp.int32, (block, block), 1)
    return key_at <= query_at


def forward_body(n, info, *refs):
    q_in, kv_in = refs[:n], refs[n : 2 * n]
    outs, stats, ot = refs[2 * n : 3 * n], refs[3 * n], refs[3 * n + 1]
    qs, ks, vs, vt, mixed, sems = refs[3 * n + 2 :]
    me, length, spot = info[0], info[1], info[2]
    count, width = q_in[0].shape
    heads = width // HEAD_DIM
    total = n * count
    blocks = total // ATT_BLOCK
    copies = []
    for r in range(n):
        rows = pl.ds(aligned(me ^ r, count), count)
        query_rows = pl.ds(aligned(spot ^ r, count), count)
        for k, (src, dst) in enumerate(
            (
                (kv_in[r].at[:, pl.ds(0, width)], ks.at[rows]),
                (kv_in[r].at[:, pl.ds(width, width)], vs.at[rows]),
                (q_in[r], qs.at[query_rows]),
            )
        ):
            copies.append(pltpu.make_async_copy(src, dst, sems.at[3 * r + k]))
    wait_all(start_all(copies))
    factor = HEAD_DIM ** (-0.5) * LOG2_E

    def transpose_values(b, _):
        at = pl.ds(pl.multiple_of(b * ATT_BLOCK, ATT_BLOCK), ATT_BLOCK)
        vt[:, at] = vs[at, :].T
        return 0

    lax.fori_loop(0, blocks, transpose_values, 0)
    live = jnp.minimum((length + ATT_BLOCK - 1) // ATT_BLOCK, blocks)

    def tile(qi, kj, state, masked):
        new = []
        q_at = pl.ds(pl.multiple_of(qi * ATT_BLOCK, ATT_BLOCK), ATT_BLOCK)
        k_at = pl.ds(pl.multiple_of(kj * ATT_BLOCK, ATT_BLOCK), ATT_BLOCK)
        for h in range(heads):
            cols = slice(h * HEAD_DIM, (h + 1) * HEAD_DIM)
            top, total_sum, acc = state[h]
            scores = nt_dot(ks[k_at, cols], qs[q_at, cols]) * factor
            if masked:
                scores = jnp.where(causal_mask(ATT_BLOCK), scores, -DEAD)
            higher = jnp.maximum(top, jnp.max(scores, axis=0, keepdims=True))
            weights = jnp.exp2(scores - higher)
            shrink = jnp.exp2(top - higher)
            total_sum = total_sum * shrink + jnp.sum(weights, axis=0, keepdims=True)
            acc = acc * shrink + jnp.dot(
                vt[cols, k_at], weights.astype(jnp.bfloat16), preferred_element_type=jnp.float32
            )
            new.append((higher, total_sum, acc))
        return tuple(new)

    stats[...] = jnp.full(stats.shape, DEAD, jnp.float32)

    def query_block(qi, _):
        first = tuple(
            (
                jnp.full((1, ATT_BLOCK), -DEAD, jnp.float32),
                jnp.zeros((1, ATT_BLOCK), jnp.float32),
                jnp.zeros((HEAD_DIM, ATT_BLOCK), jnp.float32),
            )
            for _ in range(heads)
        )
        state = lax.fori_loop(0, qi, lambda kj, s: tile(qi, kj, s, False), first)
        state = tile(qi, qi, state, True)
        q_at = pl.ds(pl.multiple_of(qi * ATT_BLOCK, ATT_BLOCK), ATT_BLOCK)
        query_at = qi * ATT_BLOCK + lax.broadcasted_iota(jnp.int32, (1, ATT_BLOCK), 1)
        alive = query_at < length
        for h in range(heads):
            cols = slice(h * HEAD_DIM, (h + 1) * HEAD_DIM)
            top, total_sum, acc = state[h]
            scaled = acc * jnp.where(alive, 1.0 / total_sum, 0.0)
            ot[cols, q_at] = scaled
            mixed[q_at, cols] = scaled.T.astype(jnp.bfloat16)
            stats[h : h + 1, q_at] = jnp.where(alive, top + jnp.log2(total_sum), DEAD)
        return 0

    lax.fori_loop(0, live, query_block, 0)

    def dead_block(qi, _):
        q_at = pl.ds(pl.multiple_of(qi * ATT_BLOCK, ATT_BLOCK), ATT_BLOCK)
        mixed[q_at, :] = jnp.zeros((ATT_BLOCK, width), jnp.bfloat16)
        ot[:, q_at] = jnp.zeros((width, ATT_BLOCK), jnp.float32)
        return 0

    lax.fori_loop(live, blocks, dead_block, 0)
    copies = []
    for r in range(n):
        rows = pl.ds(pl.multiple_of((me ^ r) * count, count), count)
        copies.append(pltpu.make_async_copy(mixed.at[rows], outs[r], sems.at[r]))
    wait_all(start_all(copies))


def attention_forward(info, q_blocks, kv_blocks):
    n = len(q_blocks)
    count, width = q_blocks[0].shape
    total = n * count
    got = call(
        functools.partial(forward_body, n),
        [info, *q_blocks, *kv_blocks],
        [IN_SMEM] + [ANYWHERE] * (2 * n),
        [((count, width), jnp.bfloat16)] * n
        + [((8, total), jnp.float32), ((width, total), jnp.float32)],
        [ANYWHERE] * n + [IN_VMEM] * 2,
        [pltpu.VMEM((total, width), jnp.bfloat16)] * 3
        + [pltpu.VMEM((width, total), jnp.bfloat16), pltpu.VMEM((total, width), jnp.bfloat16)]
        + [pltpu.SemaphoreType.DMA((3 * n,))],
        16 * 2 * total * total * width // 2,
        10 * total * width,
        "attention_forward",
    )
    return got[:n], got[n], got[n + 1]


def backward_body(n, info, *refs):
    q_in, kv_in, g_in = refs[:n], refs[n : 2 * n], refs[2 * n : 3 * n]
    stats, ot = refs[3 * n], refs[3 * n + 1]
    refs = refs[3 * n + 2 :]
    dq_out, dkv_out = refs[:n], refs[n : 2 * n]
    qs, ks, vs, gs, kt, delta, dqt, dk, dv, dq_low, dkv_low, sems = refs[2 * n :]
    me, length, spot = info[0], info[1], info[2]
    count, width = q_in[0].shape
    heads = width // HEAD_DIM
    total = n * count
    blocks = total // ATT_BLOCK
    copies = []
    for r in range(n):
        rows = pl.ds(aligned(me ^ r, count), count)
        query_rows = pl.ds(aligned(spot ^ r, count), count)
        for k, (src, dst) in enumerate(
            (
                (kv_in[r].at[:, pl.ds(0, width)], ks.at[rows]),
                (kv_in[r].at[:, pl.ds(width, width)], vs.at[rows]),
                (q_in[r], qs.at[query_rows]),
                (g_in[r], gs.at[rows]),
            )
        ):
            copies.append(pltpu.make_async_copy(src, dst, sems.at[4 * r + k]))
    start_all(copies)
    live = jnp.minimum((length + ATT_BLOCK - 1) // ATT_BLOCK, blocks)
    scale = HEAD_DIM ** (-0.5)
    factor = scale * LOG2_E

    def clear(b, _):
        at = pl.ds(pl.multiple_of(b * ATT_BLOCK, ATT_BLOCK), ATT_BLOCK)
        dqt[:, at] = jnp.zeros((width, ATT_BLOCK), jnp.float32)
        dk[at, :] = jnp.zeros((ATT_BLOCK, width), jnp.float32)
        dv[at, :] = jnp.zeros((ATT_BLOCK, width), jnp.float32)
        return 0

    lax.fori_loop(0, blocks, clear, 0)
    wait_all(copies)

    def prepare(b, _):
        at = pl.ds(pl.multiple_of(b * ATT_BLOCK, ATT_BLOCK), ATT_BLOCK)
        kt[:, at] = ks[at, :].T
        both = gs[at, :].astype(jnp.float32).T * ot[:, at]
        for h in range(heads):
            cols = slice(h * HEAD_DIM, (h + 1) * HEAD_DIM)
            delta[h : h + 1, at] = jnp.sum(both[cols], axis=0, keepdims=True)
        return 0

    lax.fori_loop(0, blocks, prepare, 0)

    def tile(qi, kj, masked):
        q_at = pl.ds(pl.multiple_of(qi * ATT_BLOCK, ATT_BLOCK), ATT_BLOCK)
        k_at = pl.ds(pl.multiple_of(kj * ATT_BLOCK, ATT_BLOCK), ATT_BLOCK)
        for h in range(heads):
            cols = slice(h * HEAD_DIM, (h + 1) * HEAD_DIM)
            q, g = qs[q_at, cols], gs[q_at, cols]
            scores = nt_dot(ks[k_at, cols], q) * factor - stats[h : h + 1, q_at]
            if masked:
                scores = jnp.where(causal_mask(ATT_BLOCK), scores, -DEAD)
            weights = jnp.exp2(scores)
            grad_weights = nt_dot(vs[k_at, cols], g)
            grad_scores = (weights * (grad_weights - delta[h : h + 1, q_at])).astype(jnp.bfloat16)
            dv[k_at, cols] += jnp.dot(
                weights.astype(jnp.bfloat16), g, preferred_element_type=jnp.float32
            )
            dk[k_at, cols] += jnp.dot(grad_scores, q, preferred_element_type=jnp.float32)
            dqt[cols, q_at] += jnp.dot(
                kt[cols, k_at], grad_scores, preferred_element_type=jnp.float32
            )

    def query_block(qi, _):
        def step(kj, _):
            tile(qi, kj, False)
            return 0

        lax.fori_loop(0, qi, step, 0)
        tile(qi, qi, True)
        return 0

    lax.fori_loop(0, live, query_block, 0)

    def finish(b, _):
        at = pl.ds(pl.multiple_of(b * ATT_BLOCK, ATT_BLOCK), ATT_BLOCK)
        dq_low[at, :] = (dqt[:, at] * scale).T.astype(jnp.bfloat16)
        dkv_low[at, :width] = (dk[at, :] * scale).astype(jnp.bfloat16)
        dkv_low[at, width:] = dv[at, :].astype(jnp.bfloat16)
        return 0

    lax.fori_loop(0, blocks, finish, 0)
    copies = []
    for r in range(n):
        rows = pl.ds(pl.multiple_of((me ^ r) * count, count), count)
        copies.append(pltpu.make_async_copy(dq_low.at[rows], dq_out[r], sems.at[2 * r]))
        copies.append(pltpu.make_async_copy(dkv_low.at[rows], dkv_out[r], sems.at[2 * r + 1]))
    wait_all(start_all(copies))


def attention_backward(info, q_blocks, kv_blocks, g_blocks, stats, ot):
    n = len(q_blocks)
    count, width = q_blocks[0].shape
    total = n * count
    low_all = pltpu.VMEM((total, width), jnp.bfloat16)
    got = call(
        functools.partial(backward_body, n),
        [info, *q_blocks, *kv_blocks, *g_blocks, stats, ot],
        [IN_SMEM] + [ANYWHERE] * (3 * n) + [IN_VMEM] * 2,
        [((count, width), jnp.bfloat16)] * n + [((count, 2 * width), jnp.bfloat16)] * n,
        [ANYWHERE] * (2 * n),
        [low_all] * 4
        + [
            pltpu.VMEM((width, total), jnp.bfloat16),
            pltpu.VMEM((8, total), jnp.float32),
            pltpu.VMEM((width, total), jnp.float32),
            pltpu.VMEM((total, width), jnp.float32),
            pltpu.VMEM((total, width), jnp.float32),
            low_all,
            pltpu.VMEM((total, 2 * width), jnp.bfloat16),
            pltpu.SemaphoreType.DMA((4 * n,)),
        ],
        40 * 2 * total * total * width // 2,
        20 * total * width,
        "attention_backward",
    )
    return got[:n], got[n:]


def pack_body(n, info, keys, values, *refs):
    outs, sems = refs[:n], refs[n]
    me = info[0]
    width = outs[0].shape[1] // 2
    copies = []
    for r in range(n):
        cols = pl.ds(aligned(me ^ r, width), width)
        copies.append(
            pltpu.make_async_copy(keys.at[:, cols], outs[r].at[:, pl.ds(0, width)], sems.at[2 * r])
        )
        copies.append(
            pltpu.make_async_copy(
                values.at[:, cols], outs[r].at[:, pl.ds(width, width)], sems.at[2 * r + 1]
            )
        )
    wait_all(start_all(copies))


def pack_keys_values(n, info, keys, values):
    count, depth = keys.shape
    return call(
        functools.partial(pack_body, n),
        [info, keys, values],
        [IN_SMEM, ANYWHERE, ANYWHERE],
        [((count, 2 * depth // n), jnp.bfloat16)] * n,
        [IN_VMEM] * n,
        [pltpu.SemaphoreType.DMA((2 * n,))],
        0,
        8 * count * depth,
        "pack_keys_values",
    )


GAIN_ROWS = 32


def norm_parts(v):
    return lax.rsqrt(jnp.mean(v * v, axis=-1, keepdims=True) + EPSILON)


def query_body(n, nd, info, *refs):
    xs, pieces = refs[:nd], refs[nd : nd + n + 1]
    q_out = refs[nd + n + 1 : nd + 2 * n + 1]
    normed, gains, weight, out_weight = refs[nd + 2 * n + 1 : nd + 2 * n + 5]
    queries, gain_rows, sems = refs[nd + 2 * n + 5 :]
    me, dp = info[0], info[1]
    count, depth = xs[0].shape
    wrows = (pieces[0].shape[0] - GAIN_ROWS) // 2
    cut = wrows - GAIN_ROWS // 2
    copies, later = [], []

    def fetch(into, k, src, dst, j):
        into.append(pltpu.make_async_copy(src, dst, sems.at[3 * k + j]))

    for k in range(n):
        first = info[3 + k] * wrows
        gain_at = gain_rows.at[pl.ds(aligned(info[3 + k], 16), 16)]
        fetch(copies, k, pieces[k].at[pl.ds(0, 16)], gain_at, 0)
        at = pl.multiple_of(first, 16)
        if k < n - 1:
            rows = pl.ds(at, wrows)
            fetch(copies, k, pieces[k].at[pl.ds(GAIN_ROWS, wrows)], weight.at[rows], 1)
            fetch(later, k, pieces[k].at[pl.ds(GAIN_ROWS + wrows, wrows)], out_weight.at[rows], 2)
        else:
            below = pl.multiple_of(first + cut, 16)
            fetch(copies, k, pieces[k].at[pl.ds(GAIN_ROWS, cut)], weight.at[pl.ds(at, cut)], 1)
            rest = pl.ds(below, wrows - cut)
            fetch(copies, k, pieces[n].at[pl.ds(0, wrows - cut)], weight.at[rest], 2)
            tail = pieces[n].at[pl.ds(wrows - cut, wrows)]
            fetch(later, n, tail, out_weight.at[pl.ds(at, wrows)], 0)
    start_all(copies)
    start_all(later)
    wait_all(copies)
    share = depth // n
    for o in range(n):
        row = gain_rows[o * 16 : o * 16 + 16, : 2 * share].astype(jnp.float32)
        gains[0:1, o * share : (o + 1) * share] = row[0:1, :share]
        gains[1:2, o * share : (o + 1) * share] = row[0:1, share:]
    for k in range(nd):
        v = xs[k][...].astype(jnp.float32)
        rows = slice(k * count, (k + 1) * count)
        normed[rows, :] = (v * norm_parts(v) * gains[0:1, :]).astype(jnp.bfloat16)
        queries[rows, :] = jnp.dot(
            normed[rows, :], weight[...], preferred_element_type=jnp.float32
        ).astype(jnp.bfloat16)
    per = n // nd
    copies = []
    for m in range(n):
        j = me ^ m
        slot = dp ^ (j // per)
        copies.append(
            pltpu.make_async_copy(
                queries.at[
                    pl.ds(aligned(slot, count), count), pl.ds(aligned(j % per, share), share)
                ],
                q_out[m],
                sems.at[3 * n + 3 + m],
            )
        )
    wait_all(start_all(copies))
    wait_all(later)


def project_queries(n, nd, info, xs, pieces):
    count, depth = xs[0].shape
    quarter = pieces[0].shape[1]
    got = call(
        functools.partial(query_body, n, nd),
        [info, *xs, *pieces],
        [IN_SMEM] + [IN_VMEM] * nd + [ANYWHERE] * (n + 1),
        [((count, depth // n), jnp.bfloat16)] * n
        + [
            ((nd * count, depth), jnp.bfloat16),
            ((8, depth), jnp.float32),
            ((depth, quarter), jnp.bfloat16),
            ((depth, quarter), jnp.bfloat16),
        ],
        [ANYWHERE] * n + [IN_VMEM] * 4,
        [
            pltpu.VMEM((nd * count, quarter), jnp.bfloat16),
            pltpu.VMEM((n * 16, quarter), jnp.bfloat16),
            pltpu.SemaphoreType.DMA((4 * n + 3,)),
        ],
        2 * count * depth * depth,
        6 * depth * depth,
        "project_queries",
    )
    return got[:n], *got[n:]


def padded(width):
    return (width + 127) // 128 * 128


def ffn_body(m, *refs):
    nf_in, cot_in, weights_in = refs[:m], refs[m : 2 * m], refs[2 * m : 2 * m + 3]
    outs = refs[2 * m + 3 : 7 * m + 3]
    nf, cot, gate_w, up_w, down_w, acts, shares, sems, out_sems = refs[7 * m + 3 :]
    weights = (gate_w, up_w, down_w)
    rows = nf_in[0].shape[0]
    hidden_units = gate_w.shape[0]

    def load(src, dst, k):
        return pltpu.make_async_copy(src, dst, sems.at[k])

    loads = [load(weights_in[k], weights[k], k) for k in range(3)]
    nf_loads = [load(nf_in[b], nf.at[b], 3 + b) for b in range(m)]
    cot_loads = [load(cot_in[b], cot.at[b], 3 + m + b) for b in range(m)]
    start_all([nf_loads[0], loads[0], loads[1], cot_loads[0], loads[2]])
    start_all([*nf_loads[1:], *cot_loads[1:]])
    copies = []

    def store(b, k, src):
        copy = pltpu.make_async_copy(src, outs[5 * b + k], out_sems.at[5 * b + k])
        copy.start()
        copies.append(copy)

    for b in range(m):
        nf_loads[b].wait()
        if b == 0:
            loads[0].wait()
        gate_value = nt_dot(nf[b], gate_w[...])
        if b == 0:
            loads[1].wait()
        up_value = nt_dot(nf[b], up_w[...])
        cot_loads[b].wait()
        if b == 0:
            loads[2].wait()
        grad_inner = nt_dot(cot[b], down_w[...])
        sigmoid = 1.0 / (1.0 + jnp.exp(-gate_value))
        act = gate_value * sigmoid
        inner = (act * up_value).astype(jnp.bfloat16)
        grad_gate = (
            grad_inner * up_value * sigmoid * (1.0 + gate_value * (1.0 - sigmoid))
        ).astype(jnp.bfloat16)
        grad_up = (grad_inner * act).astype(jnp.bfloat16)
        for k, value in enumerate((inner, grad_gate, grad_up)):
            acts[3 * b + k, :, :hidden_units] = value
            store(b, k, acts.at[3 * b + k])
        shares[2 * b] = jnp.dot(
            grad_gate, gate_w[...], preferred_element_type=jnp.float32
        ) + jnp.dot(grad_up, up_w[...], preferred_element_type=jnp.float32)
        store(b, 3, shares.at[2 * b])
        shares[2 * b + 1] = jnp.dot(inner, down_w[...], preferred_element_type=jnp.float32)
        store(b, 4, shares.at[2 * b + 1])
    wait_all(copies)


def ffn_blocks(nf, cot, weights):
    m = len(nf)
    rows, depth = nf[0].shape
    units = weights[0].shape[0]
    act = ((rows, padded(units)), jnp.bfloat16)
    share = ((rows, depth), jnp.float32)
    got = call(
        functools.partial(ffn_body, m),
        [*nf, *cot, *weights],
        [ANYWHERE] * (2 * m + 3),
        [act, act, act, share, share] * m,
        [ANYWHERE] * (5 * m),
        [pltpu.VMEM((m, rows, depth), jnp.bfloat16)] * 2
        + [pltpu.VMEM((units, depth), jnp.bfloat16)] * 3
        + [
            pltpu.VMEM((3 * m, rows, padded(units)), jnp.bfloat16),
            pltpu.VMEM((2 * m, rows, depth), jnp.float32),
            pltpu.SemaphoreType.DMA((3 + 2 * m,)),
            pltpu.SemaphoreType.DMA((5 * m,)),
        ],
        12 * m * rows * units * depth,
        6 * units * depth + 12 * m * rows * depth,
        "ffn_blocks",
    )
    return [got[5 * b : 5 * b + 5] for b in range(m)]


def weight_gradient_body(count, units, info, *refs):
    lhs_in, rhs_in = refs[:count], refs[count : 2 * count]
    kept, sent, lhs, turned, rhs, sems = refs[2 * count :]
    core = info[2]
    copies, first = [], 0
    for k in range(count):
        rows = lhs_in[k].shape[0]
        at = pl.ds(first, rows)
        copies.append(pltpu.make_async_copy(lhs_in[k], lhs.at[at], sems.at[2 * k]))
        copies.append(pltpu.make_async_copy(rhs_in[k], rhs.at[at], sems.at[2 * k + 1]))
        first += rows
    start_all(copies)
    wait_all(copies[::2])
    block = 256

    def turn(b, _):
        at = pl.ds(aligned(b, block), block)
        turned[:, at] = lhs[at, :].T
        return 0

    lax.fori_loop(0, first // block, turn, 0)
    wait_all(copies[1::2])
    half = kept.shape[1]
    piece = 256

    def step(c, _):
        to = pl.ds(aligned(c, piece), piece)
        for out, side in ((kept, core), (sent, 1 - core)):
            cols = pl.ds(pl.multiple_of(side * half + c * piece, piece), piece)
            out[:, to] = jnp.dot(
                turned[...], rhs[:, cols], preferred_element_type=jnp.float32
            )[:units].astype(jnp.bfloat16)
        return 0

    lax.fori_loop(0, half // piece, step, 0)


def weight_gradient(info, lhs, rhs, units):
    count = len(lhs)
    rows = sum(b.shape[0] for b in rhs)
    width, depth = lhs[0].shape[1], rhs[0].shape[1]
    return call(
        functools.partial(weight_gradient_body, count, units),
        [info, *lhs, *rhs],
        [IN_SMEM] + [ANYWHERE] * (2 * count),
        [((units, depth // 2), jnp.bfloat16)] * 2,
        [IN_VMEM] * 2,
        [
            pltpu.VMEM((rows, width), jnp.bfloat16),
            pltpu.VMEM((width, rows), jnp.bfloat16),
            pltpu.VMEM((rows, depth), jnp.bfloat16),
            pltpu.SemaphoreType.DMA((2 * count,)),
        ],
        2 * rows * units * depth,
        2 * rows * depth,
        "weight_gradient",
    )


def hidden_body(n, nd, info, x, gains, *refs):
    blocks, parts = refs[:n], refs[n : n + nd]
    hidden, normed, mixed = refs[n + nd : n + nd + 3]
    weight, sems = refs[n + nd + 3 :]
    me, dp = info[0], info[1]
    share, quarter = blocks[0].shape[1], parts[0].shape[1]
    copies = []
    for r in range(nd):
        cols = pl.ds(aligned(dp ^ r, quarter), quarter)
        copies.append(pltpu.make_async_copy(parts[r], weight.at[:, cols], sems.at[r]))
    for r in range(n):
        cols = pl.ds(aligned(me ^ r, share), share)
        copies.append(pltpu.make_async_copy(blocks[r], mixed.at[:, cols], sems.at[nd + r]))
    wait_all(start_all(copies))
    depth = x.shape[1]
    piece = 512

    def step(c, total):
        cols = pl.ds(aligned(c, piece), piece)
        v = x[:, cols].astype(jnp.float32) + jnp.dot(
            mixed[...], weight[:, cols], preferred_element_type=jnp.float32
        )
        hidden[:, cols] = v
        return total + jnp.sum(v * v, axis=-1, keepdims=True)

    total = lax.fori_loop(0, depth // piece, step, jnp.zeros((x.shape[0], 1), jnp.float32))
    normed[...] = (
        hidden[...] * lax.rsqrt(total / depth + EPSILON) * gains[1:2, :]
    ).astype(jnp.bfloat16)


def project_mixed(n, nd, info, x, gains, blocks, parts):
    count, depth = x.shape
    return call(
        functools.partial(hidden_body, n, nd),
        [info, x, gains, *blocks, *parts],
        [IN_SMEM, IN_VMEM, IN_VMEM] + [ANYWHERE] * (n + nd),
        [
            ((count, depth), jnp.float32),
            ((count, depth), jnp.bfloat16),
            ((count, depth), jnp.bfloat16),
        ],
        [IN_VMEM] * 3,
        [pltpu.VMEM((depth, depth), jnp.bfloat16), pltpu.SemaphoreType.DMA((n + nd,))],
        2 * count * depth * depth,
        6 * depth * depth,
        "project_mixed",
    )


def norm_grad(v, gain, upstream):
    scale = norm_parts(v)
    weighted = upstream * gain
    through = weighted * scale - v * (scale**3) * jnp.mean(weighted * v, axis=-1, keepdims=True)
    return through, jnp.sum(upstream * v * scale, axis=0, keepdims=True)


def branch_body(n, nd, info, hidden, gains, cotangent, own, first, second, *refs):
    parts, refs = refs[:nd], refs[nd:]
    gm_out, cols_out = refs[:n], refs[n : n + nd]
    grad_hidden, gain_part, branch, weight, sems = refs[n + nd :]
    me, dp = info[0], info[1]
    quarter = parts[0].shape[1]
    copies = []
    for r in range(nd):
        cols = pl.ds(aligned(dp ^ r, quarter), quarter)
        copies.append(pltpu.make_async_copy(parts[r], weight.at[:, cols], sems.at[r]))
    start_all(copies)
    upstream = own[...] + first[...].astype(jnp.float32) + second[...].astype(jnp.float32)
    through, gain = norm_grad(hidden[...], gains[1:2, :], upstream)
    gain_part[...] = jnp.broadcast_to(gain, gain_part.shape)
    total = cotangent[...].astype(jnp.float32) + through
    grad_hidden[...] = total
    branch[...] = total.astype(jnp.bfloat16)
    for r in range(nd):
        cols_out[r][...] = branch[:, pl.ds(aligned(dp ^ r, quarter), quarter)]
    wait_all(copies)
    share = gm_out[0].shape[1]
    for r in range(n):
        rows = pl.ds(aligned(me ^ r, share), share)
        gm_out[r][...] = nt_dot(branch[...], weight[rows, :]).astype(jnp.bfloat16)


def branch_gradient(n, nd, info, hidden, gains, cotangent, sums, parts):
    count, depth = cotangent.shape
    got = call(
        functools.partial(branch_body, n, nd),
        [info, hidden, gains, cotangent, *sums, *parts],
        [IN_SMEM] + [IN_VMEM] * 6 + [ANYWHERE] * nd,
        [((count, depth // n), jnp.bfloat16)] * n
        + [((count, depth // nd), jnp.bfloat16)] * nd
        + [((count, depth), jnp.float32), ((8, depth), jnp.float32)],
        [IN_VMEM] * (n + nd + 2),
        [
            pltpu.VMEM((count, depth), jnp.bfloat16),
            pltpu.VMEM((depth, depth), jnp.bfloat16),
            pltpu.SemaphoreType.DMA((nd,)),
        ],
        2 * count * depth * depth,
        6 * depth * depth,
        "branch_gradient",
    )
    return got[:n], got[n : n + nd], got[n + nd], got[n + nd + 1]


def sort_body(n, nd, info, *refs):
    blocks, cols_out = refs[:n], refs[n : n + nd]
    rows, sems = refs[n + nd :]
    me, dp = info[0], info[1]
    share, quarter = blocks[0].shape[1], cols_out[0].shape[1]
    copies = []
    for r in range(n):
        cols = pl.ds(aligned(me ^ r, share), share)
        copies.append(pltpu.make_async_copy(blocks[r], rows.at[:, cols], sems.at[r]))
    wait_all(start_all(copies))
    copies = []
    for r in range(nd):
        cols = pl.ds(aligned(dp ^ r, quarter), quarter)
        copies.append(pltpu.make_async_copy(rows.at[:, cols], cols_out[r], sems.at[r]))
    wait_all(start_all(copies))


def sort_columns(n, nd, info, blocks):
    count, share = blocks[0].shape
    depth = n * share
    return call(
        functools.partial(sort_body, n, nd),
        [info, *blocks],
        [IN_SMEM] + [ANYWHERE] * n,
        [((count, depth // nd), jnp.bfloat16)] * nd,
        [ANYWHERE] * nd,
        [pltpu.VMEM((count, depth), jnp.bfloat16), pltpu.SemaphoreType.DMA((max(n, nd),))],
        0,
        6 * count * depth,
        "sort_columns",
    )


def split_body(n, info, *refs):
    blocks, keys, values, sems = refs[:n], refs[n], refs[n + 1], refs[n + 2]
    me = info[0]
    share = blocks[0].shape[1] // 2
    copies = []
    for r in range(n):
        cols = pl.ds(aligned(me ^ r, share), share)
        copies.append(
            pltpu.make_async_copy(blocks[r].at[:, pl.ds(0, share)], keys.at[:, cols], sems.at[2 * r])
        )
        copies.append(
            pltpu.make_async_copy(
                blocks[r].at[:, pl.ds(share, share)], values.at[:, cols], sems.at[2 * r + 1]
            )
        )
    wait_all(start_all(copies))


def split_keys_values(n, info, blocks):
    count, share = blocks[0].shape
    depth = n * share // 2
    return call(
        functools.partial(split_body, n),
        [info, *blocks],
        [IN_SMEM] + [ANYWHERE] * n,
        [((count, depth), jnp.bfloat16)] * 2,
        [IN_VMEM] * 2,
        [pltpu.SemaphoreType.DMA((2 * n,))],
        0,
        8 * count * depth,
        "split_keys_values",
    )


def input_body(nd, x, gains, grad_hidden, *refs):
    cols, parts = refs[:nd], refs[nd : 2 * nd]
    out, gain_part, upstream = refs[2 * nd :]
    piece = 512

    def step(c, _):
        rows = pl.ds(aligned(c, piece), piece)
        upstream[:, rows] = sum(nt_dot(cols[r][...], parts[r][rows, :]) for r in range(nd))
        return 0

    lax.fori_loop(0, x.shape[1] // piece, step, 0)
    through, gain = norm_grad(x[...].astype(jnp.float32), gains[0:1, :], upstream[...])
    gain_part[...] = jnp.broadcast_to(gain, gain_part.shape)
    out[...] = (grad_hidden[...] + through).astype(jnp.bfloat16)


def input_gradient(nd, x, gains, grad_hidden, cols, parts):
    count, depth = x.shape
    return call(
        functools.partial(input_body, nd),
        [x, gains, grad_hidden, *cols, *parts],
        [IN_VMEM] * (3 + 2 * nd),
        [((count, depth), jnp.bfloat16), ((8, depth), jnp.float32)],
        [IN_VMEM] * 2,
        [pltpu.VMEM((count, depth), jnp.float32)],
        2 * count * depth * depth,
        6 * depth * depth,
        "input_gradient",
    )


def projections_body(n, nd, info, normed, attn_part, ffn_part, *refs):
    branch_cols, query_cols, mixed_in = refs[:nd], refs[nd : 2 * nd], refs[2 * nd : 3 * nd]
    outs = refs[3 * nd : 3 * nd + n]
    branch, query, mixed = refs[3 * nd + n :]
    count = branch_cols[0].shape[0]
    share = mixed.shape[1] // n
    for k in range(nd):
        rows = slice(k * count, (k + 1) * count)
        mixed[rows, :] = mixed_in[k][...]
        branch[rows, :] = branch_cols[k][...]
        query[rows, :] = query_cols[k][...]
    for k in range(n):
        cols = pl.ds(aligned(info[3 + k], share), share)
        outs[k][:share, :] = tn_dot(mixed[:, cols], branch[...])
        outs[k][share : 2 * share, :] = tn_dot(normed[:, cols], query[...])
        outs[k][2 * share :, :] = jnp.zeros((GAIN_ROWS, branch.shape[1]), jnp.float32)
        outs[k][2 * share : 2 * share + 8, :share] = attn_part[:, cols]
        outs[k][2 * share : 2 * share + 8, share : 2 * share] = ffn_part[:, cols]


def projection_gradients(n, nd, info, mixed, normed, attn_part, ffn_part, branch_cols, query_cols):
    rows, depth = normed.shape
    count, quarter = branch_cols[0].shape
    return call(
        functools.partial(projections_body, n, nd),
        [info, normed, attn_part, ffn_part, *branch_cols, *query_cols, *mixed],
        [IN_SMEM] + [IN_VMEM] * (3 + 3 * nd),
        [((2 * depth // n + GAIN_ROWS, quarter), jnp.float32)] * n,
        [IN_VMEM] * n,
        [pltpu.VMEM((rows, quarter), jnp.bfloat16)] * 2
        + [pltpu.VMEM((rows, depth), jnp.bfloat16)],
        4 * rows * depth * quarter,
        4 * rows * depth,
        "projection_gradients",
    )


def join_body(nd, info, *refs):
    parts, (out_grad, query_grad, gain_sum) = refs[:nd], refs[nd:]
    share = out_grad.shape[0]
    quarter = parts[0].shape[1]
    dp = info[1]
    for r in range(nd):
        cols = pl.ds(aligned(dp ^ r, quarter), quarter)
        part = parts[r][...].astype(jnp.float32)
        out_grad[:, cols] = part[:share]
        query_grad[:, cols] = part[share : 2 * share]
    tops = [parts[r][2 * share : 2 * share + 16, :].astype(jnp.float32)[:8] for r in range(nd)]
    gain_sum[...] = tree_sum(tops)


def join_projections(nd, info, parts):
    rows, quarter = parts[0].shape
    share, depth = (rows - GAIN_ROWS) // 2, quarter * nd
    return call(
        functools.partial(join_body, nd),
        [info, *parts],
        [IN_SMEM] + [IN_VMEM] * nd,
        [((share, depth), jnp.float32)] * 2 + [((8, quarter), jnp.float32)],
        [IN_VMEM] * 3,
        [],
        0,
        10 * share * depth,
        "join_projections",
    )


def chip_sum_body(kept, *refs):
    others, out = refs[:-1], refs[-1]
    half = len(others) // 2
    top = others[0].shape[0]
    for side, first in ((others[:half], 0), (others[half:], top)):
        rows = slice(first, first + side[0].shape[0])
        terms = [kept[rows, :].astype(jnp.float32)] + [v[...].astype(jnp.float32) for v in side]
        out[rows, :] = tree_sum(terms).astype(jnp.bfloat16)


def chip_sum(operands):
    shape = operands[0].shape
    return call(
        chip_sum_body,
        operands,
        [IN_VMEM] * len(operands),
        [(shape, jnp.bfloat16)],
        [IN_VMEM],
        [],
        0,
        6 * shape[0] * shape[1],
        "chip_sum",
    )[0]


def spread_body(info, mine, other, out):
    half = mine.shape[1]
    for ref, side in ((mine, info[2]), (other, 1 - info[2])):
        out[:, pl.ds(aligned(side, half), half)] = ref[...].astype(jnp.float32)


def spread_columns(info, mine, other):
    rows, half = mine.shape
    return call(
        spread_body,
        [info, mine, other],
        [IN_SMEM, IN_VMEM, IN_VMEM],
        [((rows, 2 * half), jnp.float32)],
        [IN_VMEM],
        [],
        0,
        12 * rows * half,
        "spread_columns",
    )[0]


def tree_sum(parts):
    while len(parts) > 1:
        parts = [parts[k] + parts[k + 1] for k in range(0, len(parts), 2)]
    return parts[0]


def columns(x, start, width):
    return lax.dynamic_slice_in_dim(x, start, width, 1)


def make_local(mesh):
    net = Links(mesh)
    n, nd = net.n, net.nd
    dp_order = list(range(0, nd, 2)) + list(range(1, nd, 2))
    half_way = n // 2
    ring_order = [0] + [s for k in range(1, half_way) for s in (-k, k)] + ["a", "b"]

    def exchange(blocks, axis="seq"):
        return [b if r == 0 else net.swap(b, axis, r) for r, b in enumerate(blocks)]

    def chips(x, *deps):
        sent = after(x, *deps)
        return [x] + [net.swap(sent, "dp", r) for r in range(2, nd, 2)]

    def cores(near, *deps):
        return list(near) + [net.swap(v, "dp", 1) for v in tie(near, *deps)]

    def paced(ring, blocks, spare=1):
        out, sent = [], 1
        arrived = ring.step()
        steps = half_way - 1
        for k in range(steps):
            until = 1 + (n - 1) * (k + 1) // steps
            some = tie(blocks[sent:until], *arrived)
            fresh = [net.swap(b, "seq", sent + i) for i, b in enumerate(some)]
            arrived = ring.step(*out[-len(some) :]) if k else ring.step()
            out += fresh
            sent = until
        return out

    def local(
        layer_input,
        global_keys,
        global_values,
        lengths,
        attn_gain,
        query_weight,
        out_weight,
        ffn_gain,
        gate_weight,
        up_weight,
        down_weight,
        cotangent,
    ):
        length = lengths[0]
        me, mine = lax.axis_index("seq"), lax.axis_index("dp")
        core, group = mine % 2, net.group(mine)
        place = net.place()
        depth = layer_input.shape[1]
        quarter = depth // nd
        per = n // nd
        owners = [net.owner(place, key) for key in ring_order[:-2]] + [net.owner(place, half_way)]
        info = jnp.stack([me, group, core, *owners]).astype(jnp.int32)
        heads_info = jnp.stack([me, length, group * per + me % per]).astype(jnp.int32)

        gains = jnp.concatenate([attn_gain, ffn_gain])
        gain_rows = jnp.zeros((GAIN_ROWS, quarter), jnp.bfloat16)
        gain_rows = gain_rows.at[:, : gains.shape[0]].set(gains[None])
        mine_of = [columns(w, group * quarter, quarter) for w in (query_weight, out_weight)]
        ring = RingGather(net, jnp.concatenate([gain_rows, *mine_of], 0))
        kv_sent = list(pack_keys_values(n, info, global_keys, global_values))
        kv_blocks = [kv_sent[0]] + paced(ring, kv_sent)
        got = ring.got
        xs = cores(chips(layer_input), got["a"], got["b"])
        q_sent, normed_all, gains, query_quarter, out_quarter = project_queries(
            n, nd, info, xs, [got[k] for k in ring_order]
        )
        q_sent = tie(q_sent, *kv_blocks)
        q_blocks = [net.to_heads(b, m) for m, b in enumerate(q_sent)]
        out_near = chips(out_quarter, *q_blocks)
        mixed_sent, stats, ot = attention_forward(heads_info, q_blocks, kv_blocks)
        cot_ring = RingGather(net, cotangent)
        cot_1 = cot_ring.step(*q_blocks)
        mixed_blocks = exchange(tie(mixed_sent, *cot_1))
        cot_2 = cot_ring.step(*mixed_blocks)
        out_parts = cores(out_near, *mixed_blocks[1:])
        hidden, normed_ffn, mixed = project_mixed(
            n, nd, info, layer_input, gains, mixed_blocks, out_parts
        )

        nf_ring = RingGather(net, normed_ffn)
        weights = (gate_weight, up_weight, down_weight)
        units = gate_weight.shape[0]
        made = {0: ffn_blocks([normed_ffn], [cotangent], weights)[0]}

        def ffn(*keys, deps=()):
            nf, cot = ([ring.got[k] for k in keys] for ring in (nf_ring, cot_ring))
            nf = tie(nf, *deps)
            made.update(zip(keys, ffn_blocks(nf, cot, weights)))

        fresh = nf_ring.step()
        query_near = chips(query_quarter, normed_ffn)
        cot_fresh, before = cot_2, (made[0][3],)
        for k in range(1, half_way):
            later = cot_ring.step(*fresh) if cot_ring.at < half_way else cot_fresh
            fresh = nf_ring.step(*cot_fresh, *before, *(query_near if k == half_way - 1 else ()))
            ffn(-k, k)
            before = (made[k][3], made[-k][3])
            cot_fresh = later
        query_parts = cores(query_near, *fresh)
        mixed_near = chips(mixed, *query_near)
        ffn("a", "b", deps=before)
        nf, cot = nf_ring.got, cot_ring.got

        def exchange_x(kept, *deps):
            sent = after(kept, *deps)
            return [net.swap(sent, "dp", r) for r in range(2, nd, 2)]

        grad_sum = RowSum(net, lambda key: made[key][3])
        arrived = grad_sum.step(*query_parts, *mixed_near)
        mixed_parts = cores(mixed_near, *arrived)
        kept, deps, swapped = [], (), None
        for k in range(3):
            upcoming = grad_sum.step(*deps, *(mixed_parts if k else ()))
            lhs = tie([made[key][(1, 2, 0)[k]] for key in ring_order], *arrived)
            rhs = [(nf, nf, cot)[k][key] for key in ring_order]
            if swapped:
                kept.append(low(wide(mine_half) + wide(swapped[0])))
            deps = (*swapped,) if swapped else ()
            mine_half, sent_half = weight_gradient(info, lhs, rhs, units)
            swapped = (net.swap(sent_half, "dp", 1),)
            deps = (*deps, mine_half)
            last, arrived = arrived, upcoming
        top = units // 2
        others = [exchange_x(kept[0][:top], *last)]
        grad_sums = tie(grad_sum.rest(), *deps, *others[0])
        kept.append(low(wide(mine_half) + wide(swapped[0])))
        others.append(exchange_x(kept[0][top:], *grad_sums[1:]))

        def dp_cols(cols, *deps):
            sent = tie(cols, *deps)
            return [b if r == 0 else net.swap(b, "dp", r) for r, b in zip(dp_order, sent)]

        out_sum = RowSum(net, lambda key: made[key][4])
        out_1 = out_sum.step(*grad_sums[1:])
        gm_sent, branch_cols, grad_hidden, ffn_gain_part = branch_gradient(
            n, nd, info, hidden, gains, cotangent, grad_sums, out_parts
        )
        gm_blocks = exchange(tie(gm_sent, *out_1, *others[1]))
        branch_got = dp_cols(branch_cols, *gm_sent)
        gm_blocks = tie(gm_blocks, *branch_got)
        others.append(exchange_x(kept[1][:top], *gm_blocks))
        out_2 = out_sum.step(*gm_blocks)
        dq_sent, dkv_sent = attention_backward(
            heads_info, q_blocks, kv_blocks, gm_blocks, stats, ot
        )


        dq_sent = tie(dq_sent, *out_2, *others[2])
        others.append(exchange_x(kept[1][top:], *dq_sent))
        dq_blocks = tie(exchange(dq_sent), *others[3])

        def dp_total(k, *deps):
            total = chip_sum(tie([kept[k], *others[2 * k], *others[2 * k + 1]], *deps))
            return total, net.swap(total, "dp", 1)

        query_cols = sort_columns(n, nd, info, dq_blocks)

        query_got = dp_cols(query_cols)
        out_3 = out_sum.step(*query_cols)
        gate_total = dp_total(0, *dq_blocks)
        up_total = dp_total(1, *query_cols)
        others.append(exchange_x(kept[2][:top], *query_got))
        early = (n - 1) * 4 // 7
        dkv_early = [
            net.swap(b, "seq", r + 1) for r, b in enumerate(tie(dkv_sent[1 : early + 1], *query_cols))
        ]
        input_grad, attn_gain_part = input_gradient(
            nd, layer_input, gains, grad_hidden, query_cols, query_parts
        )
        shares = projection_gradients(
            n,
            nd,
            info,
            mixed_parts,
            normed_all,
            attn_gain_part,
            ffn_gain_part,
            branch_got,
            tie(query_got, *out_3, *dkv_early, gate_total[1], up_total[1]),
        )

        def share_of(key):
            if key in ("a", "b"):
                rows = shares[-1].shape[0] // 2
                return shares[-1][:rows] if key == "a" else shares[-1][rows:]
            return shares[ring_order.index(key)]

        share_sum = RowSum(net, share_of)
        shared = share_sum.step()
        others.append(exchange_x(kept[2][top:], *shared))
        for _ in range(half_way - 3):
            shared = share_sum.step()
        dkv_more = [
            net.swap(b, "seq", early + 1 + i)
            for i, b in enumerate(tie(dkv_sent[early + 1 :], *shared))
        ]
        dkv_blocks = [dkv_sent[0], *dkv_early, *dkv_more]
        shared = share_sum.step()
        out_sum.step(*shared)
        share_sum.step(*others[4])
        own, first, second = share_sum.rest()
        down_total = dp_total(2, first, second)
        gate_grad, up_grad, down_grad = [
            spread_columns(info, *t) for t in (gate_total, up_total, down_total)
        ]
        projections = low(own + wide(first) + wide(second))
        out_grad, query_grad, gain_sum = join_projections(
            nd, info, cores(chips(projections))
        )
        own, first, second = out_sum.rest()
        layer_output = low(hidden + (own + wide(first) + wide(second)))
        key_grad, value_grad = split_keys_values(n, info, dkv_blocks)
        attn_count = attn_gain.shape[0]
        return (
            layer_output,
            input_grad,
            key_grad,
            value_grad,
            gain_sum[0, :attn_count],
            query_grad,
            out_grad,
            gain_sum[0, attn_count : 2 * attn_count],
            gate_grad,
            up_grad,
            down_grad,
        )

    return local


def solution(mesh):
    placed = (
        P(("dp", "seq"), None),
        P(("dp", "seq"), None),
        P(("dp", "seq"), None),
        P("dp"),
        P("seq"),
        P("seq", None),
        P("seq", None),
        P("seq"),
        P("seq", None),
        P("seq", None),
        P("seq", None),
        P(("dp", "seq"), None),
    )
    return jax.shard_map(
        make_local(mesh),
        mesh=mesh,
        in_specs=placed,
        out_specs=(
            P(("dp", "seq"), None),
            P(("dp", "seq"), None),
            P(("dp", "seq"), None),
            P(("dp", "seq"), None),
            P("seq"),
            P("seq", None),
            P("seq", None),
            P("seq"),
            P("seq", None),
            P("seq", None),
            P("seq", None),
        ),
        check_vma=False,
    )
```

```python
import functools

import jax
import jax.numpy as jnp
from jax import lax
from jax.experimental import pallas as pl
from jax.experimental.pallas import tpu as pltpu
from jax.sharding import PartitionSpec as P

HEAD_DIM = 128
ATT_BLOCK = 512


EPSILON = 1e-05


def product(left_side, right_side):
    return jnp.dot(left_side, right_side, preferred_element_type=jnp.float32)


def inner_rows(left_side, right_side):
    return lax.dot_general(
        left_side, right_side, (((0,), (0,)), ((), ())), preferred_element_type=jnp.float32
    )


def outer_cols(left_side, right_side):
    return lax.dot_general(
        left_side, right_side, (((1,), (1,)), ((), ())), preferred_element_type=jnp.float32
    )


def snake(count):
    deep = 4 if count % 4 == 0 else 1
    wide = count // deep
    if deep == 1 or wide == 1:
        return list(range(count))
    order = []
    for z in range(deep):
        across = range(1, wide) if z % 2 == 0 else range(wide - 1, 0, -1)
        order += [z * wide + y for y in across]
    return order + [z * wide for z in range(deep - 1, -1, -1)]


def after(value, *others):
    return lax.optimization_barrier((value, *others))[0] if others else value


def tie(values, *others):
    return list(lax.optimization_barrier((*values, *others))[: len(values)])


def low(value):
    return value.astype(jnp.bfloat16)


def wide(value):
    return value.astype(jnp.float32)


class Links:
    def __init__(self, mesh):
        self.n = mesh.shape["seq"]
        self.nd = mesh.shape["dp"]
        self.order = snake(self.n)
        n = self.n
        self.right = [(self.order[k], self.order[(k + 1) % n]) for k in range(n)]
        self.left = [(b, a) for a, b in self.right]

    def group(self, d):
        return d % 2 * (self.nd // 2) + d // 2

    def place(self):
        me = lax.axis_index("seq")
        table = [0] * self.n
        for k, i in enumerate(self.order):
            table[i] = k
        return sum(jnp.where(me == i, table[i], 0) for i in range(self.n))

    def owner(self, place, distance):
        spot = (place + distance) % self.n
        return sum(jnp.where(spot == k, self.order[k], 0) for k in range(self.n))

    def to_right(self, x):
        return lax.ppermute(x, "seq", self.right)

    def to_left(self, x):
        return lax.ppermute(x, "seq", self.left)

    def to_heads(self, x, m):
        per, nx = self.n // self.nd, self.nd // 2
        pairs = []
        for d in range(self.nd):
            for s in range(self.n):
                j = s ^ m
                group = j // per
                to = group % nx * 2 + group // nx
                pairs.append((d * self.n + s, to * self.n + self.group(d) * per + j % per))
        return lax.ppermute(x, ("dp", "seq"), pairs)

    def swap(self, x, axis, r):
        count = self.n if axis == "seq" else self.nd
        return lax.ppermute(x, axis, [(k, k ^ r) for k in range(count)])


class RingGather:
    def __init__(self, net, x):
        self.net, self.got, self.at = net, {0: x}, 0
        self.from_left = self.from_right = x

    def step(self, *deps):
        net, half = self.net, self.net.n // 2
        self.at += 1
        left, right = self.from_left, self.from_right
        if self.at == half:
            rows = left.shape[0] // 2
            left, right = left[:rows], right[rows:]
        if self.at == 1 and half > 1:
            left = right = after(left, *deps)
        else:
            left, right = tie([left, right], *deps)
        self.from_left, self.from_right = net.to_right(left), net.to_left(right)
        keys = ("a", "b") if self.at == half else (-self.at, self.at)
        self.got[keys[0]], self.got[keys[1]] = self.from_left, self.from_right
        return self.from_left, self.from_right

    def rest(self):
        while self.at < self.net.n // 2:
            self.step()
        return self.got


class RowSum:
    def __init__(self, net, part):
        self.net, self.part, self.at = net, part, net.n // 2
        self.going_left = self.going_right = None

    def step(self, *deps):
        net, half, s = self.net, self.net.n // 2, self.at
        if s == half:
            left, right = self.part("b"), self.part("a")
        else:
            left, right = self.part(-s), self.part(s)
            if s == half - 1:
                rows = left.shape[0] // 2
                left = jnp.concatenate([left[:rows], left[rows:] + wide(self.going_left)])
                right = jnp.concatenate([right[:rows] + wide(self.going_right), right[rows:]])
            else:
                left = left + wide(self.going_left)
                right = right + wide(self.going_right)
        left, right = tie([low(left), low(right)], *deps)
        self.going_left, self.going_right = net.to_left(left), net.to_right(right)
        self.at -= 1
        return self.going_left, self.going_right

    def rest(self):
        while self.at:
            self.step()
        return self.part(0), self.going_left, self.going_right


VMEM_LIMIT = 56 * 1024 * 1024
COST_SHARE = 4
ANYWHERE = pl.BlockSpec(memory_space=pl.ANY)
IN_VMEM = pl.BlockSpec(memory_space=pltpu.VMEM)
IN_SMEM = pl.BlockSpec(memory_space=pltpu.SMEM)
LOG2_E = 1.4426950408889634
DEAD = 1e30


def nt_dot(a, b):
    return lax.dot_general(a, b, (((1,), (1,)), ((), ())), preferred_element_type=jnp.float32)


def tn_dot(a, b):
    return lax.dot_general(a, b, (((0,), (0,)), ((), ())), preferred_element_type=jnp.float32)


def call(body, operands, specs, outs, out_specs, scratch, flops, moved, name):
    return pl.pallas_call(
        body,
        name=name,
        in_specs=specs,
        out_specs=tuple(out_specs),
        out_shape=tuple(jax.ShapeDtypeStruct(s, t) for s, t in outs),
        scratch_shapes=scratch,
        compiler_params=pltpu.CompilerParams(vmem_limit_bytes=VMEM_LIMIT),
        cost_estimate=pl.CostEstimate(
            flops=flops // COST_SHARE, bytes_accessed=moved // COST_SHARE, transcendentals=0
        ),
    )(*operands)


def aligned(index, unit):
    return pl.multiple_of(index * unit, unit)


def start_all(copies):
    for copy in copies:
        copy.start()
    return copies


def wait_all(copies):
    for copy in copies:
        copy.wait()


def causal_mask(block):
    key_at = lax.broadcasted_iota(jnp.int32, (block, block), 0)
    query_at = lax.broadcasted_iota(jnp.int32, (block, block), 1)
    return key_at <= query_at


def forward_body(n, info, *refs):
    q_in, kv_in = refs[:n], refs[n : 2 * n]
    outs, stats, ot = refs[2 * n : 3 * n], refs[3 * n], refs[3 * n + 1]
    qs, ks, vs, vt, mixed, sems = refs[3 * n + 2 :]
    me, length, spot = info[0], info[1], info[2]
    count, width = q_in[0].shape
    heads = width // HEAD_DIM
    total = n * count
    blocks = total // ATT_BLOCK
    copies = []
    for r in range(n):
        rows = pl.ds(aligned(me ^ r, count), count)
        query_rows = pl.ds(aligned(spot ^ r, count), count)
        for k, (src, dst) in enumerate(
            (
                (kv_in[r].at[:, pl.ds(0, width)], ks.at[rows]),
                (kv_in[r].at[:, pl.ds(width, width)], vs.at[rows]),
                (q_in[r], qs.at[query_rows]),
            )
        ):
            copies.append(pltpu.make_async_copy(src, dst, sems.at[3 * r + k]))
    wait_all(start_all(copies))
    factor = HEAD_DIM ** (-0.5) * LOG2_E

    def transpose_values(b, _):
        at = pl.ds(pl.multiple_of(b * ATT_BLOCK, ATT_BLOCK), ATT_BLOCK)
        vt[:, at] = vs[at, :].T
        return 0

    lax.fori_loop(0, blocks, transpose_values, 0)
    live = jnp.minimum((length + ATT_BLOCK - 1) // ATT_BLOCK, blocks)

    def tile(qi, kj, state, masked):
        new = []
        q_at = pl.ds(pl.multiple_of(qi * ATT_BLOCK, ATT_BLOCK), ATT_BLOCK)
        k_at = pl.ds(pl.multiple_of(kj * ATT_BLOCK, ATT_BLOCK), ATT_BLOCK)
        for h in range(heads):
            cols = slice(h * HEAD_DIM, (h + 1) * HEAD_DIM)
            top, total_sum, acc = state[h]
            scores = nt_dot(ks[k_at, cols], qs[q_at, cols]) * factor
            if masked:
                scores = jnp.where(causal_mask(ATT_BLOCK), scores, -DEAD)
            higher = jnp.maximum(top, jnp.max(scores, axis=0, keepdims=True))
            weights = jnp.exp2(scores - higher)
            shrink = jnp.exp2(top - higher)
            total_sum = total_sum * shrink + jnp.sum(weights, axis=0, keepdims=True)
            acc = acc * shrink + jnp.dot(
                vt[cols, k_at], weights.astype(jnp.bfloat16), preferred_element_type=jnp.float32
            )
            new.append((higher, total_sum, acc))
        return tuple(new)

    stats[...] = jnp.full(stats.shape, DEAD, jnp.float32)

    def query_block(qi, _):
        first = tuple(
            (
                jnp.full((1, ATT_BLOCK), -DEAD, jnp.float32),
                jnp.zeros((1, ATT_BLOCK), jnp.float32),
                jnp.zeros((HEAD_DIM, ATT_BLOCK), jnp.float32),
            )
            for _ in range(heads)
        )
        state = lax.fori_loop(0, qi, lambda kj, s: tile(qi, kj, s, False), first)
        state = tile(qi, qi, state, True)
        q_at = pl.ds(pl.multiple_of(qi * ATT_BLOCK, ATT_BLOCK), ATT_BLOCK)
        query_at = qi * ATT_BLOCK + lax.broadcasted_iota(jnp.int32, (1, ATT_BLOCK), 1)
        alive = query_at < length
        for h in range(heads):
            cols = slice(h * HEAD_DIM, (h + 1) * HEAD_DIM)
            top, total_sum, acc = state[h]
            scaled = acc * jnp.where(alive, 1.0 / total_sum, 0.0)
            ot[cols, q_at] = scaled
            mixed[q_at, cols] = scaled.T.astype(jnp.bfloat16)
            stats[h : h + 1, q_at] = jnp.where(alive, top + jnp.log2(total_sum), DEAD)
        return 0

    lax.fori_loop(0, live, query_block, 0)

    def dead_block(qi, _):
        q_at = pl.ds(pl.multiple_of(qi * ATT_BLOCK, ATT_BLOCK), ATT_BLOCK)
        mixed[q_at, :] = jnp.zeros((ATT_BLOCK, width), jnp.bfloat16)
        ot[:, q_at] = jnp.zeros((width, ATT_BLOCK), jnp.float32)
        return 0

    lax.fori_loop(live, blocks, dead_block, 0)
    copies = []
    for r in range(n):
        rows = pl.ds(pl.multiple_of((me ^ r) * count, count), count)
        copies.append(pltpu.make_async_copy(mixed.at[rows], outs[r], sems.at[r]))
    wait_all(start_all(copies))


def attention_forward(info, q_blocks, kv_blocks):
    n = len(q_blocks)
    count, width = q_blocks[0].shape
    total = n * count
    got = call(
        functools.partial(forward_body, n),
        [info, *q_blocks, *kv_blocks],
        [IN_SMEM] + [ANYWHERE] * (2 * n),
        [((count, width), jnp.bfloat16)] * n
        + [((8, total), jnp.float32), ((width, total), jnp.float32)],
        [ANYWHERE] * n + [IN_VMEM] * 2,
        [pltpu.VMEM((total, width), jnp.bfloat16)] * 3
        + [pltpu.VMEM((width, total), jnp.bfloat16), pltpu.VMEM((total, width), jnp.bfloat16)]
        + [pltpu.SemaphoreType.DMA((3 * n,))],
        16 * 2 * total * total * width // 2,
        10 * total * width,
        "attention_forward",
    )
    return got[:n], got[n], got[n + 1]


def backward_body(n, info, *refs):
    q_in, kv_in, g_in = refs[:n], refs[n : 2 * n], refs[2 * n : 3 * n]
    stats, ot = refs[3 * n], refs[3 * n + 1]
    refs = refs[3 * n + 2 :]
    dq_out, dkv_out = refs[:n], refs[n : 2 * n]
    qs, ks, vs, gs, kt, delta, dqt, dk, dv, dq_low, dkv_low, sems = refs[2 * n :]
    me, length, spot = info[0], info[1], info[2]
    count, width = q_in[0].shape
    heads = width // HEAD_DIM
    total = n * count
    blocks = total // ATT_BLOCK
    copies = []
    for r in range(n):
        rows = pl.ds(aligned(me ^ r, count), count)
        query_rows = pl.ds(aligned(spot ^ r, count), count)
        for k, (src, dst) in enumerate(
            (
                (kv_in[r].at[:, pl.ds(0, width)], ks.at[rows]),
                (kv_in[r].at[:, pl.ds(width, width)], vs.at[rows]),
                (q_in[r], qs.at[query_rows]),
                (g_in[r], gs.at[rows]),
            )
        ):
            copies.append(pltpu.make_async_copy(src, dst, sems.at[4 * r + k]))
    start_all(copies)
    live = jnp.minimum((length + ATT_BLOCK - 1) // ATT_BLOCK, blocks)
    scale = HEAD_DIM ** (-0.5)
    factor = scale * LOG2_E

    def clear(b, _):
        at = pl.ds(pl.multiple_of(b * ATT_BLOCK, ATT_BLOCK), ATT_BLOCK)
        dqt[:, at] = jnp.zeros((width, ATT_BLOCK), jnp.float32)
        dk[at, :] = jnp.zeros((ATT_BLOCK, width), jnp.float32)
        dv[at, :] = jnp.zeros((ATT_BLOCK, width), jnp.float32)
        return 0

    lax.fori_loop(0, blocks, clear, 0)
    wait_all(copies)

    def prepare(b, _):
        at = pl.ds(pl.multiple_of(b * ATT_BLOCK, ATT_BLOCK), ATT_BLOCK)
        kt[:, at] = ks[at, :].T
        both = gs[at, :].astype(jnp.float32).T * ot[:, at]
        for h in range(heads):
            cols = slice(h * HEAD_DIM, (h + 1) * HEAD_DIM)
            delta[h : h + 1, at] = jnp.sum(both[cols], axis=0, keepdims=True)
        return 0

    lax.fori_loop(0, blocks, prepare, 0)

    def tile(qi, kj, masked):
        q_at = pl.ds(pl.multiple_of(qi * ATT_BLOCK, ATT_BLOCK), ATT_BLOCK)
        k_at = pl.ds(pl.multiple_of(kj * ATT_BLOCK, ATT_BLOCK), ATT_BLOCK)
        for h in range(heads):
            cols = slice(h * HEAD_DIM, (h + 1) * HEAD_DIM)
            q, g = qs[q_at, cols], gs[q_at, cols]
            scores = nt_dot(ks[k_at, cols], q) * factor - stats[h : h + 1, q_at]
            if masked:
                scores = jnp.where(causal_mask(ATT_BLOCK), scores, -DEAD)
            weights = jnp.exp2(scores)
            grad_weights = nt_dot(vs[k_at, cols], g)
            grad_scores = (weights * (grad_weights - delta[h : h + 1, q_at])).astype(jnp.bfloat16)
            dv[k_at, cols] += jnp.dot(
                weights.astype(jnp.bfloat16), g, preferred_element_type=jnp.float32
            )
            dk[k_at, cols] += jnp.dot(grad_scores, q, preferred_element_type=jnp.float32)
            dqt[cols, q_at] += jnp.dot(
                kt[cols, k_at], grad_scores, preferred_element_type=jnp.float32
            )

    def query_block(qi, _):
        def step(kj, _):
            tile(qi, kj, False)
            return 0

        lax.fori_loop(0, qi, step, 0)
        tile(qi, qi, True)
        return 0

    lax.fori_loop(0, live, query_block, 0)

    def finish(b, _):
        at = pl.ds(pl.multiple_of(b * ATT_BLOCK, ATT_BLOCK), ATT_BLOCK)
        dq_low[at, :] = (dqt[:, at] * scale).T.astype(jnp.bfloat16)
        dkv_low[at, :width] = (dk[at, :] * scale).astype(jnp.bfloat16)
        dkv_low[at, width:] = dv[at, :].astype(jnp.bfloat16)
        return 0

    lax.fori_loop(0, blocks, finish, 0)
    copies = []
    for r in range(n):
        rows = pl.ds(pl.multiple_of((me ^ r) * count, count), count)
        copies.append(pltpu.make_async_copy(dq_low.at[rows], dq_out[r], sems.at[2 * r]))
        copies.append(pltpu.make_async_copy(dkv_low.at[rows], dkv_out[r], sems.at[2 * r + 1]))
    wait_all(start_all(copies))


def attention_backward(info, q_blocks, kv_blocks, g_blocks, stats, ot):
    n = len(q_blocks)
    count, width = q_blocks[0].shape
    total = n * count
    low_all = pltpu.VMEM((total, width), jnp.bfloat16)
    got = call(
        functools.partial(backward_body, n),
        [info, *q_blocks, *kv_blocks, *g_blocks, stats, ot],
        [IN_SMEM] + [ANYWHERE] * (3 * n) + [IN_VMEM] * 2,
        [((count, width), jnp.bfloat16)] * n + [((count, 2 * width), jnp.bfloat16)] * n,
        [ANYWHERE] * (2 * n),
        [low_all] * 4
        + [
            pltpu.VMEM((width, total), jnp.bfloat16),
            pltpu.VMEM((8, total), jnp.float32),
            pltpu.VMEM((width, total), jnp.float32),
            pltpu.VMEM((total, width), jnp.float32),
            pltpu.VMEM((total, width), jnp.float32),
            low_all,
            pltpu.VMEM((total, 2 * width), jnp.bfloat16),
            pltpu.SemaphoreType.DMA((4 * n,)),
        ],
        40 * 2 * total * total * width // 2,
        20 * total * width,
        "attention_backward",
    )
    return got[:n], got[n:]


def pack_body(n, info, keys, values, *refs):
    outs, sems = refs[:n], refs[n]
    me = info[0]
    width = outs[0].shape[1] // 2
    copies = []
    for r in range(n):
        cols = pl.ds(aligned(me ^ r, width), width)
        copies.append(
            pltpu.make_async_copy(keys.at[:, cols], outs[r].at[:, pl.ds(0, width)], sems.at[2 * r])
        )
        copies.append(
            pltpu.make_async_copy(
                values.at[:, cols], outs[r].at[:, pl.ds(width, width)], sems.at[2 * r + 1]
            )
        )
    wait_all(start_all(copies))


def pack_keys_values(n, info, keys, values):
    count, depth = keys.shape
    return call(
        functools.partial(pack_body, n),
        [info, keys, values],
        [IN_SMEM, ANYWHERE, ANYWHERE],
        [((count, 2 * depth // n), jnp.bfloat16)] * n,
        [IN_VMEM] * n,
        [pltpu.SemaphoreType.DMA((2 * n,))],
        0,
        8 * count * depth,
        "pack_keys_values",
    )


GAIN_ROWS = 32


def norm_parts(v):
    return lax.rsqrt(jnp.mean(v * v, axis=-1, keepdims=True) + EPSILON)


def query_body(n, nd, info, *refs):
    xs, pieces = refs[:nd], refs[nd : nd + n + 1]
    q_out = refs[nd + n + 1 : nd + 2 * n + 1]
    normed, gains, weight, out_weight = refs[nd + 2 * n + 1 : nd + 2 * n + 5]
    queries, gain_rows, sems = refs[nd + 2 * n + 5 :]
    me, dp = info[0], info[1]
    count, depth = xs[0].shape
    wrows = (pieces[0].shape[0] - GAIN_ROWS) // 2
    cut = wrows - GAIN_ROWS // 2
    copies, later = [], []

    def fetch(into, k, src, dst, j):
        into.append(pltpu.make_async_copy(src, dst, sems.at[3 * k + j]))

    for k in range(n):
        first = info[3 + k] * wrows
        gain_at = gain_rows.at[pl.ds(aligned(info[3 + k], 16), 16)]
        fetch(copies, k, pieces[k].at[pl.ds(0, 16)], gain_at, 0)
        at = pl.multiple_of(first, 16)
        if k < n - 1:
            rows = pl.ds(at, wrows)
            fetch(copies, k, pieces[k].at[pl.ds(GAIN_ROWS, wrows)], weight.at[rows], 1)
            fetch(later, k, pieces[k].at[pl.ds(GAIN_ROWS + wrows, wrows)], out_weight.at[rows], 2)
        else:
            below = pl.multiple_of(first + cut, 16)
            fetch(copies, k, pieces[k].at[pl.ds(GAIN_ROWS, cut)], weight.at[pl.ds(at, cut)], 1)
            rest = pl.ds(below, wrows - cut)
            fetch(copies, k, pieces[n].at[pl.ds(0, wrows - cut)], weight.at[rest], 2)
            tail = pieces[n].at[pl.ds(wrows - cut, wrows)]
            fetch(later, n, tail, out_weight.at[pl.ds(at, wrows)], 0)
    start_all(copies)
    start_all(later)
    wait_all(copies)
    share = depth // n
    for o in range(n):
        row = gain_rows[o * 16 : o * 16 + 16, : 2 * share].astype(jnp.float32)
        gains[0:1, o * share : (o + 1) * share] = row[0:1, :share]
        gains[1:2, o * share : (o + 1) * share] = row[0:1, share:]
    for k in range(nd):
        v = xs[k][...].astype(jnp.float32)
        rows = slice(k * count, (k + 1) * count)
        normed[rows, :] = (v * norm_parts(v) * gains[0:1, :]).astype(jnp.bfloat16)
        queries[rows, :] = jnp.dot(
            normed[rows, :], weight[...], preferred_element_type=jnp.float32
        ).astype(jnp.bfloat16)
    per = n // nd
    copies = []
    for m in range(n):
        j = me ^ m
        slot = dp ^ (j // per)
        copies.append(
            pltpu.make_async_copy(
                queries.at[
                    pl.ds(aligned(slot, count), count), pl.ds(aligned(j % per, share), share)
                ],
                q_out[m],
                sems.at[3 * n + 3 + m],
            )
        )
    wait_all(start_all(copies))
    wait_all(later)


def project_queries(n, nd, info, xs, pieces):
    count, depth = xs[0].shape
    quarter = pieces[0].shape[1]
    got = call(
        functools.partial(query_body, n, nd),
        [info, *xs, *pieces],
        [IN_SMEM] + [IN_VMEM] * nd + [ANYWHERE] * (n + 1),
        [((count, depth // n), jnp.bfloat16)] * n
        + [
            ((nd * count, depth), jnp.bfloat16),
            ((8, depth), jnp.float32),
            ((depth, quarter), jnp.bfloat16),
            ((depth, quarter), jnp.bfloat16),
        ],
        [ANYWHERE] * n + [IN_VMEM] * 4,
        [
            pltpu.VMEM((nd * count, quarter), jnp.bfloat16),
            pltpu.VMEM((n * 16, quarter), jnp.bfloat16),
            pltpu.SemaphoreType.DMA((4 * n + 3,)),
        ],
        2 * count * depth * depth,
        6 * depth * depth,
        "project_queries",
    )
    return got[:n], *got[n:]


def padded(width):
    return (width + 127) // 128 * 128


def ffn_body(m, *refs):
    nf_in, cot_in, weights_in = refs[:m], refs[m : 2 * m], refs[2 * m : 2 * m + 3]
    outs = refs[2 * m + 3 : 7 * m + 3]
    nf, cot, gate_w, up_w, down_w, acts, shares, sems, out_sems = refs[7 * m + 3 :]
    weights = (gate_w, up_w, down_w)
    rows = nf_in[0].shape[0]
    hidden_units = gate_w.shape[0]

    def load(src, dst, k):
        return pltpu.make_async_copy(src, dst, sems.at[k])

    loads = [load(weights_in[k], weights[k], k) for k in range(3)]
    nf_loads = [load(nf_in[b], nf.at[b], 3 + b) for b in range(m)]
    cot_loads = [load(cot_in[b], cot.at[b], 3 + m + b) for b in range(m)]
    start_all([nf_loads[0], loads[0], loads[1], cot_loads[0], loads[2]])
    start_all([*nf_loads[1:], *cot_loads[1:]])
    copies = []

    def store(b, k, src):
        copy = pltpu.make_async_copy(src, outs[5 * b + k], out_sems.at[5 * b + k])
        copy.start()
        copies.append(copy)

    for b in range(m):
        nf_loads[b].wait()
        if b == 0:
            loads[0].wait()
        gate_value = nt_dot(nf[b], gate_w[...])
        if b == 0:
            loads[1].wait()
        up_value = nt_dot(nf[b], up_w[...])
        cot_loads[b].wait()
        if b == 0:
            loads[2].wait()
        grad_inner = nt_dot(cot[b], down_w[...])
        sigmoid = 1.0 / (1.0 + jnp.exp(-gate_value))
        act = gate_value * sigmoid
        inner = (act * up_value).astype(jnp.bfloat16)
        grad_gate = (
            grad_inner * up_value * sigmoid * (1.0 + gate_value * (1.0 - sigmoid))
        ).astype(jnp.bfloat16)
        grad_up = (grad_inner * act).astype(jnp.bfloat16)
        for k, value in enumerate((inner, grad_gate, grad_up)):
            acts[3 * b + k, :, :hidden_units] = value
            store(b, k, acts.at[3 * b + k])
        shares[2 * b] = jnp.dot(
            grad_gate, gate_w[...], preferred_element_type=jnp.float32
        ) + jnp.dot(grad_up, up_w[...], preferred_element_type=jnp.float32)
        store(b, 3, shares.at[2 * b])
        shares[2 * b + 1] = jnp.dot(inner, down_w[...], preferred_element_type=jnp.float32)
        store(b, 4, shares.at[2 * b + 1])
    wait_all(copies)


def ffn_blocks(nf, cot, weights):
    m = len(nf)
    rows, depth = nf[0].shape
    units = weights[0].shape[0]
    act = ((rows, padded(units)), jnp.bfloat16)
    share = ((rows, depth), jnp.float32)
    got = call(
        functools.partial(ffn_body, m),
        [*nf, *cot, *weights],
        [ANYWHERE] * (2 * m + 3),
        [act, act, act, share, share] * m,
        [ANYWHERE] * (5 * m),
        [pltpu.VMEM((m, rows, depth), jnp.bfloat16)] * 2
        + [pltpu.VMEM((units, depth), jnp.bfloat16)] * 3
        + [
            pltpu.VMEM((3 * m, rows, padded(units)), jnp.bfloat16),
            pltpu.VMEM((2 * m, rows, depth), jnp.float32),
            pltpu.SemaphoreType.DMA((3 + 2 * m,)),
            pltpu.SemaphoreType.DMA((5 * m,)),
        ],
        12 * m * rows * units * depth,
        6 * units * depth + 12 * m * rows * depth,
        "ffn_blocks",
    )
    return [got[5 * b : 5 * b + 5] for b in range(m)]


def weight_gradient_body(count, units, info, *refs):
    lhs_in, rhs_in = refs[:count], refs[count : 2 * count]
    kept, sent, lhs, turned, rhs, sems = refs[2 * count :]
    core = info[2]
    copies, first = [], 0
    for k in range(count):
        rows = lhs_in[k].shape[0]
        at = pl.ds(first, rows)
        copies.append(pltpu.make_async_copy(lhs_in[k], lhs.at[at], sems.at[2 * k]))
        copies.append(pltpu.make_async_copy(rhs_in[k], rhs.at[at], sems.at[2 * k + 1]))
        first += rows
    start_all(copies)
    wait_all(copies[::2])
    block = 256

    def turn(b, _):
        at = pl.ds(aligned(b, block), block)
        turned[:, at] = lhs[at, :].T
        return 0

    lax.fori_loop(0, first // block, turn, 0)
    wait_all(copies[1::2])
    half = kept.shape[1]
    piece = 256

    def step(c, _):
        to = pl.ds(aligned(c, piece), piece)
        for out, side in ((kept, core), (sent, 1 - core)):
            cols = pl.ds(pl.multiple_of(side * half + c * piece, piece), piece)
            out[:, to] = jnp.dot(
                turned[...], rhs[:, cols], preferred_element_type=jnp.float32
            )[:units].astype(jnp.bfloat16)
        return 0

    lax.fori_loop(0, half // piece, step, 0)


def weight_gradient(info, lhs, rhs, units):
    count = len(lhs)
    rows = sum(b.shape[0] for b in rhs)
    width, depth = lhs[0].shape[1], rhs[0].shape[1]
    return call(
        functools.partial(weight_gradient_body, count, units),
        [info, *lhs, *rhs],
        [IN_SMEM] + [ANYWHERE] * (2 * count),
        [((units, depth // 2), jnp.bfloat16)] * 2,
        [IN_VMEM] * 2,
        [
            pltpu.VMEM((rows, width), jnp.bfloat16),
            pltpu.VMEM((width, rows), jnp.bfloat16),
            pltpu.VMEM((rows, depth), jnp.bfloat16),
            pltpu.SemaphoreType.DMA((2 * count,)),
        ],
        2 * rows * units * depth,
        2 * rows * depth,
        "weight_gradient",
    )


def hidden_body(n, nd, info, x, gains, *refs):
    blocks, parts = refs[:n], refs[n : n + nd]
    hidden, normed, mixed = refs[n + nd : n + nd + 3]
    weight, sems = refs[n + nd + 3 :]
    me, dp = info[0], info[1]
    share, quarter = blocks[0].shape[1], parts[0].shape[1]
    copies = []
    for r in range(nd):
        cols = pl.ds(aligned(dp ^ r, quarter), quarter)
        copies.append(pltpu.make_async_copy(parts[r], weight.at[:, cols], sems.at[r]))
    for r in range(n):
        cols = pl.ds(aligned(me ^ r, share), share)
        copies.append(pltpu.make_async_copy(blocks[r], mixed.at[:, cols], sems.at[nd + r]))
    wait_all(start_all(copies))
    depth = x.shape[1]
    piece = 512

    def step(c, total):
        cols = pl.ds(aligned(c, piece), piece)
        v = x[:, cols].astype(jnp.float32) + jnp.dot(
            mixed[...], weight[:, cols], preferred_element_type=jnp.float32
        )
        hidden[:, cols] = v
        return total + jnp.sum(v * v, axis=-1, keepdims=True)

    total = lax.fori_loop(0, depth // piece, step, jnp.zeros((x.shape[0], 1), jnp.float32))
    normed[...] = (
        hidden[...] * lax.rsqrt(total / depth + EPSILON) * gains[1:2, :]
    ).astype(jnp.bfloat16)


def project_mixed(n, nd, info, x, gains, blocks, parts):
    count, depth = x.shape
    return call(
        functools.partial(hidden_body, n, nd),
        [info, x, gains, *blocks, *parts],
        [IN_SMEM, IN_VMEM, IN_VMEM] + [ANYWHERE] * (n + nd),
        [
            ((count, depth), jnp.float32),
            ((count, depth), jnp.bfloat16),
            ((count, depth), jnp.bfloat16),
        ],
        [IN_VMEM] * 3,
        [pltpu.VMEM((depth, depth), jnp.bfloat16), pltpu.SemaphoreType.DMA((n + nd,))],
        2 * count * depth * depth,
        6 * depth * depth,
        "project_mixed",
    )


def norm_grad(v, gain, upstream):
    scale = norm_parts(v)
    weighted = upstream * gain
    through = weighted * scale - v * (scale**3) * jnp.mean(weighted * v, axis=-1, keepdims=True)
    return through, jnp.sum(upstream * v * scale, axis=0, keepdims=True)


def branch_body(n, nd, info, hidden, gains, cotangent, own, first, second, *refs):
    parts, refs = refs[:nd], refs[nd:]
    gm_out, cols_out = refs[:n], refs[n : n + nd]
    grad_hidden, gain_part, branch, weight, sems = refs[n + nd :]
    me, dp = info[0], info[1]
    quarter = parts[0].shape[1]
    copies = []
    for r in range(nd):
        cols = pl.ds(aligned(dp ^ r, quarter), quarter)
        copies.append(pltpu.make_async_copy(parts[r], weight.at[:, cols], sems.at[r]))
    start_all(copies)
    upstream = own[...] + first[...].astype(jnp.float32) + second[...].astype(jnp.float32)
    through, gain = norm_grad(hidden[...], gains[1:2, :], upstream)
    gain_part[...] = jnp.broadcast_to(gain, gain_part.shape)
    total = cotangent[...].astype(jnp.float32) + through
    grad_hidden[...] = total
    branch[...] = total.astype(jnp.bfloat16)
    for r in range(nd):
        cols_out[r][...] = branch[:, pl.ds(aligned(dp ^ r, quarter), quarter)]
    wait_all(copies)
    share = gm_out[0].shape[1]
    for r in range(n):
        rows = pl.ds(aligned(me ^ r, share), share)
        gm_out[r][...] = nt_dot(branch[...], weight[rows, :]).astype(jnp.bfloat16)


def branch_gradient(n, nd, info, hidden, gains, cotangent, sums, parts):
    count, depth = cotangent.shape
    got = call(
        functools.partial(branch_body, n, nd),
        [info, hidden, gains, cotangent, *sums, *parts],
        [IN_SMEM] + [IN_VMEM] * 6 + [ANYWHERE] * nd,
        [((count, depth // n), jnp.bfloat16)] * n
        + [((count, depth // nd), jnp.bfloat16)] * nd
        + [((count, depth), jnp.float32), ((8, depth), jnp.float32)],
        [IN_VMEM] * (n + nd + 2),
        [
            pltpu.VMEM((count, depth), jnp.bfloat16),
            pltpu.VMEM((depth, depth), jnp.bfloat16),
            pltpu.SemaphoreType.DMA((nd,)),
        ],
        2 * count * depth * depth,
        6 * depth * depth,
        "branch_gradient",
    )
    return got[:n], got[n : n + nd], got[n + nd], got[n + nd + 1]


def sort_body(n, nd, info, *refs):
    blocks, cols_out = refs[:n], refs[n : n + nd]
    rows, sems = refs[n + nd :]
    me, dp = info[0], info[1]
    share, quarter = blocks[0].shape[1], cols_out[0].shape[1]
    copies = []
    for r in range(n):
        cols = pl.ds(aligned(me ^ r, share), share)
        copies.append(pltpu.make_async_copy(blocks[r], rows.at[:, cols], sems.at[r]))
    wait_all(start_all(copies))
    copies = []
    for r in range(nd):
        cols = pl.ds(aligned(dp ^ r, quarter), quarter)
        copies.append(pltpu.make_async_copy(rows.at[:, cols], cols_out[r], sems.at[r]))
    wait_all(start_all(copies))


def sort_columns(n, nd, info, blocks):
    count, share = blocks[0].shape
    depth = n * share
    return call(
        functools.partial(sort_body, n, nd),
        [info, *blocks],
        [IN_SMEM] + [ANYWHERE] * n,
        [((count, depth // nd), jnp.bfloat16)] * nd,
        [ANYWHERE] * nd,
        [pltpu.VMEM((count, depth), jnp.bfloat16), pltpu.SemaphoreType.DMA((max(n, nd),))],
        0,
        6 * count * depth,
        "sort_columns",
    )


def split_body(n, info, *refs):
    blocks, keys, values, sems = refs[:n], refs[n], refs[n + 1], refs[n + 2]
    me = info[0]
    share = blocks[0].shape[1] // 2
    copies = []
    for r in range(n):
        cols = pl.ds(aligned(me ^ r, share), share)
        copies.append(
            pltpu.make_async_copy(blocks[r].at[:, pl.ds(0, share)], keys.at[:, cols], sems.at[2 * r])
        )
        copies.append(
            pltpu.make_async_copy(
                blocks[r].at[:, pl.ds(share, share)], values.at[:, cols], sems.at[2 * r + 1]
            )
        )
    wait_all(start_all(copies))


def split_keys_values(n, info, blocks):
    count, share = blocks[0].shape
    depth = n * share // 2
    return call(
        functools.partial(split_body, n),
        [info, *blocks],
        [IN_SMEM] + [ANYWHERE] * n,
        [((count, depth), jnp.bfloat16)] * 2,
        [IN_VMEM] * 2,
        [pltpu.SemaphoreType.DMA((2 * n,))],
        0,
        8 * count * depth,
        "split_keys_values",
    )


def input_body(nd, x, gains, grad_hidden, *refs):
    cols, parts = refs[:nd], refs[nd : 2 * nd]
    out, gain_part, upstream = refs[2 * nd :]
    piece = 512

    def step(c, _):
        rows = pl.ds(aligned(c, piece), piece)
        upstream[:, rows] = sum(nt_dot(cols[r][...], parts[r][rows, :]) for r in range(nd))
        return 0

    lax.fori_loop(0, x.shape[1] // piece, step, 0)
    through, gain = norm_grad(x[...].astype(jnp.float32), gains[0:1, :], upstream[...])
    gain_part[...] = jnp.broadcast_to(gain, gain_part.shape)
    out[...] = (grad_hidden[...] + through).astype(jnp.bfloat16)


def input_gradient(nd, x, gains, grad_hidden, cols, parts):
    count, depth = x.shape
    return call(
        functools.partial(input_body, nd),
        [x, gains, grad_hidden, *cols, *parts],
        [IN_VMEM] * (3 + 2 * nd),
        [((count, depth), jnp.bfloat16), ((8, depth), jnp.float32)],
        [IN_VMEM] * 2,
        [pltpu.VMEM((count, depth), jnp.float32)],
        2 * count * depth * depth,
        6 * depth * depth,
        "input_gradient",
    )


def projections_body(n, nd, info, normed, attn_part, ffn_part, *refs):
    branch_cols, query_cols, mixed_in = refs[:nd], refs[nd : 2 * nd], refs[2 * nd : 3 * nd]
    outs = refs[3 * nd : 3 * nd + n]
    branch, query, mixed = refs[3 * nd + n :]
    count = branch_cols[0].shape[0]
    share = mixed.shape[1] // n
    for k in range(nd):
        rows = slice(k * count, (k + 1) * count)
        mixed[rows, :] = mixed_in[k][...]
        branch[rows, :] = branch_cols[k][...]
        query[rows, :] = query_cols[k][...]
    for k in range(n):
        cols = pl.ds(aligned(info[3 + k], share), share)
        outs[k][:share, :] = tn_dot(mixed[:, cols], branch[...])
        outs[k][share : 2 * share, :] = tn_dot(normed[:, cols], query[...])
        outs[k][2 * share :, :] = jnp.zeros((GAIN_ROWS, branch.shape[1]), jnp.float32)
        outs[k][2 * share : 2 * share + 8, :share] = attn_part[:, cols]
        outs[k][2 * share : 2 * share + 8, share : 2 * share] = ffn_part[:, cols]


def projection_gradients(n, nd, info, mixed, normed, attn_part, ffn_part, branch_cols, query_cols):
    rows, depth = normed.shape
    count, quarter = branch_cols[0].shape
    return call(
        functools.partial(projections_body, n, nd),
        [info, normed, attn_part, ffn_part, *branch_cols, *query_cols, *mixed],
        [IN_SMEM] + [IN_VMEM] * (3 + 3 * nd),
        [((2 * depth // n + GAIN_ROWS, quarter), jnp.float32)] * n,
        [IN_VMEM] * n,
        [pltpu.VMEM((rows, quarter), jnp.bfloat16)] * 2
        + [pltpu.VMEM((rows, depth), jnp.bfloat16)],
        4 * rows * depth * quarter,
        4 * rows * depth,
        "projection_gradients",
    )


def join_body(nd, info, *refs):
    parts, (out_grad, query_grad, gain_sum) = refs[:nd], refs[nd:]
    share = out_grad.shape[0]
    quarter = parts[0].shape[1]
    dp = info[1]
    for r in range(nd):
        cols = pl.ds(aligned(dp ^ r, quarter), quarter)
        part = parts[r][...].astype(jnp.float32)
        out_grad[:, cols] = part[:share]
        query_grad[:, cols] = part[share : 2 * share]
    tops = [parts[r][2 * share : 2 * share + 16, :].astype(jnp.float32)[:8] for r in range(nd)]
    gain_sum[...] = tree_sum(tops)


def join_projections(nd, info, parts):
    rows, quarter = parts[0].shape
    share, depth = (rows - GAIN_ROWS) // 2, quarter * nd
    return call(
        functools.partial(join_body, nd),
        [info, *parts],
        [IN_SMEM] + [IN_VMEM] * nd,
        [((share, depth), jnp.float32)] * 2 + [((8, quarter), jnp.float32)],
        [IN_VMEM] * 3,
        [],
        0,
        10 * share * depth,
        "join_projections",
    )


def chip_sum_body(kept, *refs):
    others, out = refs[:-1], refs[-1]
    half = len(others) // 2
    top = others[0].shape[0]
    for side, first in ((others[:half], 0), (others[half:], top)):
        rows = slice(first, first + side[0].shape[0])
        terms = [kept[rows, :].astype(jnp.float32)] + [v[...].astype(jnp.float32) for v in side]
        out[rows, :] = tree_sum(terms).astype(jnp.bfloat16)


def chip_sum(operands):
    shape = operands[0].shape
    return call(
        chip_sum_body,
        operands,
        [IN_VMEM] * len(operands),
        [(shape, jnp.bfloat16)],
        [IN_VMEM],
        [],
        0,
        6 * shape[0] * shape[1],
        "chip_sum",
    )[0]


def spread_body(info, mine, other, out):
    half = mine.shape[1]
    for ref, side in ((mine, info[2]), (other, 1 - info[2])):
        out[:, pl.ds(aligned(side, half), half)] = ref[...].astype(jnp.float32)


def spread_columns(info, mine, other):
    rows, half = mine.shape
    return call(
        spread_body,
        [info, mine, other],
        [IN_SMEM, IN_VMEM, IN_VMEM],
        [((rows, 2 * half), jnp.float32)],
        [IN_VMEM],
        [],
        0,
        12 * rows * half,
        "spread_columns",
    )[0]


def tree_sum(parts):
    while len(parts) > 1:
        parts = [parts[k] + parts[k + 1] for k in range(0, len(parts), 2)]
    return parts[0]


def columns(x, start, width):
    return lax.dynamic_slice_in_dim(x, start, width, 1)


def make_local(mesh):
    net = Links(mesh)
    n, nd = net.n, net.nd
    dp_order = list(range(0, nd, 2)) + list(range(1, nd, 2))
    half_way = n // 2
    ring_order = [0] + [s for k in range(1, half_way) for s in (-k, k)] + ["a", "b"]

    def exchange(blocks, axis="seq"):
        return [b if r == 0 else net.swap(b, axis, r) for r, b in enumerate(blocks)]

    def chips(x, *deps):
        sent = after(x, *deps)
        return [x] + [net.swap(sent, "dp", r) for r in range(2, nd, 2)]

    def cores(near, *deps):
        return list(near) + [net.swap(v, "dp", 1) for v in tie(near, *deps)]

    def paced(ring, blocks, spare=1):
        out, sent = [], 1
        arrived = ring.step()
        steps = half_way - 1
        for k in range(steps):
            until = 1 + (n - 1) * (k + 1) // steps
            some = tie(blocks[sent:until], *arrived)
            fresh = [net.swap(b, "seq", sent + i) for i, b in enumerate(some)]
            arrived = ring.step(*out[-len(some) :]) if k else ring.step()
            out += fresh
            sent = until
        return out

    def local(
        layer_input,
        global_keys,
        global_values,
        lengths,
        attn_gain,
        query_weight,
        out_weight,
        ffn_gain,
        gate_weight,
        up_weight,
        down_weight,
        cotangent,
    ):
        length = lengths[0]
        me, mine = lax.axis_index("seq"), lax.axis_index("dp")
        core, group = mine % 2, net.group(mine)
        place = net.place()
        depth = layer_input.shape[1]
        quarter = depth // nd
        per = n // nd
        owners = [net.owner(place, key) for key in ring_order[:-2]] + [net.owner(place, half_way)]
        info = jnp.stack([me, group, core, *owners]).astype(jnp.int32)
        heads_info = jnp.stack([me, length, group * per + me % per]).astype(jnp.int32)

        gains = jnp.concatenate([attn_gain, ffn_gain])
        gain_rows = jnp.zeros((GAIN_ROWS, quarter), jnp.bfloat16)
        gain_rows = gain_rows.at[:, : gains.shape[0]].set(gains[None])
        mine_of = [columns(w, group * quarter, quarter) for w in (query_weight, out_weight)]
        ring = RingGather(net, jnp.concatenate([gain_rows, *mine_of], 0))
        kv_sent = list(pack_keys_values(n, info, global_keys, global_values))
        kv_blocks = [kv_sent[0]] + paced(ring, kv_sent)
        got = ring.got
        xs = cores(chips(layer_input), got["a"], got["b"])
        q_sent, normed_all, gains, query_quarter, out_quarter = project_queries(
            n, nd, info, xs, [got[k] for k in ring_order]
        )
        q_sent = tie(q_sent, *kv_blocks)
        q_blocks = [net.to_heads(b, m) for m, b in enumerate(q_sent)]
        out_near = chips(out_quarter, *q_blocks)
        mixed_sent, stats, ot = attention_forward(heads_info, q_blocks, kv_blocks)
        cot_ring = RingGather(net, cotangent)
        cot_1 = cot_ring.step(*q_blocks)
        mixed_blocks = exchange(tie(mixed_sent, *cot_1))
        cot_2 = cot_ring.step(*mixed_blocks)
        out_parts = cores(out_near, *mixed_blocks[1:])
        hidden, normed_ffn, mixed = project_mixed(
            n, nd, info, layer_input, gains, mixed_blocks, out_parts
        )

        nf_ring = RingGather(net, normed_ffn)
        weights = (gate_weight, up_weight, down_weight)
        units = gate_weight.shape[0]
        made = {0: ffn_blocks([normed_ffn], [cotangent], weights)[0]}

        def ffn(*keys, deps=()):
            nf, cot = ([ring.got[k] for k in keys] for ring in (nf_ring, cot_ring))
            nf = tie(nf, *deps)
            made.update(zip(keys, ffn_blocks(nf, cot, weights)))

        fresh = nf_ring.step()
        query_near = chips(query_quarter, normed_ffn)
        cot_fresh, before = cot_2, (made[0][3],)
        for k in range(1, half_way):
            later = cot_ring.step(*fresh) if cot_ring.at < half_way else cot_fresh
            fresh = nf_ring.step(*cot_fresh, *before, *(query_near if k == half_way - 1 else ()))
            ffn(-k, k)
            before = (made[k][3], made[-k][3])
            cot_fresh = later
        query_parts = cores(query_near, *fresh)
        mixed_near = chips(mixed, *query_near)
        ffn("a", "b", deps=before)
        nf, cot = nf_ring.got, cot_ring.got

        def exchange_x(kept, *deps):
            sent = after(kept, *deps)
            return [net.swap(sent, "dp", r) for r in range(2, nd, 2)]

        grad_sum = RowSum(net, lambda key: made[key][3])
        arrived = grad_sum.step()
        kept, deps, swapped, mixed_parts = [], (), None, ()
        for k in range(3):
            upcoming = grad_sum.step(*deps, *((query_parts, mixed_near, mixed_parts)[k]))
            if k == 1:
                mixed_parts = cores(mixed_near, *arrived)
            lhs = tie([made[key][(1, 2, 0)[k]] for key in ring_order], *arrived)
            rhs = [(nf, nf, cot)[k][key] for key in ring_order]
            if swapped:
                kept.append(low(wide(mine_half) + wide(swapped[0])))
            deps = (*swapped,) if swapped else ()
            mine_half, sent_half = weight_gradient(info, lhs, rhs, units)
            swapped = (net.swap(sent_half, "dp", 1),)
            deps = (*deps, mine_half)
            last, arrived = arrived, upcoming
        top = units // 2
        others = [exchange_x(kept[0][:top], *last)]
        grad_sums = tie(grad_sum.rest(), *deps, *others[0])
        kept.append(low(wide(mine_half) + wide(swapped[0])))
        others.append(exchange_x(kept[0][top:], *grad_sums[1:]))

        def dp_cols(cols, *deps):
            sent = tie(cols, *deps)
            return [b if r == 0 else net.swap(b, "dp", r) for r, b in zip(dp_order, sent)]

        out_sum = RowSum(net, lambda key: made[key][4])
        out_1 = out_sum.step(*grad_sums[1:])
        gm_sent, branch_cols, grad_hidden, ffn_gain_part = branch_gradient(
            n, nd, info, hidden, gains, cotangent, grad_sums, out_parts
        )
        gm_blocks = exchange(tie(gm_sent, *out_1, *others[1]))
        branch_got = dp_cols(branch_cols, *gm_sent)
        gm_blocks = tie(gm_blocks, *branch_got)
        others.append(exchange_x(kept[1][:top], *gm_blocks))
        out_2 = out_sum.step(*gm_blocks)
        dq_sent, dkv_sent = attention_backward(
            heads_info, q_blocks, kv_blocks, gm_blocks, stats, ot
        )


        dq_sent = tie(dq_sent, *out_2, *others[2])
        others.append(exchange_x(kept[1][top:], *dq_sent))
        dq_blocks = tie(exchange(dq_sent), *others[3])

        def dp_total(k, *deps):
            total = chip_sum(tie([kept[k], *others[2 * k], *others[2 * k + 1]], *deps))
            return total, net.swap(total, "dp", 1)

        query_cols = sort_columns(n, nd, info, dq_blocks)

        query_got = dp_cols(query_cols)
        out_3 = out_sum.step(*query_cols)
        early = (n - 1) // 2
        dkv_early = [
            net.swap(b, "seq", r + 1) for r, b in enumerate(tie(dkv_sent[1 : early + 1], *query_cols))
        ]
        input_grad, attn_gain_part = input_gradient(
            nd, layer_input, gains, grad_hidden, query_cols, query_parts
        )
        out_4 = out_sum.step(attn_gain_part, *dkv_early)
        dkv_more = [
            net.swap(b, "seq", early + 1 + r)
            for r, b in enumerate(tie(dkv_sent[early + 1 :], *out_3, attn_gain_part))
        ]
        dkv_blocks = [dkv_sent[0], *dkv_early, *dkv_more]
        for rows in (slice(top), slice(top, units)):
            others.append(exchange_x(kept[2][rows], *query_got))
        gate_total = dp_total(0, *dq_blocks)
        up_total = dp_total(1, *query_cols)
        shares = projection_gradients(
            n,
            nd,
            info,
            mixed_parts,
            normed_all,
            attn_gain_part,
            ffn_gain_part,
            branch_got,
            query_got,
        )

        def share_of(key):
            if key in ("a", "b"):
                rows = shares[-1].shape[0] // 2
                return shares[-1][:rows] if key == "a" else shares[-1][rows:]
            return shares[ring_order.index(key)]

        share_sum = RowSum(net, share_of)
        shared = share_sum.step(*out_3, *dkv_early)
        gate_grad = spread_columns(info, *tie(gate_total, *shared))
        share_sum.step(*out_4, *dkv_more[: len(dkv_more) // 2])
        up_grad = spread_columns(info, *tie(up_total, *shared))
        for _ in range(half_way - 3):
            share_sum.step(gate_grad, *dkv_more)
        down_total = dp_total(2, *shared)
        share_sum.step(up_grad)
        down_grad = spread_columns(info, *down_total)
        key_grad, value_grad = split_keys_values(n, info, dkv_blocks)
        own, first, second = share_sum.rest()
        projections = low(own + wide(first) + wide(second))
        projections = after(projections, down_grad, key_grad)
        out_grad, query_grad, gain_sum = join_projections(
            nd, info, cores(chips(projections))
        )
        own, first, second = out_sum.rest()
        layer_output = low(hidden + (own + wide(first) + wide(second)))
        attn_count = attn_gain.shape[0]
        return (
            layer_output,
            input_grad,
            key_grad,
            value_grad,
            gain_sum[0, :attn_count],
            query_grad,
            out_grad,
            gain_sum[0, attn_count : 2 * attn_count],
            gate_grad,
            up_grad,
            down_grad,
        )

    return local


def solution(mesh):
    placed = (
        P(("dp", "seq"), None),
        P(("dp", "seq"), None),
        P(("dp", "seq"), None),
        P("dp"),
        P("seq"),
        P("seq", None),
        P("seq", None),
        P("seq"),
        P("seq", None),
        P("seq", None),
        P("seq", None),
        P(("dp", "seq"), None),
    )
    return jax.shard_map(
        make_local(mesh),
        mesh=mesh,
        in_specs=placed,
        out_specs=(
            P(("dp", "seq"), None),
            P(("dp", "seq"), None),
            P(("dp", "seq"), None),
            P(("dp", "seq"), None),
            P("seq"),
            P("seq", None),
            P("seq", None),
            P("seq"),
            P("seq", None),
            P("seq", None),
            P("seq", None),
        ),
        check_vma=False,
    )
```

```python
import functools

import jax
import jax.numpy as jnp
from jax import lax
from jax.experimental import pallas as pl
from jax.experimental.pallas import tpu as pltpu
from jax.sharding import PartitionSpec as P

HEAD_DIM = 128
ATT_BLOCK = 512


EPSILON = 1e-05


def product(left_side, right_side):
    return jnp.dot(left_side, right_side, preferred_element_type=jnp.float32)


def inner_rows(left_side, right_side):
    return lax.dot_general(
        left_side, right_side, (((0,), (0,)), ((), ())), preferred_element_type=jnp.float32
    )


def outer_cols(left_side, right_side):
    return lax.dot_general(
        left_side, right_side, (((1,), (1,)), ((), ())), preferred_element_type=jnp.float32
    )


def snake(count):
    deep = 4 if count % 4 == 0 else 1
    wide = count // deep
    if deep == 1 or wide == 1:
        return list(range(count))
    order = []
    for z in range(deep):
        across = range(1, wide) if z % 2 == 0 else range(wide - 1, 0, -1)
        order += [z * wide + y for y in across]
    return order + [z * wide for z in range(deep - 1, -1, -1)]


def after(value, *others):
    return lax.optimization_barrier((value, *others))[0] if others else value


def tie(values, *others):
    return list(lax.optimization_barrier((*values, *others))[: len(values)])


def low(value):
    return value.astype(jnp.bfloat16)


def wide(value):
    return value.astype(jnp.float32)


class Links:
    def __init__(self, mesh):
        self.n = mesh.shape["seq"]
        self.nd = mesh.shape["dp"]
        self.order = snake(self.n)
        n = self.n
        self.right = [(self.order[k], self.order[(k + 1) % n]) for k in range(n)]
        self.left = [(b, a) for a, b in self.right]

    def group(self, d):
        return d % 2 * (self.nd // 2) + d // 2

    def place(self):
        me = lax.axis_index("seq")
        table = [0] * self.n
        for k, i in enumerate(self.order):
            table[i] = k
        return sum(jnp.where(me == i, table[i], 0) for i in range(self.n))

    def owner(self, place, distance):
        spot = (place + distance) % self.n
        return sum(jnp.where(spot == k, self.order[k], 0) for k in range(self.n))

    def to_right(self, x):
        return lax.ppermute(x, "seq", self.right)

    def to_left(self, x):
        return lax.ppermute(x, "seq", self.left)

    def to_heads(self, x, m):
        per, nx = self.n // self.nd, self.nd // 2
        pairs = []
        for d in range(self.nd):
            for s in range(self.n):
                j = s ^ m
                group = j // per
                to = group % nx * 2 + group // nx
                pairs.append((d * self.n + s, to * self.n + self.group(d) * per + j % per))
        return lax.ppermute(x, ("dp", "seq"), pairs)

    def swap(self, x, axis, r):
        count = self.n if axis == "seq" else self.nd
        return lax.ppermute(x, axis, [(k, k ^ r) for k in range(count)])


class RingGather:
    def __init__(self, net, x):
        self.net, self.got, self.at = net, {0: x}, 0
        self.from_left = self.from_right = x

    def step(self, *deps):
        net, half = self.net, self.net.n // 2
        self.at += 1
        left, right = self.from_left, self.from_right
        if self.at == half:
            rows = left.shape[0] // 2
            left, right = left[:rows], right[rows:]
        if self.at == 1 and half > 1:
            left = right = after(left, *deps)
        else:
            left, right = tie([left, right], *deps)
        self.from_left, self.from_right = net.to_right(left), net.to_left(right)
        keys = ("a", "b") if self.at == half else (-self.at, self.at)
        self.got[keys[0]], self.got[keys[1]] = self.from_left, self.from_right
        return self.from_left, self.from_right

    def rest(self):
        while self.at < self.net.n // 2:
            self.step()
        return self.got


class RowSum:
    def __init__(self, net, part):
        self.net, self.part, self.at = net, part, net.n // 2
        self.going_left = self.going_right = None

    def step(self, *deps):
        net, half, s = self.net, self.net.n // 2, self.at
        if s == half:
            left, right = self.part("b"), self.part("a")
        else:
            left, right = self.part(-s), self.part(s)
            if s == half - 1:
                rows = left.shape[0] // 2
                left = jnp.concatenate([left[:rows], left[rows:] + wide(self.going_left)])
                right = jnp.concatenate([right[:rows] + wide(self.going_right), right[rows:]])
            else:
                left = left + wide(self.going_left)
                right = right + wide(self.going_right)
        left, right = tie([low(left), low(right)], *deps)
        self.going_left, self.going_right = net.to_left(left), net.to_right(right)
        self.at -= 1
        return self.going_left, self.going_right

    def rest(self):
        while self.at:
            self.step()
        return self.part(0), self.going_left, self.going_right


VMEM_LIMIT = 56 * 1024 * 1024
COST_SHARE = 4
ANYWHERE = pl.BlockSpec(memory_space=pl.ANY)
IN_VMEM = pl.BlockSpec(memory_space=pltpu.VMEM)
IN_SMEM = pl.BlockSpec(memory_space=pltpu.SMEM)
LOG2_E = 1.4426950408889634
DEAD = 1e30


def nt_dot(a, b):
    return lax.dot_general(a, b, (((1,), (1,)), ((), ())), preferred_element_type=jnp.float32)


def tn_dot(a, b):
    return lax.dot_general(a, b, (((0,), (0,)), ((), ())), preferred_element_type=jnp.float32)


def call(body, operands, specs, outs, out_specs, scratch, flops, moved, name):
    return pl.pallas_call(
        body,
        name=name,
        in_specs=specs,
        out_specs=tuple(out_specs),
        out_shape=tuple(jax.ShapeDtypeStruct(s, t) for s, t in outs),
        scratch_shapes=scratch,
        compiler_params=pltpu.CompilerParams(vmem_limit_bytes=VMEM_LIMIT),
        cost_estimate=pl.CostEstimate(
            flops=flops // COST_SHARE, bytes_accessed=moved // COST_SHARE, transcendentals=0
        ),
    )(*operands)


def aligned(index, unit):
    return pl.multiple_of(index * unit, unit)


def start_all(copies):
    for copy in copies:
        copy.start()
    return copies


def wait_all(copies):
    for copy in copies:
        copy.wait()


def causal_mask(block):
    key_at = lax.broadcasted_iota(jnp.int32, (block, block), 0)
    query_at = lax.broadcasted_iota(jnp.int32, (block, block), 1)
    return key_at <= query_at


def forward_body(n, info, *refs):
    q_in, kv_in = refs[:n], refs[n : 2 * n]
    outs, stats, ot = refs[2 * n : 3 * n], refs[3 * n], refs[3 * n + 1]
    qs, ks, vs, vt, mixed, sems = refs[3 * n + 2 :]
    me, length, spot = info[0], info[1], info[2]
    count, width = q_in[0].shape
    heads = width // HEAD_DIM
    total = n * count
    blocks = total // ATT_BLOCK
    copies = []
    for r in range(n):
        rows = pl.ds(aligned(me ^ r, count), count)
        query_rows = pl.ds(aligned(spot ^ r, count), count)
        for k, (src, dst) in enumerate(
            (
                (kv_in[r].at[:, pl.ds(0, width)], ks.at[rows]),
                (kv_in[r].at[:, pl.ds(width, width)], vs.at[rows]),
                (q_in[r], qs.at[query_rows]),
            )
        ):
            copies.append(pltpu.make_async_copy(src, dst, sems.at[3 * r + k]))
    wait_all(start_all(copies))
    factor = HEAD_DIM ** (-0.5) * LOG2_E

    def transpose_values(b, _):
        at = pl.ds(pl.multiple_of(b * ATT_BLOCK, ATT_BLOCK), ATT_BLOCK)
        vt[:, at] = vs[at, :].T
        return 0

    lax.fori_loop(0, blocks, transpose_values, 0)
    live = jnp.minimum((length + ATT_BLOCK - 1) // ATT_BLOCK, blocks)

    def tile(qi, kj, state, masked):
        new = []
        q_at = pl.ds(pl.multiple_of(qi * ATT_BLOCK, ATT_BLOCK), ATT_BLOCK)
        k_at = pl.ds(pl.multiple_of(kj * ATT_BLOCK, ATT_BLOCK), ATT_BLOCK)
        for h in range(heads):
            cols = slice(h * HEAD_DIM, (h + 1) * HEAD_DIM)
            top, total_sum, acc = state[h]
            scores = nt_dot(ks[k_at, cols], qs[q_at, cols]) * factor
            if masked:
                scores = jnp.where(causal_mask(ATT_BLOCK), scores, -DEAD)
            higher = jnp.maximum(top, jnp.max(scores, axis=0, keepdims=True))
            weights = jnp.exp2(scores - higher)
            shrink = jnp.exp2(top - higher)
            total_sum = total_sum * shrink + jnp.sum(weights, axis=0, keepdims=True)
            acc = acc * shrink + jnp.dot(
                vt[cols, k_at], weights.astype(jnp.bfloat16), preferred_element_type=jnp.float32
            )
            new.append((higher, total_sum, acc))
        return tuple(new)

    stats[...] = jnp.full(stats.shape, DEAD, jnp.float32)

    def query_block(qi, _):
        first = tuple(
            (
                jnp.full((1, ATT_BLOCK), -DEAD, jnp.float32),
                jnp.zeros((1, ATT_BLOCK), jnp.float32),
                jnp.zeros((HEAD_DIM, ATT_BLOCK), jnp.float32),
            )
            for _ in range(heads)
        )
        state = lax.fori_loop(0, qi, lambda kj, s: tile(qi, kj, s, False), first)
        state = tile(qi, qi, state, True)
        q_at = pl.ds(pl.multiple_of(qi * ATT_BLOCK, ATT_BLOCK), ATT_BLOCK)
        query_at = qi * ATT_BLOCK + lax.broadcasted_iota(jnp.int32, (1, ATT_BLOCK), 1)
        alive = query_at < length
        for h in range(heads):
            cols = slice(h * HEAD_DIM, (h + 1) * HEAD_DIM)
            top, total_sum, acc = state[h]
            scaled = acc * jnp.where(alive, 1.0 / total_sum, 0.0)
            ot[cols, q_at] = scaled
            mixed[q_at, cols] = scaled.T.astype(jnp.bfloat16)
            stats[h : h + 1, q_at] = jnp.where(alive, top + jnp.log2(total_sum), DEAD)
        return 0

    lax.fori_loop(0, live, query_block, 0)

    def dead_block(qi, _):
        q_at = pl.ds(pl.multiple_of(qi * ATT_BLOCK, ATT_BLOCK), ATT_BLOCK)
        mixed[q_at, :] = jnp.zeros((ATT_BLOCK, width), jnp.bfloat16)
        ot[:, q_at] = jnp.zeros((width, ATT_BLOCK), jnp.float32)
        return 0

    lax.fori_loop(live, blocks, dead_block, 0)
    copies = []
    for r in range(n):
        rows = pl.ds(pl.multiple_of((me ^ r) * count, count), count)
        copies.append(pltpu.make_async_copy(mixed.at[rows], outs[r], sems.at[r]))
    wait_all(start_all(copies))


def attention_forward(info, q_blocks, kv_blocks):
    n = len(q_blocks)
    count, width = q_blocks[0].shape
    total = n * count
    got = call(
        functools.partial(forward_body, n),
        [info, *q_blocks, *kv_blocks],
        [IN_SMEM] + [ANYWHERE] * (2 * n),
        [((count, width), jnp.bfloat16)] * n
        + [((8, total), jnp.float32), ((width, total), jnp.float32)],
        [ANYWHERE] * n + [IN_VMEM] * 2,
        [pltpu.VMEM((total, width), jnp.bfloat16)] * 3
        + [pltpu.VMEM((width, total), jnp.bfloat16), pltpu.VMEM((total, width), jnp.bfloat16)]
        + [pltpu.SemaphoreType.DMA((3 * n,))],
        16 * 2 * total * total * width // 2,
        10 * total * width,
        "attention_forward",
    )
    return got[:n], got[n], got[n + 1]


def backward_body(n, info, *refs):
    q_in, kv_in, g_in = refs[:n], refs[n : 2 * n], refs[2 * n : 3 * n]
    stats, ot = refs[3 * n], refs[3 * n + 1]
    refs = refs[3 * n + 2 :]
    dq_out, dkv_out = refs[:n], refs[n : 2 * n]
    qs, ks, vs, gs, kt, delta, dqt, dk, dv, dq_low, dkv_low, sems = refs[2 * n :]
    me, length, spot = info[0], info[1], info[2]
    count, width = q_in[0].shape
    heads = width // HEAD_DIM
    total = n * count
    blocks = total // ATT_BLOCK
    copies = []
    for r in range(n):
        rows = pl.ds(aligned(me ^ r, count), count)
        query_rows = pl.ds(aligned(spot ^ r, count), count)
        for k, (src, dst) in enumerate(
            (
                (kv_in[r].at[:, pl.ds(0, width)], ks.at[rows]),
                (kv_in[r].at[:, pl.ds(width, width)], vs.at[rows]),
                (q_in[r], qs.at[query_rows]),
                (g_in[r], gs.at[rows]),
            )
        ):
            copies.append(pltpu.make_async_copy(src, dst, sems.at[4 * r + k]))
    start_all(copies)
    live = jnp.minimum((length + ATT_BLOCK - 1) // ATT_BLOCK, blocks)
    scale = HEAD_DIM ** (-0.5)
    factor = scale * LOG2_E

    def clear(b, _):
        at = pl.ds(pl.multiple_of(b * ATT_BLOCK, ATT_BLOCK), ATT_BLOCK)
        dqt[:, at] = jnp.zeros((width, ATT_BLOCK), jnp.float32)
        dk[at, :] = jnp.zeros((ATT_BLOCK, width), jnp.float32)
        dv[at, :] = jnp.zeros((ATT_BLOCK, width), jnp.float32)
        return 0

    lax.fori_loop(0, blocks, clear, 0)
    wait_all(copies)

    def prepare(b, _):
        at = pl.ds(pl.multiple_of(b * ATT_BLOCK, ATT_BLOCK), ATT_BLOCK)
        kt[:, at] = ks[at, :].T
        both = gs[at, :].astype(jnp.float32).T * ot[:, at]
        for h in range(heads):
            cols = slice(h * HEAD_DIM, (h + 1) * HEAD_DIM)
            delta[h : h + 1, at] = jnp.sum(both[cols], axis=0, keepdims=True)
        return 0

    lax.fori_loop(0, blocks, prepare, 0)

    def tile(qi, kj, masked):
        q_at = pl.ds(pl.multiple_of(qi * ATT_BLOCK, ATT_BLOCK), ATT_BLOCK)
        k_at = pl.ds(pl.multiple_of(kj * ATT_BLOCK, ATT_BLOCK), ATT_BLOCK)
        for h in range(heads):
            cols = slice(h * HEAD_DIM, (h + 1) * HEAD_DIM)
            q, g = qs[q_at, cols], gs[q_at, cols]
            scores = nt_dot(ks[k_at, cols], q) * factor - stats[h : h + 1, q_at]
            if masked:
                scores = jnp.where(causal_mask(ATT_BLOCK), scores, -DEAD)
            weights = jnp.exp2(scores)
            grad_weights = nt_dot(vs[k_at, cols], g)
            grad_scores = (weights * (grad_weights - delta[h : h + 1, q_at])).astype(jnp.bfloat16)
            dv[k_at, cols] += jnp.dot(
                weights.astype(jnp.bfloat16), g, preferred_element_type=jnp.float32
            )
            dk[k_at, cols] += jnp.dot(grad_scores, q, preferred_element_type=jnp.float32)
            dqt[cols, q_at] += jnp.dot(
                kt[cols, k_at], grad_scores, preferred_element_type=jnp.float32
            )

    def query_block(qi, _):
        def step(kj, _):
            tile(qi, kj, False)
            return 0

        lax.fori_loop(0, qi, step, 0)
        tile(qi, qi, True)
        return 0

    lax.fori_loop(0, live, query_block, 0)

    def finish(b, _):
        at = pl.ds(pl.multiple_of(b * ATT_BLOCK, ATT_BLOCK), ATT_BLOCK)
        dq_low[at, :] = (dqt[:, at] * scale).T.astype(jnp.bfloat16)
        dkv_low[at, :width] = (dk[at, :] * scale).astype(jnp.bfloat16)
        dkv_low[at, width:] = dv[at, :].astype(jnp.bfloat16)
        return 0

    lax.fori_loop(0, blocks, finish, 0)
    copies = []
    for r in range(n):
        rows = pl.ds(pl.multiple_of((me ^ r) * count, count), count)
        copies.append(pltpu.make_async_copy(dq_low.at[rows], dq_out[r], sems.at[2 * r]))
        copies.append(pltpu.make_async_copy(dkv_low.at[rows], dkv_out[r], sems.at[2 * r + 1]))
    wait_all(start_all(copies))


def attention_backward(info, q_blocks, kv_blocks, g_blocks, stats, ot):
    n = len(q_blocks)
    count, width = q_blocks[0].shape
    total = n * count
    low_all = pltpu.VMEM((total, width), jnp.bfloat16)
    got = call(
        functools.partial(backward_body, n),
        [info, *q_blocks, *kv_blocks, *g_blocks, stats, ot],
        [IN_SMEM] + [ANYWHERE] * (3 * n) + [IN_VMEM] * 2,
        [((count, width), jnp.bfloat16)] * n + [((count, 2 * width), jnp.bfloat16)] * n,
        [ANYWHERE] * (2 * n),
        [low_all] * 4
        + [
            pltpu.VMEM((width, total), jnp.bfloat16),
            pltpu.VMEM((8, total), jnp.float32),
            pltpu.VMEM((width, total), jnp.float32),
            pltpu.VMEM((total, width), jnp.float32),
            pltpu.VMEM((total, width), jnp.float32),
            low_all,
            pltpu.VMEM((total, 2 * width), jnp.bfloat16),
            pltpu.SemaphoreType.DMA((4 * n,)),
        ],
        40 * 2 * total * total * width // 2,
        20 * total * width,
        "attention_backward",
    )
    return got[:n], got[n:]


def pack_body(n, info, keys, values, *refs):
    outs, sems = refs[:n], refs[n]
    me = info[0]
    width = outs[0].shape[1] // 2
    copies = []
    for r in range(n):
        cols = pl.ds(aligned(me ^ r, width), width)
        copies.append(
            pltpu.make_async_copy(keys.at[:, cols], outs[r].at[:, pl.ds(0, width)], sems.at[2 * r])
        )
        copies.append(
            pltpu.make_async_copy(
                values.at[:, cols], outs[r].at[:, pl.ds(width, width)], sems.at[2 * r + 1]
            )
        )
    wait_all(start_all(copies))


def pack_keys_values(n, info, keys, values):
    count, depth = keys.shape
    return call(
        functools.partial(pack_body, n),
        [info, keys, values],
        [IN_SMEM, ANYWHERE, ANYWHERE],
        [((count, 2 * depth // n), jnp.bfloat16)] * n,
        [IN_VMEM] * n,
        [pltpu.SemaphoreType.DMA((2 * n,))],
        0,
        8 * count * depth,
        "pack_keys_values",
    )


GAIN_ROWS = 32


def norm_parts(v):
    return lax.rsqrt(jnp.mean(v * v, axis=-1, keepdims=True) + EPSILON)


def query_body(n, nd, info, *refs):
    xs, pieces = refs[:nd], refs[nd : nd + n + 1]
    q_out = refs[nd + n + 1 : nd + 2 * n + 1]
    normed, gains, weight, out_weight = refs[nd + 2 * n + 1 : nd + 2 * n + 5]
    queries, gain_rows, sems = refs[nd + 2 * n + 5 :]
    me, dp = info[0], info[1]
    count, depth = xs[0].shape
    wrows = (pieces[0].shape[0] - GAIN_ROWS) // 2
    cut = wrows - GAIN_ROWS // 2
    copies, later = [], []

    def fetch(into, k, src, dst, j):
        into.append(pltpu.make_async_copy(src, dst, sems.at[3 * k + j]))

    for k in range(n):
        first = info[3 + k] * wrows
        gain_at = gain_rows.at[pl.ds(aligned(info[3 + k], 16), 16)]
        fetch(copies, k, pieces[k].at[pl.ds(0, 16)], gain_at, 0)
        at = pl.multiple_of(first, 16)
        if k < n - 1:
            rows = pl.ds(at, wrows)
            fetch(copies, k, pieces[k].at[pl.ds(GAIN_ROWS, wrows)], weight.at[rows], 1)
            fetch(later, k, pieces[k].at[pl.ds(GAIN_ROWS + wrows, wrows)], out_weight.at[rows], 2)
        else:
            below = pl.multiple_of(first + cut, 16)
            fetch(copies, k, pieces[k].at[pl.ds(GAIN_ROWS, cut)], weight.at[pl.ds(at, cut)], 1)
            rest = pl.ds(below, wrows - cut)
            fetch(copies, k, pieces[n].at[pl.ds(0, wrows - cut)], weight.at[rest], 2)
            tail = pieces[n].at[pl.ds(wrows - cut, wrows)]
            fetch(later, n, tail, out_weight.at[pl.ds(at, wrows)], 0)
    start_all(copies)
    start_all(later)
    wait_all(copies)
    share = depth // n
    for o in range(n):
        row = gain_rows[o * 16 : o * 16 + 16, : 2 * share].astype(jnp.float32)
        gains[0:1, o * share : (o + 1) * share] = row[0:1, :share]
        gains[1:2, o * share : (o + 1) * share] = row[0:1, share:]
    for k in range(nd):
        v = xs[k][...].astype(jnp.float32)
        rows = slice(k * count, (k + 1) * count)
        normed[rows, :] = (v * norm_parts(v) * gains[0:1, :]).astype(jnp.bfloat16)
        queries[rows, :] = jnp.dot(
            normed[rows, :], weight[...], preferred_element_type=jnp.float32
        ).astype(jnp.bfloat16)
    per = n // nd
    copies = []
    for m in range(n):
        j = me ^ m
        slot = dp ^ (j // per)
        copies.append(
            pltpu.make_async_copy(
                queries.at[
                    pl.ds(aligned(slot, count), count), pl.ds(aligned(j % per, share), share)
                ],
                q_out[m],
                sems.at[3 * n + 3 + m],
            )
        )
    wait_all(start_all(copies))
    wait_all(later)


def project_queries(n, nd, info, xs, pieces):
    count, depth = xs[0].shape
    quarter = pieces[0].shape[1]
    got = call(
        functools.partial(query_body, n, nd),
        [info, *xs, *pieces],
        [IN_SMEM] + [IN_VMEM] * nd + [ANYWHERE] * (n + 1),
        [((count, depth // n), jnp.bfloat16)] * n
        + [
            ((nd * count, depth), jnp.bfloat16),
            ((8, depth), jnp.float32),
            ((depth, quarter), jnp.bfloat16),
            ((depth, quarter), jnp.bfloat16),
        ],
        [ANYWHERE] * n + [IN_VMEM] * 4,
        [
            pltpu.VMEM((nd * count, quarter), jnp.bfloat16),
            pltpu.VMEM((n * 16, quarter), jnp.bfloat16),
            pltpu.SemaphoreType.DMA((4 * n + 3,)),
        ],
        2 * count * depth * depth,
        6 * depth * depth,
        "project_queries",
    )
    return got[:n], *got[n:]


def padded(width):
    return (width + 127) // 128 * 128


def ffn_body(m, *refs):
    nf_in, cot_in, weights_in = refs[:m], refs[m : 2 * m], refs[2 * m : 2 * m + 3]
    outs = refs[2 * m + 3 : 7 * m + 3]
    nf, cot, gate_w, up_w, down_w, acts, shares, sems, out_sems = refs[7 * m + 3 :]
    weights = (gate_w, up_w, down_w)
    rows = nf_in[0].shape[0]
    hidden_units = gate_w.shape[0]

    def load(src, dst, k):
        return pltpu.make_async_copy(src, dst, sems.at[k])

    at = [pl.ds(b * rows, rows) for b in range(m)]
    loads = [load(weights_in[k], weights[k], k) for k in range(3)]
    nf_loads = [load(nf_in[b], nf.at[at[b]], 3 + b) for b in range(m)]
    cot_loads = [load(cot_in[b], cot.at[at[b]], 3 + m + b) for b in range(m)]
    start_all([*nf_loads, loads[0], loads[1], *cot_loads, loads[2]])
    copies = []

    def store(k, src):
        for b in range(m):
            copy = pltpu.make_async_copy(
                src.at[at[b]], outs[5 * b + k], out_sems.at[5 * b + k]
            )
            copy.start()
            copies.append(copy)

    wait_all(nf_loads)
    loads[0].wait()
    gate_value = nt_dot(nf[...], gate_w[...])
    loads[1].wait()
    up_value = nt_dot(nf[...], up_w[...])
    wait_all(cot_loads)
    loads[2].wait()
    grad_inner = nt_dot(cot[...], down_w[...])
    sigmoid = 1.0 / (1.0 + jnp.exp(-gate_value))
    act = gate_value * sigmoid
    inner = (act * up_value).astype(jnp.bfloat16)
    grad_gate = (
        grad_inner * up_value * sigmoid * (1.0 + gate_value * (1.0 - sigmoid))
    ).astype(jnp.bfloat16)
    grad_up = (grad_inner * act).astype(jnp.bfloat16)
    for k, value in enumerate((inner, grad_gate, grad_up)):
        acts[k, :, :hidden_units] = value
        store(k, acts.at[k])
    shares[0] = jnp.dot(grad_gate, gate_w[...], preferred_element_type=jnp.float32) + jnp.dot(
        grad_up, up_w[...], preferred_element_type=jnp.float32
    )
    store(3, shares.at[0])
    shares[1] = jnp.dot(inner, down_w[...], preferred_element_type=jnp.float32)
    store(4, shares.at[1])
    wait_all(copies)


def ffn_blocks(nf, cot, weights):
    m = len(nf)
    rows, depth = nf[0].shape
    units = weights[0].shape[0]
    act = ((rows, padded(units)), jnp.bfloat16)
    share = ((rows, depth), jnp.float32)
    got = call(
        functools.partial(ffn_body, m),
        [*nf, *cot, *weights],
        [ANYWHERE] * (2 * m + 3),
        [act, act, act, share, share] * m,
        [ANYWHERE] * (5 * m),
        [pltpu.VMEM((m * rows, depth), jnp.bfloat16)] * 2
        + [pltpu.VMEM((units, depth), jnp.bfloat16)] * 3
        + [
            pltpu.VMEM((3, m * rows, padded(units)), jnp.bfloat16),
            pltpu.VMEM((2, m * rows, depth), jnp.float32),
            pltpu.SemaphoreType.DMA((3 + 2 * m,)),
            pltpu.SemaphoreType.DMA((5 * m,)),
        ],
        12 * m * rows * units * depth,
        6 * units * depth + 12 * m * rows * depth,
        "ffn_blocks",
    )
    return [got[5 * b : 5 * b + 5] for b in range(m)]


def weight_gradient_body(count, units, info, *refs):
    lhs_in, rhs_in = refs[:count], refs[count : 2 * count]
    kept, sent, lhs, turned, rhs, sems = refs[2 * count :]
    core = info[2]
    copies, first = [], 0
    for k in range(count):
        rows = lhs_in[k].shape[0]
        at = pl.ds(first, rows)
        copies.append(pltpu.make_async_copy(lhs_in[k], lhs.at[at], sems.at[2 * k]))
        copies.append(pltpu.make_async_copy(rhs_in[k], rhs.at[at], sems.at[2 * k + 1]))
        first += rows
    start_all(copies)
    wait_all(copies[::2])
    block = 256

    def turn(b, _):
        at = pl.ds(aligned(b, block), block)
        turned[:, at] = lhs[at, :].T
        return 0

    lax.fori_loop(0, first // block, turn, 0)
    wait_all(copies[1::2])
    half = kept.shape[1]
    piece = 256

    def step(c, _):
        to = pl.ds(aligned(c, piece), piece)
        for out, side in ((kept, core), (sent, 1 - core)):
            cols = pl.ds(pl.multiple_of(side * half + c * piece, piece), piece)
            out[:, to] = jnp.dot(
                turned[...], rhs[:, cols], preferred_element_type=jnp.float32
            )[:units].astype(jnp.bfloat16)
        return 0

    lax.fori_loop(0, half // piece, step, 0)


def weight_gradient(info, lhs, rhs, units):
    count = len(lhs)
    rows = sum(b.shape[0] for b in rhs)
    width, depth = lhs[0].shape[1], rhs[0].shape[1]
    return call(
        functools.partial(weight_gradient_body, count, units),
        [info, *lhs, *rhs],
        [IN_SMEM] + [ANYWHERE] * (2 * count),
        [((units, depth // 2), jnp.bfloat16)] * 2,
        [IN_VMEM] * 2,
        [
            pltpu.VMEM((rows, width), jnp.bfloat16),
            pltpu.VMEM((width, rows), jnp.bfloat16),
            pltpu.VMEM((rows, depth), jnp.bfloat16),
            pltpu.SemaphoreType.DMA((2 * count,)),
        ],
        2 * rows * units * depth,
        2 * rows * depth,
        "weight_gradient",
    )


def hidden_body(n, nd, info, x, gains, *refs):
    blocks, parts = refs[:n], refs[n : n + nd]
    hidden, normed, mixed = refs[n + nd : n + nd + 3]
    weight, sems = refs[n + nd + 3 :]
    me, dp = info[0], info[1]
    share, quarter = blocks[0].shape[1], parts[0].shape[1]
    copies = []
    for r in range(nd):
        cols = pl.ds(aligned(dp ^ r, quarter), quarter)
        copies.append(pltpu.make_async_copy(parts[r], weight.at[:, cols], sems.at[r]))
    for r in range(n):
        cols = pl.ds(aligned(me ^ r, share), share)
        copies.append(pltpu.make_async_copy(blocks[r], mixed.at[:, cols], sems.at[nd + r]))
    start_all(copies[nd:] + copies[:nd])
    wait_all(copies[nd:])
    depth = x.shape[1]
    total = jnp.zeros((x.shape[0], 1), jnp.float32)
    for r in range(nd):
        copies[r].wait()
        cols = pl.ds(aligned(dp ^ r, quarter), quarter)
        v = x[:, cols].astype(jnp.float32) + jnp.dot(
            mixed[...], weight[:, cols], preferred_element_type=jnp.float32
        )
        hidden[:, cols] = v
        total = total + jnp.sum(v * v, axis=-1, keepdims=True)
    normed[...] = (
        hidden[...] * lax.rsqrt(total / depth + EPSILON) * gains[1:2, :]
    ).astype(jnp.bfloat16)


def project_mixed(n, nd, info, x, gains, blocks, parts):
    count, depth = x.shape
    return call(
        functools.partial(hidden_body, n, nd),
        [info, x, gains, *blocks, *parts],
        [IN_SMEM, IN_VMEM, IN_VMEM] + [ANYWHERE] * (n + nd),
        [
            ((count, depth), jnp.float32),
            ((count, depth), jnp.bfloat16),
            ((count, depth), jnp.bfloat16),
        ],
        [IN_VMEM] * 3,
        [pltpu.VMEM((depth, depth), jnp.bfloat16), pltpu.SemaphoreType.DMA((n + nd,))],
        2 * count * depth * depth,
        6 * depth * depth,
        "project_mixed",
    )


def norm_grad(v, gain, upstream):
    scale = norm_parts(v)
    weighted = upstream * gain
    through = weighted * scale - v * (scale**3) * jnp.mean(weighted * v, axis=-1, keepdims=True)
    return through, jnp.sum(upstream * v * scale, axis=0, keepdims=True)


def branch_body(n, nd, info, hidden, gains, cotangent, own, first, second, *refs):
    parts, refs = refs[:nd], refs[nd:]
    gm_out, cols_out = refs[:n], refs[n : n + nd]
    grad_hidden, gain_part, branch, weight, sems = refs[n + nd :]
    me, dp = info[0], info[1]
    quarter = parts[0].shape[1]
    copies = []
    for r in range(nd):
        cols = pl.ds(aligned(dp ^ r, quarter), quarter)
        copies.append(pltpu.make_async_copy(parts[r], weight.at[:, cols], sems.at[r]))
    start_all(copies)
    upstream = own[...] + first[...].astype(jnp.float32) + second[...].astype(jnp.float32)
    through, gain = norm_grad(hidden[...], gains[1:2, :], upstream)
    gain_part[...] = jnp.broadcast_to(gain, gain_part.shape)
    total = cotangent[...].astype(jnp.float32) + through
    grad_hidden[...] = total
    branch[...] = total.astype(jnp.bfloat16)
    for r in range(nd):
        cols_out[r][...] = branch[:, pl.ds(aligned(dp ^ r, quarter), quarter)]
    wait_all(copies)
    share = gm_out[0].shape[1]
    for r in range(n):
        rows = pl.ds(aligned(me ^ r, share), share)
        gm_out[r][...] = nt_dot(branch[...], weight[rows, :]).astype(jnp.bfloat16)


def branch_gradient(n, nd, info, hidden, gains, cotangent, sums, parts):
    count, depth = cotangent.shape
    got = call(
        functools.partial(branch_body, n, nd),
        [info, hidden, gains, cotangent, *sums, *parts],
        [IN_SMEM] + [IN_VMEM] * 6 + [ANYWHERE] * nd,
        [((count, depth // n), jnp.bfloat16)] * n
        + [((count, depth // nd), jnp.bfloat16)] * nd
        + [((count, depth), jnp.float32), ((8, depth), jnp.float32)],
        [IN_VMEM] * (n + nd + 2),
        [
            pltpu.VMEM((count, depth), jnp.bfloat16),
            pltpu.VMEM((depth, depth), jnp.bfloat16),
            pltpu.SemaphoreType.DMA((nd,)),
        ],
        2 * count * depth * depth,
        6 * depth * depth,
        "branch_gradient",
    )
    return got[:n], got[n : n + nd], got[n + nd], got[n + nd + 1]


def sort_body(n, nd, info, *refs):
    blocks, cols_out = refs[:n], refs[n : n + nd]
    rows, sems = refs[n + nd :]
    me, dp = info[0], info[1]
    share, quarter = blocks[0].shape[1], cols_out[0].shape[1]
    copies = []
    for r in range(n):
        cols = pl.ds(aligned(me ^ r, share), share)
        copies.append(pltpu.make_async_copy(blocks[r], rows.at[:, cols], sems.at[r]))
    wait_all(start_all(copies))
    copies = []
    for r in range(nd):
        cols = pl.ds(aligned(dp ^ r, quarter), quarter)
        copies.append(pltpu.make_async_copy(rows.at[:, cols], cols_out[r], sems.at[r]))
    wait_all(start_all(copies))


def sort_columns(n, nd, info, blocks):
    count, share = blocks[0].shape
    depth = n * share
    return call(
        functools.partial(sort_body, n, nd),
        [info, *blocks],
        [IN_SMEM] + [ANYWHERE] * n,
        [((count, depth // nd), jnp.bfloat16)] * nd,
        [ANYWHERE] * nd,
        [pltpu.VMEM((count, depth), jnp.bfloat16), pltpu.SemaphoreType.DMA((max(n, nd),))],
        0,
        6 * count * depth,
        "sort_columns",
    )


def split_body(n, info, *refs):
    blocks, keys, values, sems = refs[:n], refs[n], refs[n + 1], refs[n + 2]
    me = info[0]
    share = blocks[0].shape[1] // 2
    copies = []
    for r in range(n):
        cols = pl.ds(aligned(me ^ r, share), share)
        copies.append(
            pltpu.make_async_copy(blocks[r].at[:, pl.ds(0, share)], keys.at[:, cols], sems.at[2 * r])
        )
        copies.append(
            pltpu.make_async_copy(
                blocks[r].at[:, pl.ds(share, share)], values.at[:, cols], sems.at[2 * r + 1]
            )
        )
    wait_all(start_all(copies))


def split_keys_values(n, info, blocks):
    count, share = blocks[0].shape
    depth = n * share // 2
    return call(
        functools.partial(split_body, n),
        [info, *blocks],
        [IN_SMEM] + [ANYWHERE] * n,
        [((count, depth), jnp.bfloat16)] * 2,
        [IN_VMEM] * 2,
        [pltpu.SemaphoreType.DMA((2 * n,))],
        0,
        8 * count * depth,
        "split_keys_values",
    )


def input_body(nd, x, gains, grad_hidden, *refs):
    cols, parts = refs[:nd], refs[nd : 2 * nd]
    out, gain_part, upstream = refs[2 * nd :]
    piece = 512

    def step(c, _):
        rows = pl.ds(aligned(c, piece), piece)
        upstream[:, rows] = sum(nt_dot(cols[r][...], parts[r][rows, :]) for r in range(nd))
        return 0

    lax.fori_loop(0, x.shape[1] // piece, step, 0)
    through, gain = norm_grad(x[...].astype(jnp.float32), gains[0:1, :], upstream[...])
    gain_part[...] = jnp.broadcast_to(gain, gain_part.shape)
    out[...] = (grad_hidden[...] + through).astype(jnp.bfloat16)


def input_gradient(nd, x, gains, grad_hidden, cols, parts):
    count, depth = x.shape
    return call(
        functools.partial(input_body, nd),
        [x, gains, grad_hidden, *cols, *parts],
        [IN_VMEM] * (3 + 2 * nd),
        [((count, depth), jnp.bfloat16), ((8, depth), jnp.float32)],
        [IN_VMEM] * 2,
        [pltpu.VMEM((count, depth), jnp.float32)],
        2 * count * depth * depth,
        6 * depth * depth,
        "input_gradient",
    )


def projections_body(n, nd, info, normed, attn_part, ffn_part, *refs):
    branch_cols, query_cols, mixed_in = refs[:nd], refs[nd : 2 * nd], refs[2 * nd : 3 * nd]
    outs = refs[3 * nd : 3 * nd + n]
    branch, query, mixed = refs[3 * nd + n :]
    count = branch_cols[0].shape[0]
    share = mixed.shape[1] // n
    for k in range(nd):
        rows = slice(k * count, (k + 1) * count)
        mixed[rows, :] = mixed_in[k][...]
        branch[rows, :] = branch_cols[k][...]
        query[rows, :] = query_cols[k][...]
    for k in range(n):
        cols = pl.ds(aligned(info[3 + k], share), share)
        outs[k][:share, :] = tn_dot(mixed[:, cols], branch[...])
        outs[k][share : 2 * share, :] = tn_dot(normed[:, cols], query[...])
        outs[k][2 * share :, :] = jnp.zeros((GAIN_ROWS, branch.shape[1]), jnp.float32)
        outs[k][2 * share : 2 * share + 8, :share] = attn_part[:, cols]
        outs[k][2 * share : 2 * share + 8, share : 2 * share] = ffn_part[:, cols]


def projection_gradients(n, nd, info, mixed, normed, attn_part, ffn_part, branch_cols, query_cols):
    rows, depth = normed.shape
    count, quarter = branch_cols[0].shape
    return call(
        functools.partial(projections_body, n, nd),
        [info, normed, attn_part, ffn_part, *branch_cols, *query_cols, *mixed],
        [IN_SMEM] + [IN_VMEM] * (3 + 3 * nd),
        [((2 * depth // n + GAIN_ROWS, quarter), jnp.float32)] * n,
        [IN_VMEM] * n,
        [pltpu.VMEM((rows, quarter), jnp.bfloat16)] * 2
        + [pltpu.VMEM((rows, depth), jnp.bfloat16)],
        4 * rows * depth * quarter,
        4 * rows * depth,
        "projection_gradients",
    )


def join_body(nd, info, *refs):
    parts, (out_grad, query_grad, gain_sum) = refs[:nd], refs[nd:]
    share = out_grad.shape[0]
    quarter = parts[0].shape[1]
    dp = info[1]
    for r in range(nd):
        cols = pl.ds(aligned(dp ^ r, quarter), quarter)
        part = parts[r][...].astype(jnp.float32)
        out_grad[:, cols] = part[:share]
        query_grad[:, cols] = part[share : 2 * share]
    tops = [parts[r][2 * share : 2 * share + 16, :].astype(jnp.float32)[:8] for r in range(nd)]
    gain_sum[...] = tree_sum(tops)


def join_projections(nd, info, parts):
    rows, quarter = parts[0].shape
    share, depth = (rows - GAIN_ROWS) // 2, quarter * nd
    return call(
        functools.partial(join_body, nd),
        [info, *parts],
        [IN_SMEM] + [IN_VMEM] * nd,
        [((share, depth), jnp.float32)] * 2 + [((8, quarter), jnp.float32)],
        [IN_VMEM] * 3,
        [],
        0,
        10 * share * depth,
        "join_projections",
    )


def chip_sum_body(kept, *refs):
    others, out = refs[:-1], refs[-1]
    half = len(others) // 2
    top = others[0].shape[0]
    for side, first in ((others[:half], 0), (others[half:], top)):
        rows = slice(first, first + side[0].shape[0])
        terms = [kept[rows, :].astype(jnp.float32)] + [v[...].astype(jnp.float32) for v in side]
        out[rows, :] = tree_sum(terms).astype(jnp.bfloat16)


def chip_sum(operands):
    shape = operands[0].shape
    return call(
        chip_sum_body,
        operands,
        [IN_VMEM] * len(operands),
        [(shape, jnp.bfloat16)],
        [IN_VMEM],
        [],
        0,
        6 * shape[0] * shape[1],
        "chip_sum",
    )[0]


def spread_body(info, mine, other, out):
    half = mine.shape[1]
    for ref, side in ((mine, info[2]), (other, 1 - info[2])):
        out[:, pl.ds(aligned(side, half), half)] = ref[...].astype(jnp.float32)


def spread_columns(info, mine, other):
    rows, half = mine.shape
    return call(
        spread_body,
        [info, mine, other],
        [IN_SMEM, IN_VMEM, IN_VMEM],
        [((rows, 2 * half), jnp.float32)],
        [IN_VMEM],
        [],
        0,
        12 * rows * half,
        "spread_columns",
    )[0]


def tree_sum(parts):
    while len(parts) > 1:
        parts = [parts[k] + parts[k + 1] for k in range(0, len(parts), 2)]
    return parts[0]


def columns(x, start, width):
    return lax.dynamic_slice_in_dim(x, start, width, 1)


def make_local(mesh):
    net = Links(mesh)
    n, nd = net.n, net.nd
    dp_order = list(range(0, nd, 2)) + list(range(1, nd, 2))
    half_way = n // 2
    ring_order = [0] + [s for k in range(1, half_way) for s in (-k, k)] + ["a", "b"]

    def exchange(blocks, axis="seq"):
        return [b if r == 0 else net.swap(b, axis, r) for r, b in enumerate(blocks)]

    def chips(x, *deps):
        sent = after(x, *deps)
        return [x] + [net.swap(sent, "dp", r) for r in range(2, nd, 2)]

    def cores(near, *deps):
        return list(near) + [net.swap(v, "dp", 1) for v in tie(near, *deps)]

    def paced(ring, blocks, spare=1):
        out, sent = [], 1
        arrived = ring.step()
        steps = half_way - 1
        for k in range(steps):
            until = 1 + (n - 1) * (k + 1) // steps
            some = tie(blocks[sent:until], *arrived)
            fresh = [net.swap(b, "seq", sent + i) for i, b in enumerate(some)]
            arrived = ring.step(*out[-len(some) :]) if k else ring.step()
            out += fresh
            sent = until
        return out

    def local(
        layer_input,
        global_keys,
        global_values,
        lengths,
        attn_gain,
        query_weight,
        out_weight,
        ffn_gain,
        gate_weight,
        up_weight,
        down_weight,
        cotangent,
    ):
        length = lengths[0]
        me, mine = lax.axis_index("seq"), lax.axis_index("dp")
        core, group = mine % 2, net.group(mine)
        place = net.place()
        depth = layer_input.shape[1]
        quarter = depth // nd
        per = n // nd
        owners = [net.owner(place, key) for key in ring_order[:-2]] + [net.owner(place, half_way)]
        info = jnp.stack([me, group, core, *owners]).astype(jnp.int32)
        heads_info = jnp.stack([me, length, group * per + me % per]).astype(jnp.int32)

        gains = jnp.concatenate([attn_gain, ffn_gain])
        gain_rows = jnp.zeros((GAIN_ROWS, quarter), jnp.bfloat16)
        gain_rows = gain_rows.at[:, : gains.shape[0]].set(gains[None])
        mine_of = [columns(w, group * quarter, quarter) for w in (query_weight, out_weight)]
        ring = RingGather(net, jnp.concatenate([gain_rows, *mine_of], 0))
        kv_sent = list(pack_keys_values(n, info, global_keys, global_values))
        kv_blocks = [kv_sent[0]] + paced(ring, kv_sent)
        got = ring.got
        xs = cores(chips(layer_input), got["a"], got["b"])
        q_sent, normed_all, gains, query_quarter, out_quarter = project_queries(
            n, nd, info, xs, [got[k] for k in ring_order]
        )
        q_sent = tie(q_sent, *kv_blocks)
        q_blocks = [net.to_heads(b, m) for m, b in enumerate(q_sent)]
        out_near = chips(out_quarter, *q_blocks)
        mixed_sent, stats, ot = attention_forward(heads_info, q_blocks, kv_blocks)
        cot_ring = RingGather(net, cotangent)
        cot_1 = cot_ring.step(*q_blocks)
        mixed_blocks = exchange(tie(mixed_sent, *cot_1))
        cot_2 = cot_ring.step(*mixed_blocks)
        out_parts = cores(out_near, *mixed_blocks[1:])
        hidden, normed_ffn, mixed = project_mixed(
            n, nd, info, layer_input, gains, mixed_blocks, out_parts
        )

        nf_ring = RingGather(net, normed_ffn)
        weights = (gate_weight, up_weight, down_weight)
        units = gate_weight.shape[0]
        made = {0: ffn_blocks([normed_ffn], [cotangent], weights)[0]}

        def ffn(*keys, deps=()):
            nf, cot = ([ring.got[k] for k in keys] for ring in (nf_ring, cot_ring))
            nf = tie(nf, *deps)
            made.update(zip(keys, ffn_blocks(nf, cot, weights)))

        fresh = nf_ring.step()
        query_near = chips(query_quarter, normed_ffn)
        cot_fresh, before = cot_2, (made[0][3],)
        for k in range(1, half_way):
            later = cot_ring.step(*fresh) if cot_ring.at < half_way else cot_fresh
            fresh = nf_ring.step(*cot_fresh, *before, *(query_near if k == half_way - 1 else ()))
            ffn(-k, k)
            before = (made[k][3], made[-k][3])
            cot_fresh = later
        query_parts = cores(query_near, *fresh)
        mixed_near = chips(mixed, *query_near)
        ffn("a", "b", deps=before)
        nf, cot = nf_ring.got, cot_ring.got

        def exchange_x(kept, *deps):
            sent = after(kept, *deps)
            return [net.swap(sent, "dp", r) for r in range(2, nd, 2)]

        grad_sum = RowSum(net, lambda key: made[key][3])
        out_sum = RowSum(net, lambda key: made[key][4])
        arrived = grad_sum.step()
        kept, deps, swapped, mixed_parts, out_1 = [], (), None, (), ()
        for k in range(3):
            upcoming = grad_sum.step(*deps, *out_1, *((query_parts, mixed_near, mixed_parts)[k]))
            if k == 1:
                out_1 = out_sum.step(*arrived)
            if k == 1:
                mixed_parts = cores(mixed_near, *arrived)
            lhs = tie([made[key][(1, 2, 0)[k]] for key in ring_order], *arrived)
            rhs = [(nf, nf, cot)[k][key] for key in ring_order]
            if swapped:
                kept.append(low(wide(mine_half) + wide(swapped[0])))
            deps = (*swapped,) if swapped else ()
            mine_half, sent_half = weight_gradient(info, lhs, rhs, units)
            swapped = (net.swap(sent_half, "dp", 1),)
            deps = (*deps, mine_half)
            last, arrived = arrived, upcoming
        top = units // 2
        others = [exchange_x(kept[0][:top], *last)]
        grad_sums = tie(grad_sum.rest(), *deps, *others[0])
        kept.append(low(wide(mine_half) + wide(swapped[0])))
        others.append(exchange_x(kept[0][top:], *grad_sums[1:]))

        def dp_cols(cols, *deps):
            sent = tie(cols, *deps)
            return [b if r == 0 else net.swap(b, "dp", r) for r, b in zip(dp_order, sent)]

        out_2 = out_sum.step(*grad_sums[1:])
        gm_sent, branch_cols, grad_hidden, ffn_gain_part = branch_gradient(
            n, nd, info, hidden, gains, cotangent, grad_sums, out_parts
        )
        gm_blocks = exchange(tie(gm_sent, *others[1]))
        branch_got = dp_cols(branch_cols, *gm_sent)
        gm_blocks = tie(gm_blocks, *branch_got, *out_2)
        others.append(exchange_x(kept[1][:top], *gm_blocks))
        out_3 = out_sum.step(*gm_blocks)
        dq_sent, dkv_sent = attention_backward(
            heads_info, q_blocks, kv_blocks, gm_blocks, stats, ot
        )


        dq_sent = tie(dq_sent, *out_3, *others[2])
        others.append(exchange_x(kept[1][top:], *dq_sent))
        dq_blocks = tie(exchange(dq_sent), *others[3])

        def dp_total(k, *deps):
            total = chip_sum(tie([kept[k], *others[2 * k], *others[2 * k + 1]], *deps))
            return total, net.swap(total, "dp", 1)

        query_cols = sort_columns(n, nd, info, dq_blocks)

        query_got = dp_cols(query_cols)
        out_4 = out_sum.step(*query_cols)
        early = (n - 1) * 2 // 7
        dkv_early = [
            net.swap(b, "seq", r + 1) for r, b in enumerate(tie(dkv_sent[1 : early + 1], *query_cols))
        ]
        input_grad, attn_gain_part = input_gradient(
            nd, layer_input, gains, grad_hidden, query_cols, query_parts
        )
        dkv_more = [
            net.swap(b, "seq", early + 1 + r)
            for r, b in enumerate(tie(dkv_sent[early + 1 :], attn_gain_part))
        ]
        dkv_blocks = [dkv_sent[0], *dkv_early, *dkv_more]
        for rows in (slice(top), slice(top, units)):
            others.append(exchange_x(kept[2][rows], *query_got))
        gate_total = dp_total(0, *dq_blocks)
        up_total = dp_total(1, *query_cols)
        shares = projection_gradients(
            n,
            nd,
            info,
            mixed_parts,
            normed_all,
            attn_gain_part,
            ffn_gain_part,
            branch_got,
            query_got,
        )

        def share_of(key):
            if key in ("a", "b"):
                rows = shares[-1].shape[0] // 2
                return shares[-1][:rows] if key == "a" else shares[-1][rows:]
            return shares[ring_order.index(key)]

        share_sum = RowSum(net, share_of)
        shared = share_sum.step(*out_4, *dkv_early)
        gate_grad = spread_columns(info, *tie(gate_total, *shared))
        share_sum.step(*dkv_more[: len(dkv_more) // 2])
        up_grad = spread_columns(info, *tie(up_total, *shared))
        for _ in range(half_way - 3):
            share_sum.step(gate_grad, *dkv_more)
        down_total = dp_total(2, *shared)
        share_sum.step(up_grad)
        down_grad = spread_columns(info, *down_total)
        key_grad, value_grad = split_keys_values(n, info, dkv_blocks)
        own, first, second = share_sum.rest()
        projections = low(own + wide(first) + wide(second))
        projections = after(projections, down_grad, key_grad)
        out_grad, query_grad, gain_sum = join_projections(
            nd, info, cores(chips(projections))
        )
        own, first, second = out_sum.rest()
        layer_output = low(hidden + (own + wide(first) + wide(second)))
        attn_count = attn_gain.shape[0]
        return (
            layer_output,
            input_grad,
            key_grad,
            value_grad,
            gain_sum[0, :attn_count],
            query_grad,
            out_grad,
            gain_sum[0, attn_count : 2 * attn_count],
            gate_grad,
            up_grad,
            down_grad,
        )

    return local


def solution(mesh):
    placed = (
        P(("dp", "seq"), None),
        P(("dp", "seq"), None),
        P(("dp", "seq"), None),
        P("dp"),
        P("seq"),
        P("seq", None),
        P("seq", None),
        P("seq"),
        P("seq", None),
        P("seq", None),
        P("seq", None),
        P(("dp", "seq"), None),
    )
    return jax.shard_map(
        make_local(mesh),
        mesh=mesh,
        in_specs=placed,
        out_specs=(
            P(("dp", "seq"), None),
            P(("dp", "seq"), None),
            P(("dp", "seq"), None),
            P(("dp", "seq"), None),
            P("seq"),
            P("seq", None),
            P("seq", None),
            P("seq"),
            P("seq", None),
            P("seq", None),
            P("seq", None),
        ),
        check_vma=False,
    )
```

```python
import functools

import jax
import jax.numpy as jnp
from jax import lax
from jax.experimental import pallas as pl
from jax.experimental.pallas import tpu as pltpu
from jax.sharding import PartitionSpec as P

HEAD_DIM = 128
ATT_BLOCK = 512


EPSILON = 1e-05


def product(left_side, right_side):
    return jnp.dot(left_side, right_side, preferred_element_type=jnp.float32)


def inner_rows(left_side, right_side):
    return lax.dot_general(
        left_side, right_side, (((0,), (0,)), ((), ())), preferred_element_type=jnp.float32
    )


def outer_cols(left_side, right_side):
    return lax.dot_general(
        left_side, right_side, (((1,), (1,)), ((), ())), preferred_element_type=jnp.float32
    )


def snake(count):
    deep = 4 if count % 4 == 0 else 1
    wide = count // deep
    if deep == 1 or wide == 1:
        return list(range(count))
    order = []
    for z in range(deep):
        across = range(1, wide) if z % 2 == 0 else range(wide - 1, 0, -1)
        order += [z * wide + y for y in across]
    return order + [z * wide for z in range(deep - 1, -1, -1)]


def after(value, *others):
    return lax.optimization_barrier((value, *others))[0] if others else value


def tie(values, *others):
    return list(lax.optimization_barrier((*values, *others))[: len(values)])


def low(value):
    return value.astype(jnp.bfloat16)


def wide(value):
    return value.astype(jnp.float32)


class Links:
    def __init__(self, mesh):
        self.n = mesh.shape["seq"]
        self.nd = mesh.shape["dp"]
        self.order = snake(self.n)
        n = self.n
        self.right = [(self.order[k], self.order[(k + 1) % n]) for k in range(n)]
        self.left = [(b, a) for a, b in self.right]

    def group(self, d):
        return d % 2 * (self.nd // 2) + d // 2

    def place(self):
        me = lax.axis_index("seq")
        table = [0] * self.n
        for k, i in enumerate(self.order):
            table[i] = k
        return sum(jnp.where(me == i, table[i], 0) for i in range(self.n))

    def owner(self, place, distance):
        spot = (place + distance) % self.n
        return sum(jnp.where(spot == k, self.order[k], 0) for k in range(self.n))

    def to_right(self, x):
        return lax.ppermute(x, "seq", self.right)

    def to_left(self, x):
        return lax.ppermute(x, "seq", self.left)

    def to_heads(self, x, m):
        per, nx = self.n // self.nd, self.nd // 2
        pairs = []
        for d in range(self.nd):
            for s in range(self.n):
                j = s ^ m
                group = j // per
                to = group % nx * 2 + group // nx
                pairs.append((d * self.n + s, to * self.n + self.group(d) * per + j % per))
        return lax.ppermute(x, ("dp", "seq"), pairs)

    def swap(self, x, axis, r):
        count = self.n if axis == "seq" else self.nd
        return lax.ppermute(x, axis, [(k, k ^ r) for k in range(count)])


class RingGather:
    def __init__(self, net, x):
        self.net, self.got, self.at = net, {0: x}, 0
        self.from_left = self.from_right = x

    def step(self, *deps):
        net, half = self.net, self.net.n // 2
        self.at += 1
        left, right = self.from_left, self.from_right
        if self.at == half:
            rows = left.shape[0] // 2
            left, right = left[:rows], right[rows:]
        if self.at == 1 and half > 1:
            left = right = after(left, *deps)
        else:
            left, right = tie([left, right], *deps)
        self.from_left, self.from_right = net.to_right(left), net.to_left(right)
        keys = ("a", "b") if self.at == half else (-self.at, self.at)
        self.got[keys[0]], self.got[keys[1]] = self.from_left, self.from_right
        return self.from_left, self.from_right

    def rest(self):
        while self.at < self.net.n // 2:
            self.step()
        return self.got


class RowSum:
    def __init__(self, net, part):
        self.net, self.part, self.at = net, part, net.n // 2
        self.going_left = self.going_right = None

    def step(self, *deps):
        net, half, s = self.net, self.net.n // 2, self.at
        if s == half:
            left, right = self.part("b"), self.part("a")
        else:
            left, right = self.part(-s), self.part(s)
            if s == half - 1:
                rows = left.shape[0] // 2
                left = jnp.concatenate([left[:rows], left[rows:] + wide(self.going_left)])
                right = jnp.concatenate([right[:rows] + wide(self.going_right), right[rows:]])
            else:
                left = left + wide(self.going_left)
                right = right + wide(self.going_right)
        left, right = tie([low(left), low(right)], *deps)
        self.going_left, self.going_right = net.to_left(left), net.to_right(right)
        self.at -= 1
        return self.going_left, self.going_right

    def rest(self):
        while self.at:
            self.step()
        return self.part(0), self.going_left, self.going_right


VMEM_LIMIT = 56 * 1024 * 1024
COST_SHARE = 4
ANYWHERE = pl.BlockSpec(memory_space=pl.ANY)
IN_VMEM = pl.BlockSpec(memory_space=pltpu.VMEM)
IN_SMEM = pl.BlockSpec(memory_space=pltpu.SMEM)
LOG2_E = 1.4426950408889634
DEAD = 1e30


def nt_dot(a, b):
    return lax.dot_general(a, b, (((1,), (1,)), ((), ())), preferred_element_type=jnp.float32)


def tn_dot(a, b):
    return lax.dot_general(a, b, (((0,), (0,)), ((), ())), preferred_element_type=jnp.float32)


def call(body, operands, specs, outs, out_specs, scratch, flops, moved, name):
    return pl.pallas_call(
        body,
        name=name,
        in_specs=specs,
        out_specs=tuple(out_specs),
        out_shape=tuple(jax.ShapeDtypeStruct(s, t) for s, t in outs),
        scratch_shapes=scratch,
        compiler_params=pltpu.CompilerParams(vmem_limit_bytes=VMEM_LIMIT),
        cost_estimate=pl.CostEstimate(
            flops=flops // COST_SHARE, bytes_accessed=moved // COST_SHARE, transcendentals=0
        ),
    )(*operands)


def aligned(index, unit):
    return pl.multiple_of(index * unit, unit)


def start_all(copies):
    for copy in copies:
        copy.start()
    return copies


def wait_all(copies):
    for copy in copies:
        copy.wait()


def causal_mask(block):
    key_at = lax.broadcasted_iota(jnp.int32, (block, block), 0)
    query_at = lax.broadcasted_iota(jnp.int32, (block, block), 1)
    return key_at <= query_at


def forward_body(n, info, *refs):
    q_in, kv_in = refs[:n], refs[n : 2 * n]
    outs, stats, ot = refs[2 * n : 3 * n], refs[3 * n], refs[3 * n + 1]
    qs, ks, vs, vt, mixed, sems = refs[3 * n + 2 :]
    me, length, spot = info[0], info[1], info[2]
    count, width = q_in[0].shape
    heads = width // HEAD_DIM
    total = n * count
    blocks = total // ATT_BLOCK
    copies = []
    for r in range(n):
        rows = pl.ds(aligned(me ^ r, count), count)
        query_rows = pl.ds(aligned(spot ^ r, count), count)
        for k, (src, dst) in enumerate(
            (
                (kv_in[r].at[:, pl.ds(0, width)], ks.at[rows]),
                (kv_in[r].at[:, pl.ds(width, width)], vs.at[rows]),
                (q_in[r], qs.at[query_rows]),
            )
        ):
            copies.append(pltpu.make_async_copy(src, dst, sems.at[3 * r + k]))
    wait_all(start_all(copies))
    factor = HEAD_DIM ** (-0.5) * LOG2_E

    def transpose_values(b, _):
        at = pl.ds(pl.multiple_of(b * ATT_BLOCK, ATT_BLOCK), ATT_BLOCK)
        vt[:, at] = vs[at, :].T
        return 0

    lax.fori_loop(0, blocks, transpose_values, 0)
    live = jnp.minimum((length + ATT_BLOCK - 1) // ATT_BLOCK, blocks)

    def tile(qi, kj, state, masked):
        new = []
        q_at = pl.ds(pl.multiple_of(qi * ATT_BLOCK, ATT_BLOCK), ATT_BLOCK)
        k_at = pl.ds(pl.multiple_of(kj * ATT_BLOCK, ATT_BLOCK), ATT_BLOCK)
        for h in range(heads):
            cols = slice(h * HEAD_DIM, (h + 1) * HEAD_DIM)
            top, total_sum, acc = state[h]
            scores = nt_dot(ks[k_at, cols], qs[q_at, cols]) * factor
            if masked:
                scores = jnp.where(causal_mask(ATT_BLOCK), scores, -DEAD)
            higher = jnp.maximum(top, jnp.max(scores, axis=0, keepdims=True))
            weights = jnp.exp2(scores - higher)
            shrink = jnp.exp2(top - higher)
            total_sum = total_sum * shrink + jnp.sum(weights, axis=0, keepdims=True)
            acc = acc * shrink + jnp.dot(
                vt[cols, k_at], weights.astype(jnp.bfloat16), preferred_element_type=jnp.float32
            )
            new.append((higher, total_sum, acc))
        return tuple(new)

    stats[...] = jnp.full(stats.shape, DEAD, jnp.float32)

    def query_block(qi, _):
        first = tuple(
            (
                jnp.full((1, ATT_BLOCK), -DEAD, jnp.float32),
                jnp.zeros((1, ATT_BLOCK), jnp.float32),
                jnp.zeros((HEAD_DIM, ATT_BLOCK), jnp.float32),
            )
            for _ in range(heads)
        )
        state = lax.fori_loop(0, qi, lambda kj, s: tile(qi, kj, s, False), first)
        state = tile(qi, qi, state, True)
        q_at = pl.ds(pl.multiple_of(qi * ATT_BLOCK, ATT_BLOCK), ATT_BLOCK)
        query_at = qi * ATT_BLOCK + lax.broadcasted_iota(jnp.int32, (1, ATT_BLOCK), 1)
        alive = query_at < length
        for h in range(heads):
            cols = slice(h * HEAD_DIM, (h + 1) * HEAD_DIM)
            top, total_sum, acc = state[h]
            scaled = acc * jnp.where(alive, 1.0 / total_sum, 0.0)
            ot[cols, q_at] = scaled
            mixed[q_at, cols] = scaled.T.astype(jnp.bfloat16)
            stats[h : h + 1, q_at] = jnp.where(alive, top + jnp.log2(total_sum), DEAD)
        return 0

    lax.fori_loop(0, live, query_block, 0)

    def dead_block(qi, _):
        q_at = pl.ds(pl.multiple_of(qi * ATT_BLOCK, ATT_BLOCK), ATT_BLOCK)
        mixed[q_at, :] = jnp.zeros((ATT_BLOCK, width), jnp.bfloat16)
        ot[:, q_at] = jnp.zeros((width, ATT_BLOCK), jnp.float32)
        return 0

    lax.fori_loop(live, blocks, dead_block, 0)
    copies = []
    for r in range(n):
        rows = pl.ds(pl.multiple_of((me ^ r) * count, count), count)
        copies.append(pltpu.make_async_copy(mixed.at[rows], outs[r], sems.at[r]))
    wait_all(start_all(copies))


def attention_forward(info, q_blocks, kv_blocks):
    n = len(q_blocks)
    count, width = q_blocks[0].shape
    total = n * count
    got = call(
        functools.partial(forward_body, n),
        [info, *q_blocks, *kv_blocks],
        [IN_SMEM] + [ANYWHERE] * (2 * n),
        [((count, width), jnp.bfloat16)] * n
        + [((8, total), jnp.float32), ((width, total), jnp.float32)],
        [ANYWHERE] * n + [IN_VMEM] * 2,
        [pltpu.VMEM((total, width), jnp.bfloat16)] * 3
        + [pltpu.VMEM((width, total), jnp.bfloat16), pltpu.VMEM((total, width), jnp.bfloat16)]
        + [pltpu.SemaphoreType.DMA((3 * n,))],
        16 * 2 * total * total * width // 2,
        10 * total * width,
        "attention_forward",
    )
    return got[:n], got[n], got[n + 1]


def backward_body(n, info, *refs):
    q_in, kv_in, g_in = refs[:n], refs[n : 2 * n], refs[2 * n : 3 * n]
    stats, ot = refs[3 * n], refs[3 * n + 1]
    refs = refs[3 * n + 2 :]
    dq_out, dkv_out = refs[:n], refs[n : 2 * n]
    qs, ks, vs, gs, kt, delta, dqt, dk, dv, dq_low, dkv_low, sems = refs[2 * n :]
    me, length, spot = info[0], info[1], info[2]
    count, width = q_in[0].shape
    heads = width // HEAD_DIM
    total = n * count
    blocks = total // ATT_BLOCK
    copies = []
    for r in range(n):
        rows = pl.ds(aligned(me ^ r, count), count)
        query_rows = pl.ds(aligned(spot ^ r, count), count)
        for k, (src, dst) in enumerate(
            (
                (kv_in[r].at[:, pl.ds(0, width)], ks.at[rows]),
                (kv_in[r].at[:, pl.ds(width, width)], vs.at[rows]),
                (q_in[r], qs.at[query_rows]),
                (g_in[r], gs.at[rows]),
            )
        ):
            copies.append(pltpu.make_async_copy(src, dst, sems.at[4 * r + k]))
    start_all(copies)
    live = jnp.minimum((length + ATT_BLOCK - 1) // ATT_BLOCK, blocks)
    scale = HEAD_DIM ** (-0.5)
    factor = scale * LOG2_E

    def clear(b, _):
        at = pl.ds(pl.multiple_of(b * ATT_BLOCK, ATT_BLOCK), ATT_BLOCK)
        dqt[:, at] = jnp.zeros((width, ATT_BLOCK), jnp.float32)
        dk[at, :] = jnp.zeros((ATT_BLOCK, width), jnp.float32)
        dv[at, :] = jnp.zeros((ATT_BLOCK, width), jnp.float32)
        return 0

    lax.fori_loop(0, blocks, clear, 0)
    wait_all(copies)

    def prepare(b, _):
        at = pl.ds(pl.multiple_of(b * ATT_BLOCK, ATT_BLOCK), ATT_BLOCK)
        kt[:, at] = ks[at, :].T
        both = gs[at, :].astype(jnp.float32).T * ot[:, at]
        for h in range(heads):
            cols = slice(h * HEAD_DIM, (h + 1) * HEAD_DIM)
            delta[h : h + 1, at] = jnp.sum(both[cols], axis=0, keepdims=True)
        return 0

    lax.fori_loop(0, blocks, prepare, 0)

    def tile(qi, kj, masked):
        q_at = pl.ds(pl.multiple_of(qi * ATT_BLOCK, ATT_BLOCK), ATT_BLOCK)
        k_at = pl.ds(pl.multiple_of(kj * ATT_BLOCK, ATT_BLOCK), ATT_BLOCK)
        for h in range(heads):
            cols = slice(h * HEAD_DIM, (h + 1) * HEAD_DIM)
            q, g = qs[q_at, cols], gs[q_at, cols]
            scores = nt_dot(ks[k_at, cols], q) * factor - stats[h : h + 1, q_at]
            if masked:
                scores = jnp.where(causal_mask(ATT_BLOCK), scores, -DEAD)
            weights = jnp.exp2(scores)
            grad_weights = nt_dot(vs[k_at, cols], g)
            grad_scores = (weights * (grad_weights - delta[h : h + 1, q_at])).astype(jnp.bfloat16)
            dv[k_at, cols] += jnp.dot(
                weights.astype(jnp.bfloat16), g, preferred_element_type=jnp.float32
            )
            dk[k_at, cols] += jnp.dot(grad_scores, q, preferred_element_type=jnp.float32)
            dqt[cols, q_at] += jnp.dot(
                kt[cols, k_at], grad_scores, preferred_element_type=jnp.float32
            )

    def query_block(qi, _):
        def step(kj, _):
            tile(qi, kj, False)
            return 0

        lax.fori_loop(0, qi, step, 0)
        tile(qi, qi, True)
        return 0

    lax.fori_loop(0, live, query_block, 0)

    def finish(b, _):
        at = pl.ds(pl.multiple_of(b * ATT_BLOCK, ATT_BLOCK), ATT_BLOCK)
        dq_low[at, :] = (dqt[:, at] * scale).T.astype(jnp.bfloat16)
        dkv_low[at, :width] = (dk[at, :] * scale).astype(jnp.bfloat16)
        dkv_low[at, width:] = dv[at, :].astype(jnp.bfloat16)
        return 0

    lax.fori_loop(0, blocks, finish, 0)
    copies = []
    for r in range(n):
        rows = pl.ds(pl.multiple_of((me ^ r) * count, count), count)
        copies.append(pltpu.make_async_copy(dq_low.at[rows], dq_out[r], sems.at[2 * r]))
        copies.append(pltpu.make_async_copy(dkv_low.at[rows], dkv_out[r], sems.at[2 * r + 1]))
    wait_all(start_all(copies))


def attention_backward(info, q_blocks, kv_blocks, g_blocks, stats, ot):
    n = len(q_blocks)
    count, width = q_blocks[0].shape
    total = n * count
    low_all = pltpu.VMEM((total, width), jnp.bfloat16)
    got = call(
        functools.partial(backward_body, n),
        [info, *q_blocks, *kv_blocks, *g_blocks, stats, ot],
        [IN_SMEM] + [ANYWHERE] * (3 * n) + [IN_VMEM] * 2,
        [((count, width), jnp.bfloat16)] * n + [((count, 2 * width), jnp.bfloat16)] * n,
        [ANYWHERE] * (2 * n),
        [low_all] * 4
        + [
            pltpu.VMEM((width, total), jnp.bfloat16),
            pltpu.VMEM((8, total), jnp.float32),
            pltpu.VMEM((width, total), jnp.float32),
            pltpu.VMEM((total, width), jnp.float32),
            pltpu.VMEM((total, width), jnp.float32),
            low_all,
            pltpu.VMEM((total, 2 * width), jnp.bfloat16),
            pltpu.SemaphoreType.DMA((4 * n,)),
        ],
        40 * 2 * total * total * width // 2,
        20 * total * width,
        "attention_backward",
    )
    return got[:n], got[n:]


def pack_body(n, info, keys, values, *refs):
    outs, sems = refs[:n], refs[n]
    me = info[0]
    width = outs[0].shape[1] // 2
    copies = []
    for r in range(n):
        cols = pl.ds(aligned(me ^ r, width), width)
        copies.append(
            pltpu.make_async_copy(keys.at[:, cols], outs[r].at[:, pl.ds(0, width)], sems.at[2 * r])
        )
        copies.append(
            pltpu.make_async_copy(
                values.at[:, cols], outs[r].at[:, pl.ds(width, width)], sems.at[2 * r + 1]
            )
        )
    wait_all(start_all(copies))


def pack_keys_values(n, info, keys, values):
    count, depth = keys.shape
    return call(
        functools.partial(pack_body, n),
        [info, keys, values],
        [IN_SMEM, ANYWHERE, ANYWHERE],
        [((count, 2 * depth // n), jnp.bfloat16)] * n,
        [IN_VMEM] * n,
        [pltpu.SemaphoreType.DMA((2 * n,))],
        0,
        8 * count * depth,
        "pack_keys_values",
    )


GAIN_ROWS = 32


def norm_parts(v):
    return lax.rsqrt(jnp.mean(v * v, axis=-1, keepdims=True) + EPSILON)


def query_body(n, nd, info, *refs):
    xs, pieces = refs[:nd], refs[nd : nd + n + 1]
    q_out = refs[nd + n + 1 : nd + 2 * n + 1]
    normed, gains, weight, out_weight = refs[nd + 2 * n + 1 : nd + 2 * n + 5]
    queries, gain_rows, sems = refs[nd + 2 * n + 5 :]
    me, dp = info[0], info[1]
    count, depth = xs[0].shape
    wrows = (pieces[0].shape[0] - GAIN_ROWS) // 2
    cut = wrows - GAIN_ROWS // 2
    copies, later = [], []

    def fetch(into, k, src, dst, j):
        into.append(pltpu.make_async_copy(src, dst, sems.at[3 * k + j]))

    for k in range(n):
        first = info[3 + k] * wrows
        gain_at = gain_rows.at[pl.ds(aligned(info[3 + k], 16), 16)]
        fetch(copies, k, pieces[k].at[pl.ds(0, 16)], gain_at, 0)
        at = pl.multiple_of(first, 16)
        if k < n - 1:
            rows = pl.ds(at, wrows)
            fetch(copies, k, pieces[k].at[pl.ds(GAIN_ROWS, wrows)], weight.at[rows], 1)
            fetch(later, k, pieces[k].at[pl.ds(GAIN_ROWS + wrows, wrows)], out_weight.at[rows], 2)
        else:
            below = pl.multiple_of(first + cut, 16)
            fetch(copies, k, pieces[k].at[pl.ds(GAIN_ROWS, cut)], weight.at[pl.ds(at, cut)], 1)
            rest = pl.ds(below, wrows - cut)
            fetch(copies, k, pieces[n].at[pl.ds(0, wrows - cut)], weight.at[rest], 2)
            tail = pieces[n].at[pl.ds(wrows - cut, wrows)]
            fetch(later, n, tail, out_weight.at[pl.ds(at, wrows)], 0)
    start_all(copies)
    start_all(later)
    wait_all(copies)
    share = depth // n
    for o in range(n):
        row = gain_rows[o * 16 : o * 16 + 16, : 2 * share].astype(jnp.float32)
        gains[0:1, o * share : (o + 1) * share] = row[0:1, :share]
        gains[1:2, o * share : (o + 1) * share] = row[0:1, share:]
    for k in range(nd):
        v = xs[k][...].astype(jnp.float32)
        rows = slice(k * count, (k + 1) * count)
        normed[rows, :] = (v * norm_parts(v) * gains[0:1, :]).astype(jnp.bfloat16)
        queries[rows, :] = jnp.dot(
            normed[rows, :], weight[...], preferred_element_type=jnp.float32
        ).astype(jnp.bfloat16)
    per = n // nd
    copies = []
    for m in range(n):
        j = me ^ m
        slot = dp ^ (j // per)
        copies.append(
            pltpu.make_async_copy(
                queries.at[
                    pl.ds(aligned(slot, count), count), pl.ds(aligned(j % per, share), share)
                ],
                q_out[m],
                sems.at[3 * n + 3 + m],
            )
        )
    wait_all(start_all(copies))
    wait_all(later)


def project_queries(n, nd, info, xs, pieces):
    count, depth = xs[0].shape
    quarter = pieces[0].shape[1]
    got = call(
        functools.partial(query_body, n, nd),
        [info, *xs, *pieces],
        [IN_SMEM] + [IN_VMEM] * nd + [ANYWHERE] * (n + 1),
        [((count, depth // n), jnp.bfloat16)] * n
        + [
            ((nd * count, depth), jnp.bfloat16),
            ((8, depth), jnp.float32),
            ((depth, quarter), jnp.bfloat16),
            ((depth, quarter), jnp.bfloat16),
        ],
        [ANYWHERE] * n + [IN_VMEM] * 4,
        [
            pltpu.VMEM((nd * count, quarter), jnp.bfloat16),
            pltpu.VMEM((n * 16, quarter), jnp.bfloat16),
            pltpu.SemaphoreType.DMA((4 * n + 3,)),
        ],
        2 * count * depth * depth,
        6 * depth * depth,
        "project_queries",
    )
    return got[:n], *got[n:]


def padded(width):
    return (width + 127) // 128 * 128


def ffn_body(m, *refs):
    nf_in, cot_in, weights_in = refs[:m], refs[m : 2 * m], refs[2 * m : 2 * m + 3]
    outs = refs[2 * m + 3 : 7 * m + 3]
    nf, cot, gate_w, up_w, down_w, acts, shares, sems, out_sems = refs[7 * m + 3 :]
    weights = (gate_w, up_w, down_w)
    rows = nf_in[0].shape[0]
    hidden_units = gate_w.shape[0]

    def load(src, dst, k):
        return pltpu.make_async_copy(src, dst, sems.at[k])

    at = [pl.ds(b * rows, rows) for b in range(m)]
    loads = [load(weights_in[k], weights[k], k) for k in range(3)]
    nf_loads = [load(nf_in[b], nf.at[at[b]], 3 + b) for b in range(m)]
    cot_loads = [load(cot_in[b], cot.at[at[b]], 3 + m + b) for b in range(m)]
    start_all([*nf_loads, loads[0], loads[1], *cot_loads, loads[2]])
    copies = []

    def store(k, src):
        for b in range(m):
            copy = pltpu.make_async_copy(
                src.at[at[b]], outs[5 * b + k], out_sems.at[5 * b + k]
            )
            copy.start()
            copies.append(copy)

    wait_all(nf_loads)
    loads[0].wait()
    gate_value = nt_dot(nf[...], gate_w[...])
    loads[1].wait()
    up_value = nt_dot(nf[...], up_w[...])
    wait_all(cot_loads)
    loads[2].wait()
    grad_inner = nt_dot(cot[...], down_w[...])
    sigmoid = 1.0 / (1.0 + jnp.exp(-gate_value))
    act = gate_value * sigmoid
    inner = (act * up_value).astype(jnp.bfloat16)
    grad_gate = (
        grad_inner * up_value * sigmoid * (1.0 + gate_value * (1.0 - sigmoid))
    ).astype(jnp.bfloat16)
    grad_up = (grad_inner * act).astype(jnp.bfloat16)
    for k, value in enumerate((inner, grad_gate, grad_up)):
        acts[k, :, :hidden_units] = value
        store(k, acts.at[k])
    shares[0] = jnp.dot(grad_gate, gate_w[...], preferred_element_type=jnp.float32) + jnp.dot(
        grad_up, up_w[...], preferred_element_type=jnp.float32
    )
    store(3, shares.at[0])
    shares[1] = jnp.dot(inner, down_w[...], preferred_element_type=jnp.float32)
    store(4, shares.at[1])
    wait_all(copies)


def ffn_blocks(nf, cot, weights):
    m = len(nf)
    rows, depth = nf[0].shape
    units = weights[0].shape[0]
    act = ((rows, padded(units)), jnp.bfloat16)
    share = ((rows, depth), jnp.float32)
    got = call(
        functools.partial(ffn_body, m),
        [*nf, *cot, *weights],
        [ANYWHERE] * (2 * m + 3),
        [act, act, act, share, share] * m,
        [ANYWHERE] * (5 * m),
        [pltpu.VMEM((m * rows, depth), jnp.bfloat16)] * 2
        + [pltpu.VMEM((units, depth), jnp.bfloat16)] * 3
        + [
            pltpu.VMEM((3, m * rows, padded(units)), jnp.bfloat16),
            pltpu.VMEM((2, m * rows, depth), jnp.float32),
            pltpu.SemaphoreType.DMA((3 + 2 * m,)),
            pltpu.SemaphoreType.DMA((5 * m,)),
        ],
        12 * m * rows * units * depth,
        6 * units * depth + 12 * m * rows * depth,
        "ffn_blocks",
    )
    return [got[5 * b : 5 * b + 5] for b in range(m)]


def weight_gradient_body(count, units, info, *refs):
    lhs_in, rhs_in = refs[:count], refs[count : 2 * count]
    kept, sent, lhs, turned, rhs, sems = refs[2 * count :]
    core = info[2]
    copies, first = [], 0
    for k in range(count):
        rows = lhs_in[k].shape[0]
        at = pl.ds(first, rows)
        copies.append(pltpu.make_async_copy(lhs_in[k], lhs.at[at], sems.at[2 * k]))
        copies.append(pltpu.make_async_copy(rhs_in[k], rhs.at[at], sems.at[2 * k + 1]))
        first += rows
    start_all(copies)
    wait_all(copies[::2])
    block = 256

    def turn(b, _):
        at = pl.ds(aligned(b, block), block)
        turned[:, at] = lhs[at, :].T
        return 0

    lax.fori_loop(0, first // block, turn, 0)
    wait_all(copies[1::2])
    half = kept.shape[1]
    piece = 256

    def step(c, _):
        to = pl.ds(aligned(c, piece), piece)
        for out, side in ((kept, core), (sent, 1 - core)):
            cols = pl.ds(pl.multiple_of(side * half + c * piece, piece), piece)
            out[:, to] = jnp.dot(
                turned[...], rhs[:, cols], preferred_element_type=jnp.float32
            )[:units].astype(jnp.bfloat16)
        return 0

    lax.fori_loop(0, half // piece, step, 0)


def weight_gradient(info, lhs, rhs, units):
    count = len(lhs)
    rows = sum(b.shape[0] for b in rhs)
    width, depth = lhs[0].shape[1], rhs[0].shape[1]
    return call(
        functools.partial(weight_gradient_body, count, units),
        [info, *lhs, *rhs],
        [IN_SMEM] + [ANYWHERE] * (2 * count),
        [((units, depth // 2), jnp.bfloat16)] * 2,
        [IN_VMEM] * 2,
        [
            pltpu.VMEM((rows, width), jnp.bfloat16),
            pltpu.VMEM((width, rows), jnp.bfloat16),
            pltpu.VMEM((rows, depth), jnp.bfloat16),
            pltpu.SemaphoreType.DMA((2 * count,)),
        ],
        2 * rows * units * depth,
        2 * rows * depth,
        "weight_gradient",
    )


def hidden_body(n, nd, info, x, gains, *refs):
    blocks, parts = refs[:n], refs[n : n + nd]
    hidden, normed, mixed = refs[n + nd : n + nd + 3]
    weight, sems = refs[n + nd + 3 :]
    me, dp = info[0], info[1]
    share, quarter = blocks[0].shape[1], parts[0].shape[1]
    copies = []
    for r in range(nd):
        cols = pl.ds(aligned(dp ^ r, quarter), quarter)
        copies.append(pltpu.make_async_copy(parts[r], weight.at[:, cols], sems.at[r]))
    for r in range(n):
        cols = pl.ds(aligned(me ^ r, share), share)
        copies.append(pltpu.make_async_copy(blocks[r], mixed.at[:, cols], sems.at[nd + r]))
    start_all(copies[nd:] + copies[:nd])
    wait_all(copies[nd:])
    depth = x.shape[1]
    total = jnp.zeros((x.shape[0], 1), jnp.float32)
    for r in range(nd):
        copies[r].wait()
        cols = pl.ds(aligned(dp ^ r, quarter), quarter)
        v = x[:, cols].astype(jnp.float32) + jnp.dot(
            mixed[...], weight[:, cols], preferred_element_type=jnp.float32
        )
        hidden[:, cols] = v
        total = total + jnp.sum(v * v, axis=-1, keepdims=True)
    normed[...] = (
        hidden[...] * lax.rsqrt(total / depth + EPSILON) * gains[1:2, :]
    ).astype(jnp.bfloat16)


def project_mixed(n, nd, info, x, gains, blocks, parts):
    count, depth = x.shape
    return call(
        functools.partial(hidden_body, n, nd),
        [info, x, gains, *blocks, *parts],
        [IN_SMEM, IN_VMEM, IN_VMEM] + [ANYWHERE] * (n + nd),
        [
            ((count, depth), jnp.float32),
            ((count, depth), jnp.bfloat16),
            ((count, depth), jnp.bfloat16),
        ],
        [IN_VMEM] * 3,
        [pltpu.VMEM((depth, depth), jnp.bfloat16), pltpu.SemaphoreType.DMA((n + nd,))],
        2 * count * depth * depth,
        6 * depth * depth,
        "project_mixed",
    )


def norm_grad(v, gain, upstream):
    scale = norm_parts(v)
    weighted = upstream * gain
    through = weighted * scale - v * (scale**3) * jnp.mean(weighted * v, axis=-1, keepdims=True)
    return through, jnp.sum(upstream * v * scale, axis=0, keepdims=True)


def branch_body(n, nd, info, hidden, gains, cotangent, own, first, second, *refs):
    parts, refs = refs[:nd], refs[nd:]
    gm_out, cols_out = refs[:n], refs[n : n + nd]
    grad_hidden, gain_part, branch, weight, sems = refs[n + nd :]
    me, dp = info[0], info[1]
    quarter = parts[0].shape[1]
    copies = []
    for r in range(nd):
        cols = pl.ds(aligned(dp ^ r, quarter), quarter)
        copies.append(pltpu.make_async_copy(parts[r], weight.at[:, cols], sems.at[r]))
    start_all(copies)
    upstream = own[...] + first[...].astype(jnp.float32) + second[...].astype(jnp.float32)
    through, gain = norm_grad(hidden[...], gains[1:2, :], upstream)
    gain_part[...] = jnp.broadcast_to(gain, gain_part.shape)
    total = cotangent[...].astype(jnp.float32) + through
    grad_hidden[...] = total
    branch[...] = total.astype(jnp.bfloat16)
    for r in range(nd):
        cols_out[r][...] = branch[:, pl.ds(aligned(dp ^ r, quarter), quarter)]
    wait_all(copies)
    share = gm_out[0].shape[1]
    for r in range(n):
        rows = pl.ds(aligned(me ^ r, share), share)
        gm_out[r][...] = nt_dot(branch[...], weight[rows, :]).astype(jnp.bfloat16)


def branch_gradient(n, nd, info, hidden, gains, cotangent, sums, parts):
    count, depth = cotangent.shape
    got = call(
        functools.partial(branch_body, n, nd),
        [info, hidden, gains, cotangent, *sums, *parts],
        [IN_SMEM] + [IN_VMEM] * 6 + [ANYWHERE] * nd,
        [((count, depth // n), jnp.bfloat16)] * n
        + [((count, depth // nd), jnp.bfloat16)] * nd
        + [((count, depth), jnp.float32), ((8, depth), jnp.float32)],
        [IN_VMEM] * (n + nd + 2),
        [
            pltpu.VMEM((count, depth), jnp.bfloat16),
            pltpu.VMEM((depth, depth), jnp.bfloat16),
            pltpu.SemaphoreType.DMA((nd,)),
        ],
        2 * count * depth * depth,
        6 * depth * depth,
        "branch_gradient",
    )
    return got[:n], got[n : n + nd], got[n + nd], got[n + nd + 1]


def sort_body(n, nd, info, *refs):
    blocks, cols_out = refs[:n], refs[n : n + nd]
    rows, sems = refs[n + nd :]
    me, dp = info[0], info[1]
    share, quarter = blocks[0].shape[1], cols_out[0].shape[1]
    copies = []
    for r in range(n):
        cols = pl.ds(aligned(me ^ r, share), share)
        copies.append(pltpu.make_async_copy(blocks[r], rows.at[:, cols], sems.at[r]))
    wait_all(start_all(copies))
    copies = []
    for r in range(nd):
        cols = pl.ds(aligned(dp ^ r, quarter), quarter)
        copies.append(pltpu.make_async_copy(rows.at[:, cols], cols_out[r], sems.at[r]))
    wait_all(start_all(copies))


def sort_columns(n, nd, info, blocks):
    count, share = blocks[0].shape
    depth = n * share
    return call(
        functools.partial(sort_body, n, nd),
        [info, *blocks],
        [IN_SMEM] + [ANYWHERE] * n,
        [((count, depth // nd), jnp.bfloat16)] * nd,
        [ANYWHERE] * nd,
        [pltpu.VMEM((count, depth), jnp.bfloat16), pltpu.SemaphoreType.DMA((max(n, nd),))],
        0,
        6 * count * depth,
        "sort_columns",
    )


def split_body(n, info, *refs):
    blocks, keys, values, sems = refs[:n], refs[n], refs[n + 1], refs[n + 2]
    me = info[0]
    share = blocks[0].shape[1] // 2
    copies = []
    for r in range(n):
        cols = pl.ds(aligned(me ^ r, share), share)
        copies.append(
            pltpu.make_async_copy(blocks[r].at[:, pl.ds(0, share)], keys.at[:, cols], sems.at[2 * r])
        )
        copies.append(
            pltpu.make_async_copy(
                blocks[r].at[:, pl.ds(share, share)], values.at[:, cols], sems.at[2 * r + 1]
            )
        )
    wait_all(start_all(copies))


def split_keys_values(n, info, blocks):
    count, share = blocks[0].shape
    depth = n * share // 2
    return call(
        functools.partial(split_body, n),
        [info, *blocks],
        [IN_SMEM] + [ANYWHERE] * n,
        [((count, depth), jnp.bfloat16)] * 2,
        [IN_VMEM] * 2,
        [pltpu.SemaphoreType.DMA((2 * n,))],
        0,
        8 * count * depth,
        "split_keys_values",
    )


def input_body(nd, x, gains, grad_hidden, *refs):
    cols, parts = refs[:nd], refs[nd : 2 * nd]
    out, gain_part, upstream = refs[2 * nd :]
    piece = 512

    def step(c, _):
        rows = pl.ds(aligned(c, piece), piece)
        upstream[:, rows] = sum(nt_dot(cols[r][...], parts[r][rows, :]) for r in range(nd))
        return 0

    lax.fori_loop(0, x.shape[1] // piece, step, 0)
    through, gain = norm_grad(x[...].astype(jnp.float32), gains[0:1, :], upstream[...])
    gain_part[...] = jnp.broadcast_to(gain, gain_part.shape)
    out[...] = (grad_hidden[...] + through).astype(jnp.bfloat16)


def input_gradient(nd, x, gains, grad_hidden, cols, parts):
    count, depth = x.shape
    return call(
        functools.partial(input_body, nd),
        [x, gains, grad_hidden, *cols, *parts],
        [IN_VMEM] * (3 + 2 * nd),
        [((count, depth), jnp.bfloat16), ((8, depth), jnp.float32)],
        [IN_VMEM] * 2,
        [pltpu.VMEM((count, depth), jnp.float32)],
        2 * count * depth * depth,
        6 * depth * depth,
        "input_gradient",
    )


def projections_body(n, nd, info, normed, attn_part, ffn_part, *refs):
    branch_cols, query_cols, mixed_in = refs[:nd], refs[nd : 2 * nd], refs[2 * nd : 3 * nd]
    outs = refs[3 * nd : 3 * nd + n]
    branch, query, mixed, made, sems = refs[3 * nd + n :]
    count = branch_cols[0].shape[0]
    share = mixed.shape[1] // n
    for k in range(nd):
        rows = slice(k * count, (k + 1) * count)
        mixed[rows, :] = mixed_in[k][...]
        branch[rows, :] = branch_cols[k][...]
        query[rows, :] = query_cols[k][...]
    copies = []
    for k in range(n):
        cols = pl.ds(aligned(info[3 + k], share), share)
        block = made.at[k]
        block[:share, :] = tn_dot(mixed[:, cols], branch[...])
        block[share : 2 * share, :] = tn_dot(normed[:, cols], query[...])
        block[2 * share :, :] = jnp.zeros((GAIN_ROWS, branch.shape[1]), jnp.float32)
        block[2 * share : 2 * share + 8, :share] = attn_part[:, cols]
        block[2 * share : 2 * share + 8, share : 2 * share] = ffn_part[:, cols]
        copies.append(pltpu.make_async_copy(block, outs[k], sems.at[k]))
        copies[-1].start()
    wait_all(copies)


def projection_gradients(n, nd, info, mixed, normed, attn_part, ffn_part, branch_cols, query_cols):
    rows, depth = normed.shape
    count, quarter = branch_cols[0].shape
    return call(
        functools.partial(projections_body, n, nd),
        [info, normed, attn_part, ffn_part, *branch_cols, *query_cols, *mixed],
        [IN_SMEM] + [IN_VMEM] * (3 + 3 * nd),
        [((2 * depth // n + GAIN_ROWS, quarter), jnp.float32)] * n,
        [ANYWHERE] * n,
        [pltpu.VMEM((rows, quarter), jnp.bfloat16)] * 2
        + [
            pltpu.VMEM((rows, depth), jnp.bfloat16),
            pltpu.VMEM((n, 2 * depth // n + GAIN_ROWS, quarter), jnp.float32),
            pltpu.SemaphoreType.DMA((n,)),
        ],
        4 * rows * depth * quarter,
        4 * rows * depth,
        "projection_gradients",
    )


def join_body(nd, info, *refs):
    parts, (out_grad, query_grad, gain_sum) = refs[:nd], refs[nd:]
    share = out_grad.shape[0]
    quarter = parts[0].shape[1]
    dp = info[1]
    for r in range(nd):
        cols = pl.ds(aligned(dp ^ r, quarter), quarter)
        part = parts[r][...].astype(jnp.float32)
        out_grad[:, cols] = part[:share]
        query_grad[:, cols] = part[share : 2 * share]
    tops = [parts[r][2 * share : 2 * share + 16, :].astype(jnp.float32)[:8] for r in range(nd)]
    gain_sum[...] = tree_sum(tops)


def join_projections(nd, info, parts):
    rows, quarter = parts[0].shape
    share, depth = (rows - GAIN_ROWS) // 2, quarter * nd
    return call(
        functools.partial(join_body, nd),
        [info, *parts],
        [IN_SMEM] + [IN_VMEM] * nd,
        [((share, depth), jnp.float32)] * 2 + [((8, quarter), jnp.float32)],
        [IN_VMEM] * 3,
        [],
        0,
        10 * share * depth,
        "join_projections",
    )


def chip_sum_body(kept, *refs):
    others, out = refs[:-1], refs[-1]
    half = len(others) // 2
    top = others[0].shape[0]
    for side, first in ((others[:half], 0), (others[half:], top)):
        rows = slice(first, first + side[0].shape[0])
        terms = [kept[rows, :].astype(jnp.float32)] + [v[...].astype(jnp.float32) for v in side]
        out[rows, :] = tree_sum(terms).astype(jnp.bfloat16)


def chip_sum(operands):
    shape = operands[0].shape
    return call(
        chip_sum_body,
        operands,
        [IN_VMEM] * len(operands),
        [(shape, jnp.bfloat16)],
        [IN_VMEM],
        [],
        0,
        6 * shape[0] * shape[1],
        "chip_sum",
    )[0]


def spread_body(info, mine, other, out):
    half = mine.shape[1]
    for ref, side in ((mine, info[2]), (other, 1 - info[2])):
        out[:, pl.ds(aligned(side, half), half)] = ref[...].astype(jnp.float32)


def spread_columns(info, mine, other):
    rows, half = mine.shape
    return call(
        spread_body,
        [info, mine, other],
        [IN_SMEM, IN_VMEM, IN_VMEM],
        [((rows, 2 * half), jnp.float32)],
        [IN_VMEM],
        [],
        0,
        12 * rows * half,
        "spread_columns",
    )[0]


def tree_sum(parts):
    while len(parts) > 1:
        parts = [parts[k] + parts[k + 1] for k in range(0, len(parts), 2)]
    return parts[0]


def columns(x, start, width):
    return lax.dynamic_slice_in_dim(x, start, width, 1)


def make_local(mesh):
    net = Links(mesh)
    n, nd = net.n, net.nd
    dp_order = list(range(0, nd, 2)) + list(range(1, nd, 2))
    half_way = n // 2
    ring_order = [0] + [s for k in range(1, half_way) for s in (-k, k)] + ["a", "b"]

    def exchange(blocks, axis="seq"):
        return [b if r == 0 else net.swap(b, axis, r) for r, b in enumerate(blocks)]

    def chips(x, *deps):
        sent = after(x, *deps)
        return [x] + [net.swap(sent, "dp", r) for r in range(2, nd, 2)]

    def cores(near, *deps):
        return list(near) + [net.swap(v, "dp", 1) for v in tie(near, *deps)]

    def paced(ring, blocks, spare=1):
        out, sent = [], 1
        arrived = ring.step()
        steps = half_way - 1
        for k in range(steps):
            until = 1 + (n - 1) * (k + 1) // steps
            some = tie(blocks[sent:until], *arrived)
            fresh = [net.swap(b, "seq", sent + i) for i, b in enumerate(some)]
            arrived = ring.step(*out[-len(some) :]) if k else ring.step()
            out += fresh
            sent = until
        return out

    def local(
        layer_input,
        global_keys,
        global_values,
        lengths,
        attn_gain,
        query_weight,
        out_weight,
        ffn_gain,
        gate_weight,
        up_weight,
        down_weight,
        cotangent,
    ):
        length = lengths[0]
        me, mine = lax.axis_index("seq"), lax.axis_index("dp")
        core, group = mine % 2, net.group(mine)
        place = net.place()
        depth = layer_input.shape[1]
        quarter = depth // nd
        per = n // nd
        owners = [net.owner(place, key) for key in ring_order[:-2]] + [net.owner(place, half_way)]
        info = jnp.stack([me, group, core, *owners]).astype(jnp.int32)
        heads_info = jnp.stack([me, length, group * per + me % per]).astype(jnp.int32)

        gains = jnp.concatenate([attn_gain, ffn_gain])
        gain_rows = jnp.zeros((GAIN_ROWS, quarter), jnp.bfloat16)
        gain_rows = gain_rows.at[:, : gains.shape[0]].set(gains[None])
        mine_of = [columns(w, group * quarter, quarter) for w in (query_weight, out_weight)]
        ring = RingGather(net, jnp.concatenate([gain_rows, *mine_of], 0))
        kv_sent = list(pack_keys_values(n, info, global_keys, global_values))
        kv_blocks = [kv_sent[0]] + paced(ring, kv_sent)
        got = ring.got
        xs = cores(chips(layer_input), got["a"], got["b"])
        q_sent, normed_all, gains, query_quarter, out_quarter = project_queries(
            n, nd, info, xs, [got[k] for k in ring_order]
        )
        q_sent = tie(q_sent, *kv_blocks)
        q_blocks = [net.to_heads(b, m) for m, b in enumerate(q_sent)]
        out_near = chips(out_quarter, *q_blocks)
        mixed_sent, stats, ot = attention_forward(heads_info, q_blocks, kv_blocks)
        cot_ring = RingGather(net, cotangent)
        cot_1 = cot_ring.step(*q_blocks)
        mixed_blocks = exchange(tie(mixed_sent, *cot_1))
        cot_2 = cot_ring.step(*mixed_blocks)
        out_parts = cores(out_near, *mixed_blocks[1:])
        hidden, normed_ffn, mixed = project_mixed(
            n, nd, info, layer_input, gains, mixed_blocks, out_parts
        )

        nf_ring = RingGather(net, normed_ffn)
        weights = (gate_weight, up_weight, down_weight)
        units = gate_weight.shape[0]
        made = {0: ffn_blocks([normed_ffn], [cotangent], weights)[0]}

        def ffn(*keys, deps=()):
            nf, cot = ([ring.got[k] for k in keys] for ring in (nf_ring, cot_ring))
            nf = tie(nf, *deps)
            made.update(zip(keys, ffn_blocks(nf, cot, weights)))

        fresh = nf_ring.step()
        query_near = chips(query_quarter, normed_ffn)
        cot_fresh, before = cot_2, (made[0][3],)
        for k in range(1, half_way):
            later = cot_ring.step(*fresh) if cot_ring.at < half_way else cot_fresh
            fresh = nf_ring.step(*cot_fresh, *before, *(query_near if k == half_way - 1 else ()))
            ffn(-k, k)
            before = (made[k][3], made[-k][3])
            cot_fresh = later
        query_parts = cores(query_near, *fresh)
        mixed_near = chips(mixed, *query_near)
        ffn("a", "b", deps=before)
        nf, cot = nf_ring.got, cot_ring.got

        def exchange_x(kept, *deps):
            sent = after(kept, *deps)
            return [net.swap(sent, "dp", r) for r in range(2, nd, 2)]

        grad_sum = RowSum(net, lambda key: made[key][3])
        out_sum = RowSum(net, lambda key: made[key][4])
        arrived = grad_sum.step()
        kept, deps, swapped, mixed_parts, out_1 = [], (), None, (), ()
        for k in range(3):
            upcoming = grad_sum.step(*deps, *out_1, *((query_parts, mixed_near, mixed_parts)[k]))
            if k == 1:
                out_1 = out_sum.step(*arrived)
            if k == 1:
                mixed_parts = cores(mixed_near, *arrived)
            lhs = tie([made[key][(1, 2, 0)[k]] for key in ring_order], *arrived)
            rhs = [(nf, nf, cot)[k][key] for key in ring_order]
            if swapped:
                kept.append(low(wide(mine_half) + wide(swapped[0])))
            deps = (*swapped,) if swapped else ()
            mine_half, sent_half = weight_gradient(info, lhs, rhs, units)
            swapped = (net.swap(sent_half, "dp", 1),)
            deps = (*deps, mine_half)
            last, arrived = arrived, upcoming
        top = units // 2
        others = [exchange_x(kept[0][:top], *last)]
        grad_sums = tie(grad_sum.rest(), *deps, *others[0])
        kept.append(low(wide(mine_half) + wide(swapped[0])))
        others.append(exchange_x(kept[0][top:], *grad_sums[1:]))

        def dp_cols(cols, *deps):
            sent = tie(cols, *deps)
            return [b if r == 0 else net.swap(b, "dp", r) for r, b in zip(dp_order, sent)]

        out_2 = out_sum.step(*grad_sums[1:])
        gm_sent, branch_cols, grad_hidden, ffn_gain_part = branch_gradient(
            n, nd, info, hidden, gains, cotangent, grad_sums, out_parts
        )
        gm_blocks = exchange(tie(gm_sent, *others[1]))
        branch_got = dp_cols(branch_cols, *gm_sent)
        gm_blocks = tie(gm_blocks, *branch_got, *out_2)
        others.append(exchange_x(kept[1][:top], *gm_blocks))
        out_3 = out_sum.step(*gm_blocks)
        dq_sent, dkv_sent = attention_backward(
            heads_info, q_blocks, kv_blocks, gm_blocks, stats, ot
        )


        dq_sent = tie(dq_sent, *out_3, *others[2])
        others.append(exchange_x(kept[1][top:], *dq_sent))
        dq_blocks = tie(exchange(dq_sent), *others[3])

        def dp_total(k, *deps):
            total = chip_sum(tie([kept[k], *others[2 * k], *others[2 * k + 1]], *deps))
            return total, net.swap(total, "dp", 1)

        query_cols = sort_columns(n, nd, info, dq_blocks)

        query_got = dp_cols(query_cols)
        out_4 = out_sum.step(*query_cols)
        early = (n - 1) * 2 // 7
        dkv_early = [
            net.swap(b, "seq", r + 1) for r, b in enumerate(tie(dkv_sent[1 : early + 1], *query_cols))
        ]
        input_grad, attn_gain_part = input_gradient(
            nd, layer_input, gains, grad_hidden, query_cols, query_parts
        )
        dkv_more = [
            net.swap(b, "seq", early + 1 + r)
            for r, b in enumerate(tie(dkv_sent[early + 1 :], attn_gain_part))
        ]
        dkv_blocks = [dkv_sent[0], *dkv_early, *dkv_more]
        for rows in (slice(top), slice(top, units)):
            others.append(exchange_x(kept[2][rows], *query_got))
        gate_total = dp_total(0, *dq_blocks)
        up_total = dp_total(1, *query_cols)
        shares = projection_gradients(
            n,
            nd,
            info,
            mixed_parts,
            normed_all,
            attn_gain_part,
            ffn_gain_part,
            branch_got,
            query_got,
        )

        def share_of(key):
            if key in ("a", "b"):
                rows = shares[-1].shape[0] // 2
                return shares[-1][:rows] if key == "a" else shares[-1][rows:]
            return shares[ring_order.index(key)]

        share_sum = RowSum(net, share_of)
        shared = share_sum.step(*out_4, *dkv_early)
        gate_grad = spread_columns(info, *tie(gate_total, *shared))
        share_sum.step(*dkv_more[: len(dkv_more) // 2])
        up_grad = spread_columns(info, *tie(up_total, *shared))
        for _ in range(half_way - 3):
            share_sum.step(gate_grad, *dkv_more)
        down_total = dp_total(2, *shared)
        share_sum.step(up_grad)
        down_grad = spread_columns(info, *down_total)
        key_grad, value_grad = split_keys_values(n, info, dkv_blocks)
        own, first, second = share_sum.rest()
        projections = low(own + wide(first) + wide(second))
        projections = after(projections, down_grad, key_grad)
        out_grad, query_grad, gain_sum = join_projections(
            nd, info, cores(chips(projections))
        )
        own, first, second = out_sum.rest()
        layer_output = low(hidden + (own + wide(first) + wide(second)))
        attn_count = attn_gain.shape[0]
        return (
            layer_output,
            input_grad,
            key_grad,
            value_grad,
            gain_sum[0, :attn_count],
            query_grad,
            out_grad,
            gain_sum[0, attn_count : 2 * attn_count],
            gate_grad,
            up_grad,
            down_grad,
        )

    return local


def solution(mesh):
    placed = (
        P(("dp", "seq"), None),
        P(("dp", "seq"), None),
        P(("dp", "seq"), None),
        P("dp"),
        P("seq"),
        P("seq", None),
        P("seq", None),
        P("seq"),
        P("seq", None),
        P("seq", None),
        P("seq", None),
        P(("dp", "seq"), None),
    )
    return jax.shard_map(
        make_local(mesh),
        mesh=mesh,
        in_specs=placed,
        out_specs=(
            P(("dp", "seq"), None),
            P(("dp", "seq"), None),
            P(("dp", "seq"), None),
            P(("dp", "seq"), None),
            P("seq"),
            P("seq", None),
            P("seq", None),
            P("seq"),
            P("seq", None),
            P("seq", None),
            P("seq", None),
        ),
        check_vma=False,
    )
```
